32 devices in a mesh: section: 2 (over x), dp: 4 (over z), mp: 4 (over y, core).
Axes of the slice: x: 2, y: 2, z: 4, core: 2. Of those that a mesh axis runs over, the one named last changes fastest.
Arguments:
- block_input: bfloat16 [2, 1024, 12, 1024], P('section', 'mp', 'dp'), may hold values from -6 to 6
- cotangent: bfloat16 [2, 1024, 12, 1024], P('section', 'mp', 'dp'), may hold values from -6 to 6
- segments: int32 [2, 12, 1024], P(None, 'dp'), may hold values from 0 to 2, as said below
- attn_weight: bfloat16 [2, 1024, 3, 1024], P('section', None, None, 'mp'), may hold values from -0.1875 to 0.1875
- attn_out: bfloat16 [2, 1024, 1024], P('section', 'mp'), may hold values from -1.5 to 1.5
- ffn_in: bfloat16 [2, 1024, 2, 2816], P('section', None, None, 'mp'), may hold values from -0.1875 to 0.1875
- ffn_out: bfloat16 [2, 2816, 1024], P('section', 'mp'), may hold values from -0.109375 to 0.109375
- cross_weight: bfloat16 [2, 1024, 2, 1024], P('section', None, None, 'mp'), may hold values from -1 to 1
- gains: float32 [2, 3, 1024], P('section'), may hold values from 0.1 to 1.9
Outputs:
- block_out: bfloat16 [2, 1024, 12, 1024], P('section', 'mp', 'dp')
- input_grad: float32 [2, 1024, 12, 1024], P('section', 'mp', 'dp')
- attn_weight_grad: float32 [2, 1024, 3, 1024], P('section', 'dp', None, 'mp')
- attn_out_grad: float32 [2, 1024, 1024], P('section', 'mp', 'dp')
- ffn_in_grad: float32 [2, 1024, 2, 2816], P('section', 'dp', None, 'mp')
- ffn_out_grad: float32 [2, 2816, 1024], P('section', 'mp', 'dp')
- cross_weight_grad: float32 [2, 1024, 2, 1024], P('section', 'dp', None, 'mp')
- gains_grad: float32 [2, 3, 1024], P('section', None, ('dp', 'mp'))
The draws below stay inside these ranges and needn't reach their ends.
Inputs may be any that keep to these rules, and one draw needn't show every extreme that they name: `segments`: each row holds documents 0, 1 and 2 in order of position; documents 0 and 2 each have at least 1 and fewer than 128 positions, document 1 all positions between.
All inputs are finite; a program needn't handle non-finite values.
Results may differ from the reference program's by a relative error of at most 0.025.
Values may be sent and summed in bfloat16 or wider, within the bound.
A program may use at most 448 MiB of HBM per device.

```python
import math
import jax
import jax.numpy as jnp
from jax import lax

D = 1024
HEADS = 16
DK = 64
FF = 2816
LEN = 1024
HD = 1024
ROWS = 12


def draw_segments(key, part):
    key = jax.random.fold_in(key, 7)
    first_key, last_key = jax.random.split(key)
    first_cut = jax.random.randint(first_key, (2, ROWS, 1), 1, LEN // 8)
    last_cut = LEN - jax.random.randint(last_key, (2, ROWS, 1), 1, LEN // 8)
    place = lax.broadcasted_iota(jnp.int32, (2, ROWS, LEN), 2)
    return (place >= first_cut).astype(jnp.int32) + (place >= last_cut).astype(jnp.int32)


def draw_cross_weight(key, part):
    key = jax.random.fold_in(key, 11)
    base = jax.random.normal(key, (2, D, 2, HD), jnp.float32)
    slot = lax.broadcasted_iota(jnp.int32, (2, D, 2, HD), 0)
    feature = lax.broadcasted_iota(jnp.int32, (2, D, 2, HD), 1)
    column = lax.broadcasted_iota(jnp.int32, (2, D, 2, HD), 2)
    head_col = lax.broadcasted_iota(jnp.int32, (2, D, 2, HD), 3)
    output_part = (slot == 1) & (column == 1)
    factor = jnp.where(output_part, 8.0 / math.sqrt(HD), 1.0 / math.sqrt(D))
    values = jnp.clip(base * factor, -1.0, 1.0)
    corner = output_part & (feature == 0)
    values = jnp.where(corner & (head_col == 0), 1.0, values)
    values = jnp.where(corner & (head_col == 1), -1.0, values)
    return values.astype(jnp.bfloat16)


def level_of(rng, dims, cuts, smallest, top_value):
    def one(axis_at, parts):
        heights = jax.random.uniform(jax.random.fold_in(jax.random.fold_in(rng, 6), axis_at), (parts,), jnp.float32, smallest / len(cuts), top_value / len(cuts))
        return jnp.repeat(jnp.exp(heights), dims[axis_at] // parts).reshape((-1,) + (1,) * (len(dims) - axis_at - 1))

    gain = one(*cuts[0])
    for cut in cuts[1:]:
        gain = gain * one(*cut)
    return gain


def bell_draw(stream_key, dims, scale, limit, cuts=(), kind=jnp.bfloat16):
    loudness = level_of(stream_key, dims, cuts, -0.22, 0.18) if cuts else 1.0
    values = jax.random.normal(stream_key, dims, jnp.float32) * scale * loudness
    return jnp.minimum(jnp.maximum(values, -limit), limit).astype(kind)


def setup_inputs(seed: int = 0) -> dict:
    streams_of = jax.random.split(jax.random.key(seed), 10)
    block_input = bell_draw(streams_of[0], (2, LEN, ROWS, D), 1.0, 6.0, ((0, 2), (1, 4), (2, 4)))
    cotangent = bell_draw(streams_of[1], (2, LEN, ROWS, D), 1.0, 6.0, ((0, 2), (1, 4), (2, 4)))
    segments = draw_segments(jax.random.fold_in(streams_of[9], 71), 0)
    attn_weight = bell_draw(streams_of[3], (2, D, 3, HD), D ** -0.5, 0.1875, ((0, 2), (3, 4)))
    attn_out = bell_draw(streams_of[4], (2, HD, D), (HD // 64) ** -0.5, 1.5, ((0, 2), (1, 4)))
    ffn_in = bell_draw(streams_of[5], (2, D, 2, FF), D ** -0.5, 0.1875, ((0, 2), (3, 4)))
    ffn_out = bell_draw(streams_of[6], (2, FF, D), FF ** -0.5, 0.109375, ((0, 2), (1, 4)))
    cross_weight = draw_cross_weight(jax.random.fold_in(streams_of[9], 71), 0)
    gains = jnp.clip(1.0 + 0.18 * jax.random.normal(streams_of[8], (2, 3, D), jnp.float32), 0.1, 1.9)
    return {"block_input": block_input, "cotangent": cotangent, "segments": segments, "attn_weight": attn_weight, "attn_out": attn_out, "ffn_in": ffn_in, "ffn_out": ffn_out, "cross_weight": cross_weight, "gains": gains}


@jax.custom_vjp
def low(v):
    return lax.optimization_barrier(v.astype(jnp.bfloat16)).astype(jnp.float32)

@jax.custom_vjp
def low_back(v):
    return v

def low_keep(v):
    return (low(v), None)

def low_pass(kept, grad):
    return (grad,)

def back_keep(v):
    return (v, None)

def back_low(kept, grad):
    return (low(grad),)
low.defvjp(low_keep, low_pass)
low_back.defvjp(back_keep, back_low)
eps = 1e-06
neg_fill = -1e+30
highest = lax.Precision.HIGHEST

def both_round(tensor):
    return low(low_back(tensor))

def norm_scale(tensor, scale_gain):
    return tensor * lax.rsqrt(lax.optimization_barrier(jnp.mean(tensor * tensor, axis=-1, keepdims=True)) + eps) * scale_gain

def attention(queries, key_heads, value_heads, allowed):
    scores = jnp.einsum('qhd,khd->hqk', queries, key_heads, precision=highest) * DK ** (-0.5)
    scores = jnp.where(allowed[None], low_back(scores), neg_fill)
    row_max = lax.optimization_barrier(jnp.max(scores, axis=-1, keepdims=True))
    exponent = jnp.exp(scores - row_max)
    weights_low = low(exponent / lax.optimization_barrier(jnp.sum(exponent, axis=-1, keepdims=True)))
    mixture = jnp.einsum('hqk,khd->qhd', weights_low, value_heads, precision=highest)
    return both_round(mixture.reshape(LEN, HEADS * DK))

def feed_forward(normed, w_in, w_down):
    gate_up = low_back(jnp.einsum('ld,dcf->lcf', normed, w_in, precision=highest))
    hidden = low(jax.nn.gelu(gate_up[:, 0], approximate=True) * gate_up[:, 1])
    return low_back(jnp.dot(hidden, w_down, precision=highest))

def one_row(params, inputs, seg_pair):
    attn_weight, attn_out, ffn_in, ffn_out, cross_weight, gains = params
    seg_enc = seg_pair[0]
    seg_dec = seg_pair[1]
    place = jnp.arange(LEN, dtype=jnp.int32)
    same_enc = seg_enc[:, None] == seg_enc[None, :]
    causal = (seg_dec[:, None] == seg_dec[None, :]) & (place[None, :] <= place[:, None])
    across = seg_dec[:, None] == seg_enc[None, :]

    def self_block(stream, which, allowed):
        normed = low(norm_scale(stream, gains[which, 0]))
        qkv = both_round(jnp.einsum('ld,dch->lch', normed, attn_weight[which], precision=highest))
        head_split = qkv.reshape(LEN, 3, HEADS, DK)
        mixture = attention(head_split[:, 0], head_split[:, 1], head_split[:, 2], allowed)
        return stream + low_back(jnp.dot(mixture, attn_out[which], precision=highest))
    enc_mid_one = self_block(inputs[0], 0, same_enc)
    enc_mid_two = enc_mid_one + feed_forward(low(norm_scale(enc_mid_one, gains[0, 1])), ffn_in[0], ffn_out[0])
    memory = low(norm_scale(enc_mid_two, gains[0, 2]))
    mem_pair = both_round(jnp.einsum('ld,dch->lch', memory, cross_weight[0], precision=highest))
    mem_pair = mem_pair.reshape(LEN, 2, HEADS, DK)
    dec_mid_one = self_block(inputs[1], 1, causal)
    normed = low(norm_scale(dec_mid_one, gains[1, 1]))
    cross_query = both_round(jnp.dot(normed, cross_weight[1][:, 0], precision=highest)).reshape(LEN, HEADS, DK)
    mixture = attention(cross_query, mem_pair[:, 0], mem_pair[:, 1], across)
    dec_mid_two = dec_mid_one + low_back(jnp.einsum('lh,dh->ld', mixture, cross_weight[1][:, 1], precision=highest))
    dec_out = dec_mid_two + feed_forward(low(norm_scale(dec_mid_two, gains[1, 2])), ffn_in[1], ffn_out[1])
    return jnp.stack([memory, dec_out])

def reference(block_input, cotangent, segments, attn_weight, attn_out, ffn_in, ffn_out, cross_weight, gains):
    params = (attn_weight.astype(jnp.float32), attn_out.astype(jnp.float32), ffn_in.astype(jnp.float32), ffn_out.astype(jnp.float32), cross_weight.astype(jnp.float32), gains.astype(jnp.float32))
    inputs = jnp.moveaxis(block_input.astype(jnp.float32), 2, 0)
    seg_rows = jnp.moveaxis(segments, 1, 0)

    def forward(weights, row_inputs):

        def per_row(item):
            return one_row(weights, item[0], item[1])
        return lax.map(jax.checkpoint(per_row), (row_inputs, seg_rows))
    outputs, pull_back = jax.vjp(forward, params, inputs)
    weight_grads, input_grads = pull_back(jnp.moveaxis(cotangent.astype(jnp.float32), 2, 0))
    block_out = jnp.moveaxis(outputs, 0, 2).astype(jnp.bfloat16)
    input_grad = jnp.moveaxis(input_grads, 0, 2)
    return (block_out, input_grad, weight_grads[0], weight_grads[1], weight_grads[2], weight_grads[3], weight_grads[4], weight_grads[5])
```

```python
import functools
import math

import jax
import jax.numpy as jnp
from jax import lax
from jax.experimental import pallas as pl
from jax.experimental.pallas import tpu as pltpu
from jax.sharding import PartitionSpec as P

DK = 64
EPS = 1e-06
BIG = -1e30
SCALE = DK**-0.5
LOG_SCALE = SCALE * math.log2(math.e)
BF, F32 = jnp.bfloat16, jnp.float32

DOC_LANES = 3
OFFSET_LANE = 3
BLOCK_LANE = 8

MESH = pl.DeviceIdType.MESH

NT = (((1,), (1,)), ((), ()))
NN = (((1,), (0,)), ((), ()))
TN = (((0,), (0,)), ((), ()))


def dot(a, b, dims=NN):
    return lax.dot_general(a, b, dims, preferred_element_type=F32)


def norm_scale(tensor, gain):
    return tensor * lax.rsqrt(jnp.mean(tensor * tensor, axis=-1, keepdims=True) + EPS) * gain


def norm_back(tensor, gain, gradient):
    _, pull_back = jax.vjp(norm_scale, tensor, gain)
    return pull_back(gradient)


def split_three(column):
    high = column.astype(BF)
    rest = column - high.astype(F32)
    middle = rest.astype(BF)
    low = (rest - middle.astype(F32)).astype(BF)
    return high, middle, low


def with_offsets(base, column):
    lane = lax.broadcasted_iota(jnp.int32, base.shape, 1)
    out = base.astype(F32)
    for i, piece in enumerate(split_three(column)):
        out = jnp.where(lane == OFFSET_LANE + i, piece.astype(F32), out)
    return out.astype(BF)


def attn_fwd_kernel(size, *refs):
    q_ref, k_ref, v_ref, qa_ref, ka_ref = refs[:5]
    tri_ref = refs[5] if len(refs) == 8 else None
    mix_ref, aug_ref = refs[-2:]
    key_aug = ka_ref[...]
    for head in range(2):
        lanes = slice(head * DK, (head + 1) * DK)
        keys = jnp.concatenate([k_ref[:, lanes], key_aug], axis=1)
        values = jnp.concatenate([v_ref[:, lanes], key_aug], axis=1)
        for c in range(q_ref.shape[0] // size):
            rows = slice(c * size, (c + 1) * size)
            base = qa_ref[rows, :]
            query = jnp.concatenate([q_ref[rows, lanes], base], axis=1)
            scores = []
            for j in range(k_ref.shape[0] // size):
                s = dot(query, keys[j * size : (j + 1) * size], NT)
                scores.append(s + tri_ref[...] if tri_ref is not None and j == c else s)
            top = functools.reduce(jnp.maximum, scores)
            top = jnp.max(top, axis=1, keepdims=True)
            total = None
            for j, s in enumerate(scores):
                p = jnp.exp2((s - top) * LOG_SCALE).astype(BF)
                o = dot(p, values[j * size : (j + 1) * size])
                total = o if total is None else total + o
            weight = total[:, DK + OFFSET_LANE : DK + OFFSET_LANE + 1]
            mix_ref[rows, lanes] = (total[:, :DK] / weight).astype(BF)
            log_raw = top + jnp.log2(weight) * (1.0 / LOG_SCALE)
            aug_ref[rows, lanes] = with_offsets(base, -log_raw)


def attn_bwd_kernel(size, places, hid, *refs):
    q_ref, k_ref, v_ref, do_ref, mix_ref, aug_ref, ka_ref = refs[:7]
    out_refs = [refs[at - len(places_used(places))] for at, _ in places]
    tri_ref = refs[7] if len(refs) == 8 + len(places_used(places)) else None
    length = k_ref.shape[0]
    key_aug = ka_ref[...]
    at_lane = pl.program_id(0) * (2 * DK)
    grads_q, grads_k, grads_v = [], [], []
    for head in range(2):
        lanes = slice(head * DK, (head + 1) * DK)
        key = k_ref[:, lanes]
        keys = jnp.concatenate([key, key_aug], axis=1)
        values = jnp.concatenate([v_ref[:, lanes], key_aug], axis=1)
        grad_k = jnp.zeros((length, DK), F32)
        grad_v = jnp.zeros((length, DK), F32)
        pieces_q = []
        for c in range(q_ref.shape[0] // size):
            rows = slice(c * size, (c + 1) * size)
            query = q_ref[rows, lanes]
            grad = do_ref[rows, lanes]
            delta = jnp.sum(
                grad.astype(F32) * mix_ref[rows, lanes].astype(F32), axis=1, keepdims=True
            )
            queries = jnp.concatenate([query, aug_ref[rows, lanes]], axis=1)
            grads = jnp.concatenate(
                [grad, with_offsets(jnp.zeros((size, DK), BF), -delta)], axis=1
            )
            weights, slopes = [], []
            for j in range(length // size):
                block = slice(j * size, (j + 1) * size)
                s = dot(keys[block], queries, NT)
                if tri_ref is not None and j == c:
                    s = s + tri_ref[...]
                p = jnp.exp2(s * LOG_SCALE)
                slope = p * dot(values[block], grads, NT)
                weights.append(p.astype(BF))
                slopes.append(slope.astype(BF))
            weights = jnp.concatenate(weights, axis=0)
            slopes = jnp.concatenate(slopes, axis=0)
            grad_v = grad_v + dot(weights, grad)
            grad_k = grad_k + dot(slopes, query)
            pieces_q.append((dot(slopes, key, TN) * SCALE).astype(BF))
        grads_q.append(jnp.concatenate(pieces_q, axis=0))
        grads_k.append((grad_k * SCALE).astype(BF))
        grads_v.append(grad_v.astype(BF))
    for ref, (_, lane), halves in zip(out_refs, places, (grads_q, grads_k, grads_v)):
        where = pl.ds(pl.multiple_of(at_lane + lane * hid, 2 * DK), 2 * DK)
        ref[:, where] = jnp.concatenate(halves, axis=1)


def places_used(places):
    return sorted({at for at, _ in places})


def lane_spec(length, first):
    return pl.BlockSpec((length, 2 * DK), lambda i: (0, first + i))


def whole_spec(shape):
    return pl.BlockSpec(shape, lambda i: (0,) * len(shape))


def attn_forward(size, pairs, q, k, v, query_aug, key_aug, tri=None):
    (q, q_at), (k, k_at), (v, v_at) = q, k, v
    rows, length = q.shape[0], k.shape[0]
    out = jax.ShapeDtypeStruct((rows, pairs * 2 * DK), BF)
    extra = [] if tri is None else [tri]
    return pl.pallas_call(
        functools.partial(attn_fwd_kernel, size),
        grid=(pairs,),
        in_specs=[
            lane_spec(rows, q_at),
            lane_spec(length, k_at),
            lane_spec(length, v_at),
            *(whole_spec(a.shape) for a in (query_aug, key_aug, *extra)),
        ],
        out_specs=[lane_spec(rows, 0)] * 2,
        out_shape=[out, out],
        compiler_params=pltpu.CompilerParams(vmem_limit_bytes=48 * 1024 * 1024),
        cost_estimate=pl.CostEstimate(
            flops=pairs * 2 * rows * length * DK * 4 * 4,
            bytes_accessed=pairs * length * 2 * DK * 2 * 5,
            transcendentals=pairs * 2 * rows * length,
        ),
        name="attn_fwd",
    )(q, k, v, query_aug, key_aug, *extra)


def attn_backward(size, pairs, q, k, v, grad, mix, aug, key_aug, tri=None, joined=False):
    (q, q_at), (k, k_at), (v, v_at) = q, k, v
    rows, length = q.shape[0], k.shape[0]
    hid = pairs * 2 * DK
    extra = [] if tri is None else [tri]
    if joined:
        places = ((0, 0), (0, 1), (0, 2))
        shapes = [(length, 3 * hid)]
    else:
        places = ((0, 0), (1, 0), (1, 1))
        shapes = [(rows, hid), (length, 2 * hid)]
    return pl.pallas_call(
        functools.partial(attn_bwd_kernel, size, places, hid),
        grid=(pairs,),
        in_specs=[
            lane_spec(rows, q_at),
            lane_spec(length, k_at),
            lane_spec(length, v_at),
            lane_spec(rows, 0),
            lane_spec(rows, 0),
            lane_spec(rows, 0),
            *(whole_spec(a.shape) for a in (key_aug, *extra)),
        ],
        out_specs=[whole_spec(shape) for shape in shapes],
        out_shape=[jax.ShapeDtypeStruct(shape, BF) for shape in shapes],
        compiler_params=pltpu.CompilerParams(vmem_limit_bytes=48 * 1024 * 1024),
        cost_estimate=pl.CostEstimate(
            flops=pairs * 2 * rows * length * DK * 10 * 4,
            bytes_accessed=pairs * length * 2 * DK * 2 * 9,
            transcendentals=pairs * 2 * rows * length,
        ),
        name="attn_bwd",
    )(q, k, v, grad, mix, aug, key_aug, *extra)


def low_bit(j):
    return j & -j


def flipped(index, bit):
    return index + bit - 2 * bit * lax.rem(index // bit, 2)


class Links:
    def __init__(self, n, own, got, out, back, sems):
        self.n, self.own, self.got, self.out, self.back = n, own, got, out, back
        self.gather_send, self.gather_recv, self.sum_send, self.sum_recv = sems
        self.idx = lax.axis_index("mp")
        self.slots = range(1, n)
        self.parents = sorted({j ^ low_bit(j) for j in self.slots} - {0}, key=int.bit_count)

    def greet(self):
        barrier = pltpu.get_barrier_semaphore()
        bits = [j for j in self.slots if j == low_bit(j)]
        for bit in bits:
            pl.semaphore_signal(
                barrier, inc=1, device_id={"mp": flipped(self.idx, bit)}, device_id_type=MESH
            )
        pl.semaphore_wait(barrier, len(bits))

    def block(self, r, j):
        return self.own.at[r] if j == 0 else self.got.at[r, j - 1]

    def gather_copy(self, r, j):
        return pltpu.make_async_remote_copy(
            src_ref=self.block(r, j ^ low_bit(j)),
            dst_ref=self.got.at[r, j - 1],
            send_sem=self.gather_send.at[r, j - 1],
            recv_sem=self.gather_recv.at[r, j - 1],
            device_id={"mp": flipped(self.idx, low_bit(j))},
            device_id_type=MESH,
        )

    def sum_copy(self, r, j):
        return pltpu.make_async_remote_copy(
            src_ref=self.out.at[r, j - 1],
            dst_ref=self.back.at[r, j - 1],
            send_sem=self.sum_send.at[r, j - 1],
            recv_sem=self.sum_recv.at[r, j - 1],
            device_id={"mp": flipped(self.idx, low_bit(j))},
            device_id_type=MESH,
        )

    def start_gather(self, r):
        for j in sorted(self.slots, reverse=True):
            if j == low_bit(j):
                self.gather_copy(r, j).start()

    def forward_gather(self, r):
        for parent in self.parents:
            self.gather_copy(r, parent).wait_recv()
            for j in self.slots:
                if j ^ low_bit(j) == parent:
                    self.gather_copy(r, j).start()

    def finish_gather(self, r):
        for j in self.slots:
            if j not in self.parents:
                self.gather_copy(r, j).wait_recv()

    def terms(self, j):
        limit = low_bit(j) if j else self.n
        return [j | 1 << b for b in range(self.n.bit_length()) if 1 << b < limit]

    def start_sum(self, r):
        for j in self.slots:
            if low_bit(j) == 1:
                self.sum_copy(r, j).start()

    def forward_sum(self, r):
        for j in sorted(self.slots, key=low_bit):
            if low_bit(j) == 1:
                continue
            total = self.out[r, j - 1].astype(F32)
            for k in self.terms(j):
                self.sum_copy(r, k).wait_recv()
                total = total + self.back[r, k - 1].astype(F32)
            self.out[r, j - 1] = total.astype(BF)
            self.sum_copy(r, j).start()

    def finish_sum(self, r, own):
        for k in self.terms(0):
            self.sum_copy(r, k).wait_recv()
            own = own + self.back[r, k - 1].astype(F32)
        return own

    def drain(self, rows):
        @pl.loop(0, rows)
        def _(r):
            for j in self.slots:
                self.gather_copy(r, j).wait_send()
                self.sum_copy(r, j).wait_send()


def attend_into(size, length, hid, qkv, query_aug, key_aug, tri, mix, aug):
    keys_aug = key_aug[...]
    blocks = length // size
    for head in range(hid // DK):
        lanes = slice(head * DK, (head + 1) * DK)
        k_lanes = slice(hid + head * DK, hid + (head + 1) * DK)
        v_lanes = slice(2 * hid + head * DK, 2 * hid + (head + 1) * DK)
        keys = jnp.concatenate([qkv[:, k_lanes], keys_aug], axis=1)
        values = jnp.concatenate([qkv[:, v_lanes], keys_aug], axis=1)
        for c in range(blocks):
            rows = slice(c * size, (c + 1) * size)
            base = query_aug[rows, :]
            query = jnp.concatenate([qkv[rows, lanes], base], axis=1)
            scores = []
            for j in range(blocks):
                s = dot(query, keys[j * size : (j + 1) * size], NT)
                scores.append(s + tri[...] if j == c else s)
            top = functools.reduce(jnp.maximum, scores)
            top = jnp.max(top, axis=1, keepdims=True)
            total = None
            for j, s in enumerate(scores):
                p = jnp.exp2((s - top) * LOG_SCALE).astype(BF)
                o = dot(p, values[j * size : (j + 1) * size])
                total = o if total is None else total + o
            weight = total[:, DK + OFFSET_LANE : DK + OFFSET_LANE + 1]
            mix[rows, lanes] = (total[:, :DK] / weight).astype(BF)
            log_raw = top + jnp.log2(weight) * (1.0 / LOG_SCALE)
            aug[rows, lanes] = with_offsets(base, -log_raw)


def self_stage_kernel(
    n,
    x,
    w_qkv,
    w_out,
    query_aug,
    key_aug,
    tri,
    total,
    full_out,
    qkv_out,
    mix_out,
    aug_out,
    got,
    out,
    back,
    qkv,
    mix,
    aug,
    *sems,
):
    rows, size = x.shape[:2]
    length, hid = n * size, w_out.shape[0]
    save = sems[-1]
    links = Links(n, x, got, out, back, sems[:4])
    links.greet()

    def saves(r, which):
        for i in which:
            if i < n:
                pair = (links.block(r, i), full_out.at[r, pl.ds(i * size, size)])
            else:
                ref, dst = ((qkv, qkv_out), (mix, mix_out), (aug, aug_out))[i - n]
                pair = (ref.at[r], dst.at[r])
            yield pltpu.make_async_copy(*pair, save.at[r, i])

    for r in range(rows):
        links.start_gather(r)
    links.forward_gather(0)

    @pl.loop(0, rows)
    def _(r):
        links.finish_gather(r)
        for j in range(n):
            qkv[r, j * size : (j + 1) * size, :] = dot(links.block(r, j)[...], w_qkv[...]).astype(
                BF
            )
        for copy in saves(r, range(n + 1)):
            copy.start()

        @pl.when(r > 0)
        def _():
            links.forward_sum(r - 1)

        attend_into(
            size,
            length,
            hid,
            qkv.at[r],
            query_aug.at[r],
            key_aug.at[r],
            tri,
            mix.at[r],
            aug.at[r],
        )
        for copy in saves(r, range(n + 1, n + 3)):
            copy.start()

        @pl.when(r + 1 < rows)
        def _():
            links.forward_gather(r + 1)

        for j in reversed(range(n)):
            part = dot(mix[r, j * size : (j + 1) * size, :], w_out[...])
            if j:
                out[r, j - 1] = part.astype(BF)
                if low_bit(j) == 1:
                    links.sum_copy(r, j).start()
            else:
                total[r] = part

        @pl.when(r > 0)
        def _():
            total[r - 1] = links.finish_sum(r - 1, total[r - 1])

    links.forward_sum(rows - 1)
    total[rows - 1] = links.finish_sum(rows - 1, total[rows - 1])
    links.drain(rows)

    @pl.loop(0, rows)
    def _(r):
        for copy in saves(r, range(n + 3)):
            copy.wait()


def self_stage(n, x, w_qkv, w_out, query_aug, key_aug, tri):
    rows, size, width = x.shape
    length, hid = n * size, w_out.shape[0]
    vmem = pl.BlockSpec(memory_space=pltpu.VMEM)
    hbm = pl.BlockSpec(memory_space=pl.ANY)
    slots = (rows, n - 1)
    return pl.pallas_call(
        functools.partial(self_stage_kernel, n),
        in_specs=[vmem] * 6,
        out_specs=[vmem] + [hbm] * 4,
        out_shape=[
            jax.ShapeDtypeStruct((rows, size, width), F32),
            jax.ShapeDtypeStruct((rows, length, width), BF),
            jax.ShapeDtypeStruct((rows, length, 3 * hid), BF),
            jax.ShapeDtypeStruct((rows, length, hid), BF),
            jax.ShapeDtypeStruct((rows, length, hid), BF),
        ],
        scratch_shapes=[
            pltpu.VMEM((*slots, size, width), BF),
            pltpu.VMEM((*slots, size, width), BF),
            pltpu.VMEM((*slots, size, width), BF),
            pltpu.VMEM((rows, length, 3 * hid), BF),
            pltpu.VMEM((rows, length, hid), BF),
            pltpu.VMEM((rows, length, hid), BF),
            *[pltpu.SemaphoreType.DMA(slots)] * 4,
            pltpu.SemaphoreType.DMA((rows, n + 3)),
        ],
        compiler_params=pltpu.CompilerParams(
            collective_id=1, has_side_effects=True, vmem_limit_bytes=56 * 1024 * 1024
        ),
        cost_estimate=pl.CostEstimate(
            flops=rows * length * width * hid * 8 + rows * length * length * hid * 16,
            bytes_accessed=rows * length * width * 16,
            transcendentals=rows * length * length * hid // DK,
        ),
        name="self_stage",
    )(x, w_qkv, w_out, query_aug, key_aug, tri)


def gelu(gate):
    return jax.nn.gelu(gate, approximate=True)


def body(
    block_input, cotangent, segments, attn_weight, attn_out, ffn_in, ffn_out, cross_weight, gains
):
    enc = lax.axis_index("section") == 0
    idx = lax.axis_index("mp")
    n = lax.axis_size("mp")
    dp_size = lax.axis_size("dp")
    bits = [1 << b for b in range(n.bit_length() - 1)]
    inner, outer = bits[:1], bits[1:]
    size, row_count, width = block_input.shape[1:]
    length = size * n
    hid = attn_weight.shape[3]
    ffd = ffn_in.shape[3]
    pairs = hid // (2 * DK)
    rows = range(row_count)

    def across(tensor, bit):
        return lax.ppermute(tensor, "mp", [(i, i ^ bit) for i in range(n)])

    def spread(tensor, over):
        have = {0: tensor}
        for bit in reversed(over):
            for j in list(have):
                have[j ^ bit] = across(have[j], bit)
        return [have[j] for j in sorted(have)]

    def gather(tensor, over):
        return jnp.concatenate(spread(tensor, over), axis=0)

    def collect(have, over):
        have = dict(have)
        for bit in over:
            for j in sorted((j for j in have if j & bit), reverse=True):
                came = across(have.pop(j), bit)
                total = have[j ^ bit].astype(F32) + came.astype(F32)
                have[j ^ bit] = total if len(have) == 1 else total.astype(BF)
        return have[0].astype(F32)

    def scatter_sum(parts):
        return collect(enumerate(parts), bits)

    def pair_sum(out):
        return out[:size] + across(out[size:].astype(BF), 1).astype(F32)

    def pieces(a, b, dims=NN):
        return tuple(dot(a[j * size : (j + 1) * size], b, dims).astype(BF) for j in range(n))

    def total_of(terms):
        terms = list(terms)
        return functools.reduce(jnp.add, terms)

    def on(side, fn):
        shapes = jax.eval_shape(fn)
        blank = lambda: jax.tree.map(lambda o: jnp.zeros(o.shape, o.dtype), shapes)
        return lax.cond(enc, *((fn, blank) if side == "enc" else (blank, fn)))

    w_qkv = attn_weight[0].reshape(width, 3 * hid)
    w_out = attn_out[0]
    gain = gains[0]
    rows_bf = [block_input[0, :, r] for r in rows]
    rows_in = [v.astype(F32) for v in rows_bf]
    rows_cot = [cotangent[0, :, r] for r in rows]

    order = jnp.arange(n, dtype=jnp.int32) ^ idx
    block_of = jnp.repeat(order, size)
    lane = jnp.arange(DK, dtype=jnp.int32)[None]

    def local_order(seg):
        return jnp.take(seg.reshape(n, size), order, axis=0).reshape(length)

    def query_features(seg, causal):
        doc = (lane < DOC_LANES) & (lane != seg[:, None])
        later = (lane >= BLOCK_LANE) & (lane < BLOCK_LANE + n)
        later = later & (lane - BLOCK_LANE > block_of[: seg.shape[0], None]) & causal
        return jnp.where(doc | later, BIG, 0.0).astype(BF)

    def key_features(seg):
        doc = (lane < DOC_LANES) & (lane == seg[:, None])
        ones = (lane >= OFFSET_LANE) & (lane < OFFSET_LANE + 3)
        place = lane - BLOCK_LANE == block_of[:, None]
        return jnp.where(doc | ones | place, 1.0, 0.0).astype(BF)

    above = jnp.arange(size)[None, :] > jnp.arange(size)[:, None]
    tri = jnp.where(above & ~enc, BIG, 0.0).astype(F32)
    feats = []
    for r in rows:
        seg_enc, seg_dec = local_order(segments[0, r]), local_order(segments[1, r])
        own = jnp.where(enc, seg_enc, seg_dec)
        feats.append(
            (
                query_features(own, ~enc),
                key_features(own),
                query_features(seg_dec[: 2 * size], False),
                key_features(seg_enc),
            )
        )

    normed1 = jnp.stack([norm_scale(v, gain[0]).astype(BF) for v in rows_in])
    total1, full1, qkv1, mix1, aug1 = self_stage(
        n,
        normed1,
        w_qkv,
        w_out,
        jnp.stack([f[0] for f in feats]),
        jnp.stack([f[1] for f in feats]),
        tri,
    )
    saved1 = [(qkv1[r], mix1[r], aug1[r]) for r in rows]
    mid1 = [rows_in[r] + total1[r] for r in rows]

    w_in = spread(ffn_in[0].reshape(width, 2 * ffd), outer)
    w_down = spread(ffn_out[0], outer)
    w_cross = spread(cross_weight[0].reshape(width, 2 * hid), outer)
    w_kv = [lax.ppermute(w, "section", [(0, 1)]) for w in w_cross]
    w_q = [w[:, :hid] for w in w_cross]
    w_o = [w[:, hid:] for w in w_cross]
    parts = range(len(w_in))

    def gate_up_of(full):
        return [dot(full, w) for w in w_in]

    def ffn_out_of(gate_up):
        hidden = [(gelu(g[:, :ffd]) * g[:, ffd:]).astype(BF) for g in gate_up]
        return total_of(dot(h, w) for h, w in zip(hidden, w_down))

    def ffn_back(grad_full, gate_up):
        kept, grad_normed = [], []
        for b in parts:
            gate, up = gate_up[b][:, :ffd].astype(F32), gate_up[b][:, ffd:].astype(F32)
            activated, pull = jax.vjp(gelu, gate)
            hidden = (activated * up).astype(BF)
            grad_hidden = dot(grad_full, w_down[b], NT)
            grad_gate = pull(grad_hidden * up)[0].astype(BF)
            grad_up = (grad_hidden * activated).astype(BF)
            grad_pair = jnp.concatenate([grad_gate, grad_up], axis=1)
            grad_normed.append(dot(grad_pair, w_in[b], NT))
            kept.append((hidden, grad_pair))
        return total_of(grad_normed), kept

    def cross_fwd(full, mem, r):
        outs, saved = [], []
        for b in parts:
            q = dot(full, w_q[b]).astype(BF)
            kv = dot(mem, w_kv[b]).astype(BF)
            mix, aug = attn_forward(
                size, pairs, (q, 0), (kv, 0), (kv, pairs), feats[r][2], feats[r][3]
            )
            outs.append(dot(mix, w_o[b], NT))
            saved.append((q, kv, mix, aug))
        return total_of(outs), saved

    def cross_back(grad_full, saved, r):
        kept, grad_normed, grad_mem = [], [], []
        for b in parts:
            q, kv, mix, aug = saved[b]
            grad_mix = dot(grad_full, w_o[b]).astype(BF)
            dq, dkv = attn_backward(
                size, pairs, (q, 0), (kv, 0), (kv, pairs), grad_mix, mix, aug, feats[r][3]
            )
            grad_normed.append(dot(dq, w_q[b], NT))
            grad_mem.append(dot(dkv, w_kv[b], NT))
            kept.append((dq, dkv))
        grad_mem = total_of(grad_mem).astype(BF)
        return total_of(grad_normed), tuple(
            grad_mem[j * size : (j + 1) * size] for j in range(n)
        ), kept

    full2, gate_up2, mid2_e, memory, mem_full = [], [], [], [], []
    for r in rows:
        full2.append(gather(norm_scale(mid1[r], gain[1]).astype(BF), inner))

        def enc_ffn(r=r):
            gate_up = gate_up_of(full2[r])
            return ffn_out_of(gate_up), [g.astype(BF) for g in gate_up]

        out, gate_up = on("enc", enc_ffn)
        gate_up2.append(gate_up)
        mid2_e.append(mid1[r] + pair_sum(out))
        memory.append(norm_scale(mid2_e[r], gain[2]).astype(BF))
        mem_full.append(gather(lax.ppermute(memory[r], "section", [(0, 1)]), bits))

    saved_x, mid2_d, full3, dec_out, kept3, grad_mid2_d = [], [], [], [], [], []
    grad_full3, grad_full2_d, kept_x, grad_mid1_d, grad_memory = [], [], [], [], []
    gain_sums = [[], [], []]
    for r in rows:
        out, saved = on("dec", lambda r=r: cross_fwd(full2[r], mem_full[r], r))
        saved_x.append(saved)
        mid2_d.append(mid1[r] + pair_sum(out))
    for r in rows:
        full3.append(gather(norm_scale(mid2_d[r], gain[2]).astype(BF), inner))
        grad_full3.append(gather(rows_cot[r], inner))

        def dec_ffn(r=r):
            gate_up = gate_up_of(full3[r])
            grad_normed, kept = ffn_back(grad_full3[r], gate_up)
            return ffn_out_of(gate_up), grad_normed, kept

        out, grad_normed, kept = on("dec", dec_ffn)
        kept3.append(kept)
        dec_out.append((mid2_d[r] + pair_sum(out)).astype(BF))
        part, gain_grad = norm_back(mid2_d[r], gain[2], pair_sum(grad_normed))
        gain_sums[2].append(jnp.where(enc, 0.0, gain_grad))
        grad_mid2_d.append(rows_cot[r].astype(F32) + part)
    for r in rows:
        grad_full2_d.append(gather(grad_mid2_d[r].astype(BF), inner))
        grad_normed, grad_mem, kept = on(
            "dec", lambda r=r: cross_back(grad_full2_d[r], saved_x[r], r)
        )
        kept_x.append(kept)
        arrived = lax.ppermute(scatter_sum(grad_mem).astype(BF), "section", [(1, 0)])
        grad_memory.append(arrived.astype(F32))
        part, gain_grad = norm_back(mid1[r], gain[1], pair_sum(grad_normed))
        gain_sums[1].append(jnp.where(enc, 0.0, gain_grad))
        grad_mid1_d.append(grad_mid2_d[r] + part)

    kept2, grad_full2_e, grad_mid1 = [], [], []
    for r in rows:
        part, gain_grad = norm_back(
            mid2_e[r], gain[2], rows_cot[r].astype(F32) + grad_memory[r]
        )
        gain_sums[2].append(jnp.where(enc, gain_grad, 0.0))
        grad_mid2 = part
        grad_full2_e.append(gather(grad_mid2.astype(BF), inner))
        grad_normed, kept = on("enc", lambda r=r: ffn_back(grad_full2_e[r], gate_up2[r]))
        kept2.append(kept)
        part, gain_grad = norm_back(mid1[r], gain[1], pair_sum(grad_normed))
        gain_sums[1].append(jnp.where(enc, gain_grad, 0.0))
        grad_mid1.append(jnp.where(enc, grad_mid2 + part, grad_mid1_d[r]))

    grad_full1, grad_qkv, input_grad = [], [], []
    for r in rows:
        qkv, mix, aug = saved1[r]
        grad_full1.append(gather(grad_mid1[r].astype(BF), bits))
        grad_mix = dot(grad_full1[r], w_out, NT).astype(BF)
        (dqkv,) = attn_backward(
            size,
            pairs,
            (qkv, 0),
            (qkv, pairs),
            (qkv, 2 * pairs),
            grad_mix,
            mix,
            aug,
            feats[r][1],
            tri.T,
            joined=True,
        )
        grad_qkv.append(dqkv)
        part, gain_grad = norm_back(
            rows_in[r], gain[0], scatter_sum(pieces(dqkv, w_qkv, NT))
        )
        gain_sums[0].append(gain_grad)
        input_grad.append(grad_mid1[r] + part)

    def contract(lefts, rights):
        return total_of(dot(a, b, TN) for a, b in zip(lefts, rights)).astype(BF)

    def ffn_weights(full, kept, grad_full):
        return (
            [contract(full, [kept[r][b][1] for r in rows]) for b in parts],
            [contract([kept[r][b][0] for r in rows], grad_full) for b in parts],
        )

    def cross_weights():
        q = [contract(full2, [kept_x[r][b][0] for r in rows]) for b in parts]
        o = [contract(grad_full2_d, [saved_x[r][b][2] for r in rows]) for b in parts]
        kv = [contract(mem_full, [kept_x[r][b][1] for r in rows]) for b in parts]
        return [jnp.concatenate(qo, axis=1) for qo in zip(q, o)], kv

    def over_outer(blocks):
        step = 2
        return collect({step * b: t for b, t in enumerate(blocks)}, outer).astype(BF)

    def over_rows(total, dim):
        return lax.psum_scatter(total, "dp", scatter_dimension=dim, tiled=True).astype(F32)

    sum_in, sum_down = lax.cond(
        enc,
        lambda: ffn_weights(full2, kept2, grad_full2_e),
        lambda: ffn_weights(full3, kept3, grad_full3),
    )
    sum_qo, sum_kv = on("dec", cross_weights)
    sum_qkv = contract([full1[r] for r in rows], grad_qkv)
    sum_out = contract([s[1] for s in saved1], grad_full1)

    quarter = width // dp_size
    out_in = over_rows(over_outer(sum_in), 0).reshape(quarter, 2, ffd)
    out_down = over_rows(over_outer(sum_down), 1)
    sum_kv = lax.ppermute(over_outer(sum_kv), "section", [(1, 0)])
    sum_cross = jnp.where(enc, sum_kv, over_outer(sum_qo))
    out_cross = over_rows(sum_cross, 0).reshape(quarter, 2, hid)
    out_qkv = over_rows(sum_qkv, 0).reshape(quarter, 3, hid)
    out_out = over_rows(sum_out, 1)
    gain_total = lax.psum_scatter(
        jnp.stack([total_of(items) for items in gain_sums]),
        ("dp", "mp"),
        scatter_dimension=1,
        tiled=True,
    )
    block_out = jnp.stack([jnp.where(enc, memory[r], dec_out[r]) for r in rows], axis=1)
    return (
        block_out[None],
        jnp.stack(input_grad, axis=1)[None],
        out_qkv[None],
        out_out[None],
        out_in[None],
        out_down[None],
        out_cross[None],
        gain_total[None],
    )


def solution(mesh):
    in_specs = (
        P("section", "mp", "dp", None),
        P("section", "mp", "dp", None),
        P(None, "dp", None),
        P("section", None, None, "mp"),
        P("section", "mp", None),
        P("section", None, None, "mp"),
        P("section", "mp", None),
        P("section", None, None, "mp"),
        P("section", None, None),
    )
    out_specs = (
        P("section", "mp", "dp", None),
        P("section", "mp", "dp", None),
        P("section", "dp", None, "mp"),
        P("section", "mp", "dp"),
        P("section", "dp", None, "mp"),
        P("section", "mp", "dp"),
        P("section", "dp", None, "mp"),
        P("section", None, ("dp", "mp")),
    )
    return jax.shard_map(body, mesh=mesh, in_specs=in_specs, out_specs=out_specs, check_vma=False)
```

```python
import functools
import math

import jax
import jax.numpy as jnp
from jax import lax
from jax.experimental import pallas as pl
from jax.experimental.pallas import tpu as pltpu
from jax.sharding import PartitionSpec as P

DK = 64
EPS = 1e-06
BIG = -1e30
SCALE = DK**-0.5
LOG_SCALE = SCALE * math.log2(math.e)
BF, F32 = jnp.bfloat16, jnp.float32

DOC_LANES = 3
OFFSET_LANE = 3
BLOCK_LANE = 8

MESH = pl.DeviceIdType.MESH

NT = (((1,), (1,)), ((), ()))
NN = (((1,), (0,)), ((), ()))
TN = (((0,), (0,)), ((), ()))


def dot(a, b, dims=NN):
    return lax.dot_general(a, b, dims, preferred_element_type=F32)


def norm_scale(tensor, gain):
    return tensor * lax.rsqrt(jnp.mean(tensor * tensor, axis=-1, keepdims=True) + EPS) * gain


def norm_back(tensor, gain, gradient):
    _, pull_back = jax.vjp(norm_scale, tensor, gain)
    return pull_back(gradient)


def split_three(column):
    high = column.astype(BF)
    rest = column - high.astype(F32)
    middle = rest.astype(BF)
    low = (rest - middle.astype(F32)).astype(BF)
    return high, middle, low


def with_offsets(base, column):
    lane = lax.broadcasted_iota(jnp.int32, base.shape, 1)
    out = base.astype(F32)
    for i, piece in enumerate(split_three(column)):
        out = jnp.where(lane == OFFSET_LANE + i, piece.astype(F32), out)
    return out.astype(BF)


def low_bit(j):
    return j & -j


def flipped(index, bit):
    return index + bit - 2 * bit * lax.rem(index // bit, 2)


def greet(n, section=False):
    barrier = pltpu.get_barrier_semaphore()
    idx = lax.axis_index("mp")
    bits = [j for j in range(1, n) if j == low_bit(j)]
    for bit in bits:
        pl.semaphore_signal(
            barrier, inc=1, device_id={"mp": flipped(idx, bit)}, device_id_type=MESH
        )
    if section:
        other = 1 - lax.axis_index("section")
        pl.semaphore_signal(barrier, inc=1, device_id={"section": other}, device_id_type=MESH)
    pl.semaphore_wait(barrier, len(bits) + (1 if section else 0))


class Gather:
    def __init__(self, n, own, got, send, recv):
        self.n, self.own, self.got, self.send, self.recv = n, own, got, send, recv
        self.idx = lax.axis_index("mp")
        self.slots = range(1, n)
        self.parents = sorted({j ^ low_bit(j) for j in self.slots} - {0}, key=int.bit_count)

    def block(self, r, j):
        return self.own.at[r] if j == 0 else self.got.at[r, j - 1]

    def copy(self, r, j):
        return pltpu.make_async_remote_copy(
            src_ref=self.block(r, j ^ low_bit(j)),
            dst_ref=self.got.at[r, j - 1],
            send_sem=self.send.at[r, j - 1],
            recv_sem=self.recv.at[r, j - 1],
            device_id={"mp": flipped(self.idx, low_bit(j))},
            device_id_type=MESH,
        )

    def start(self, r):
        for j in sorted(self.slots, reverse=True):
            if j == low_bit(j):
                self.copy(r, j).start()

    def forward(self, r):
        for parent in self.parents:
            self.copy(r, parent).wait_recv()
            for j in self.slots:
                if j ^ low_bit(j) == parent:
                    self.copy(r, j).start()

    def finish(self, r):
        for j in self.slots:
            if j not in self.parents:
                self.copy(r, j).wait_recv()

    def drain(self, r):
        for j in self.slots:
            self.copy(r, j).wait_send()


class Sums:
    def __init__(self, n, out, back, send, recv):
        self.n, self.out, self.back, self.send, self.recv = n, out, back, send, recv
        self.idx = lax.axis_index("mp")
        self.slots = range(1, n)

    def copy(self, r, j):
        return pltpu.make_async_remote_copy(
            src_ref=self.out.at[r, j - 1],
            dst_ref=self.back.at[r, j - 1],
            send_sem=self.send.at[r, j - 1],
            recv_sem=self.recv.at[r, j - 1],
            device_id={"mp": flipped(self.idx, low_bit(j))},
            device_id_type=MESH,
        )

    def terms(self, j):
        limit = low_bit(j) if j else self.n
        return [j | 1 << b for b in range(self.n.bit_length()) if 1 << b < limit]

    def put(self, r, j, part):
        self.out[r, j - 1] = part.astype(BF)
        if low_bit(j) == 1:
            self.copy(r, j).start()

    def forward(self, r):
        for j in sorted(self.slots, key=low_bit):
            if low_bit(j) == 1:
                continue
            total = self.out[r, j - 1].astype(F32)
            for k in self.terms(j):
                self.copy(r, k).wait_recv()
                total = total + self.back[r, k - 1].astype(F32)
            self.out[r, j - 1] = total.astype(BF)
            self.copy(r, j).start()

    def total(self, r, own):
        for k in self.terms(0):
            self.copy(r, k).wait_recv()
            own = own + self.back[r, k - 1].astype(F32)
        return own

    def drain(self, r):
        for j in self.slots:
            self.copy(r, j).wait_send()


def attend_into(size, heads, q, k, v, query_aug, key_aug, tri, mix, aug):
    keys_aug = key_aug[...]
    blocks = mix.shape[0] // size
    lanes_of = lambda at, head: slice(at + head * DK, at + (head + 1) * DK)
    for head in range(heads):
        lanes = lanes_of(0, head)
        keys = jnp.concatenate([k[0][:, lanes_of(k[1], head)], keys_aug], axis=1)
        values = jnp.concatenate([v[0][:, lanes_of(v[1], head)], keys_aug], axis=1)
        for c in range(blocks):
            rows = slice(c * size, (c + 1) * size)
            base = query_aug[rows, :]
            query = jnp.concatenate([q[0][rows, lanes_of(q[1], head)], base], axis=1)
            scores = []
            for j in range(blocks):
                s = dot(query, keys[j * size : (j + 1) * size], NT)
                scores.append(s + tri[...] if tri is not None and j == c else s)
            top = functools.reduce(jnp.maximum, scores)
            top = jnp.max(top, axis=1, keepdims=True)
            total = None
            for j, s in enumerate(scores):
                p = jnp.exp2((s - top) * LOG_SCALE).astype(BF)
                o = dot(p, values[j * size : (j + 1) * size])
                total = o if total is None else total + o
            weight = total[:, DK + OFFSET_LANE : DK + OFFSET_LANE + 1]
            mix[rows, lanes] = (total[:, :DK] / weight).astype(BF)
            log_raw = top + jnp.log2(weight) * (1.0 / LOG_SCALE)
            aug[rows, lanes] = with_offsets(base, -log_raw)


def attend_back_into(size, heads, q, k, v, grad, mix, aug, key_aug, tri, dq, dk, dv):
    keys_aug = key_aug[...]
    length = k[0].shape[0]
    at = lambda ref, head: slice(ref[1] + head * DK, ref[1] + (head + 1) * DK)
    for head in range(heads):
        key = k[0][:, at(k, head)]
        keys = jnp.concatenate([key, keys_aug], axis=1)
        values = jnp.concatenate([v[0][:, at(v, head)], keys_aug], axis=1)
        grad_k = jnp.zeros((length, DK), F32)
        grad_v = jnp.zeros((length, DK), F32)
        for c in range(length // size):
            rows = slice(c * size, (c + 1) * size)
            query = q[0][rows, at(q, head)]
            slope_in = grad[0][rows, at(grad, head)]
            delta = jnp.sum(
                slope_in.astype(F32) * mix[0][rows, at(mix, head)].astype(F32),
                axis=1,
                keepdims=True,
            )
            queries = jnp.concatenate([query, aug[0][rows, at(aug, head)]], axis=1)
            grads = jnp.concatenate(
                [slope_in, with_offsets(jnp.zeros((size, DK), BF), -delta)], axis=1
            )
            weights, slopes = [], []
            for j in range(length // size):
                block = slice(j * size, (j + 1) * size)
                s = dot(keys[block], queries, NT)
                if tri is not None and j == c:
                    s = s + tri[...]
                p = jnp.exp2(s * LOG_SCALE)
                slope = p * dot(values[block], grads, NT)
                weights.append(p.astype(BF))
                slopes.append(slope.astype(BF))
            weights = jnp.concatenate(weights, axis=0)
            slopes = jnp.concatenate(slopes, axis=0)
            grad_v = grad_v + dot(weights, slope_in)
            grad_k = grad_k + dot(slopes, query)
            dq[0][rows, at(dq, head)] = (dot(slopes, key, TN) * SCALE).astype(BF)
        dk[0][:, at(dk, head)] = (grad_k * SCALE).astype(BF)
        dv[0][:, at(dv, head)] = grad_v.astype(BF)


GELU_A, GELU_B = math.sqrt(2.0 / math.pi), 0.044715


def gelu_and_slope(x):
    square = x * x
    t = jnp.tanh(GELU_A * x * (1.0 + GELU_B * square))
    half = 0.5 * (1.0 + t)
    slope = half + 0.5 * x * (1.0 - t * t) * (GELU_A * (1.0 + 3.0 * GELU_B * square))
    return x * half, slope


def norm_parts(stream):
    return lax.rsqrt(jnp.mean(stream * stream, axis=-1, keepdims=True) + EPS)


def norm_back_parts(stream, gain, gradient):
    root = norm_parts(stream)
    unit = stream * root
    scaled = gradient * gain
    inner = jnp.mean(scaled * unit, axis=-1, keepdims=True)
    return root * (scaled - unit * inner), gradient * unit


def gain_terms(terms):
    return jnp.sum(terms.reshape(terms.shape[0] // 8, 8, terms.shape[1]), axis=0)


VMEM_LIMIT = 60 * 1024 * 1024


def call_stage(kernel, name, number, inputs, outputs, scratch, flops):
    vmem = pl.BlockSpec(memory_space=pltpu.VMEM)
    hbm = pl.BlockSpec(memory_space=pl.ANY)
    return pl.pallas_call(
        kernel,
        in_specs=[vmem if near else hbm for _, near in inputs],
        out_specs=[vmem if near else hbm for _, _, near in outputs],
        out_shape=[jax.ShapeDtypeStruct(shape, kind) for shape, kind, _ in outputs],
        scratch_shapes=scratch,
        compiler_params=pltpu.CompilerParams(
            collective_id=number, has_side_effects=True, vmem_limit_bytes=VMEM_LIMIT
        ),
        cost_estimate=pl.CostEstimate(
            flops=flops, bytes_accessed=1 << 25, transcendentals=1 << 24
        ),
        name=name,
    )(*(array for array, _ in inputs))


def self_stage_kernel(n, *refs):
    (x, w_qkv, w_out, query_aug, key_aug, tri) = refs[:6]
    (total, full_out, qkv_out, mix_out, aug_out) = refs[6:11]
    (got, out, back, qkv, mix, aug) = refs[11:17]
    sems = refs[17:]
    rows, size = x.shape[:2]
    hid = w_out.shape[0]
    gather = Gather(n, x, got, *sems[:2])
    sums = Sums(n, out, back, *sems[2:4])
    save = sems[4]
    greet(n)

    def saves(r, which):
        for i in which:
            if i < n:
                pair = (gather.block(r, i), full_out.at[r, pl.ds(i * size, size)])
            else:
                ref, dst = ((qkv, qkv_out), (mix, mix_out), (aug, aug_out))[i - n]
                pair = (ref.at[r], dst.at[r])
            yield pltpu.make_async_copy(*pair, save.at[r, i])

    for r in range(rows):
        gather.start(r)
    gather.forward(0)

    @pl.loop(0, rows)
    def _(r):
        gather.finish(r)
        for j in range(n):
            qkv[r, j * size : (j + 1) * size, :] = dot(
                gather.block(r, j)[...], w_qkv[...]
            ).astype(BF)
        for copy in saves(r, range(n + 1)):
            copy.start()

        @pl.when(r > 0)
        def _():
            sums.forward(r - 1)

        row = qkv.at[r]
        attend_into(
            size,
            hid // DK,
            (row, 0),
            (row, hid),
            (row, 2 * hid),
            query_aug.at[r],
            key_aug.at[r],
            tri,
            mix.at[r],
            aug.at[r],
        )
        for copy in saves(r, range(n + 1, n + 3)):
            copy.start()

        @pl.when(r + 1 < rows)
        def _():
            gather.forward(r + 1)

        for j in reversed(range(n)):
            part = dot(mix[r, j * size : (j + 1) * size, :], w_out[...])
            if j:
                sums.put(r, j, part)
            else:
                total[r] = part

        @pl.when(r > 0)
        def _():
            total[r - 1] = sums.total(r - 1, total[r - 1])

    sums.forward(rows - 1)
    total[rows - 1] = sums.total(rows - 1, total[rows - 1])

    @pl.loop(0, rows)
    def _(r):
        gather.drain(r)
        sums.drain(r)
        for copy in saves(r, range(n + 3)):
            copy.wait()


def self_stage(n, x, w_qkv, w_out, query_aug, key_aug, tri):
    rows, size, width = x.shape
    length, hid = n * size, w_out.shape[0]
    slots = (rows, n - 1)
    return call_stage(
        functools.partial(self_stage_kernel, n),
        "self_stage",
        1,
        [(a, True) for a in (x, w_qkv, w_out, query_aug, key_aug, tri)],
        [
            ((rows, size, width), F32, True),
            ((rows, length, width), BF, False),
            ((rows, length, 3 * hid), BF, False),
            ((rows, length, hid), BF, False),
            ((rows, length, hid), BF, False),
        ],
        [
            *[pltpu.VMEM((*slots, size, width), BF)] * 3,
            pltpu.VMEM((rows, length, 3 * hid), BF),
            pltpu.VMEM((rows, length, hid), BF),
            pltpu.VMEM((rows, length, hid), BF),
            *[pltpu.SemaphoreType.DMA(slots)] * 4,
            pltpu.SemaphoreType.DMA((rows, n + 3)),
        ],
        rows * length * width * hid * 8 + rows * length * length * hid * 16,
    )


def self_back_kernel(n, *refs):
    (x, w_qkv, w_out, key_aug, tri_t, qkv_in, mix_in, aug_in) = refs[:8]
    (total, full_out, dqkv_out) = refs[8:11]
    (got, out, back, qkv, mix, aug, grad, dqkv) = refs[11:19]
    sems = refs[19:]
    rows, size = x.shape[:2]
    hid = w_out.shape[0]
    gather = Gather(n, x, got, *sems[:2])
    sums = Sums(n, out, back, *sems[2:4])
    save, load = sems[4:]
    greet(n)

    def loads(r):
        for i, (src, dst) in enumerate(((qkv_in, qkv), (mix_in, mix), (aug_in, aug))):
            yield pltpu.make_async_copy(src.at[r], dst.at[r], load.at[r, i])

    def saves(r, which):
        for i in which:
            if i < n:
                pair = (gather.block(r, i), full_out.at[r, pl.ds(i * size, size)])
            else:
                pair = (dqkv.at[r], dqkv_out.at[r])
            yield pltpu.make_async_copy(*pair, save.at[r, i])

    for r in range(rows):
        gather.start(r)
        for copy in loads(r):
            copy.start()
    gather.forward(0)

    @pl.loop(0, rows)
    def _(r):
        gather.finish(r)
        for j in range(n):
            grad[j * size : (j + 1) * size, :] = dot(
                gather.block(r, j)[...], w_out[...], NT
            ).astype(BF)
        for copy in saves(r, range(n)):
            copy.start()
        for copy in loads(r):
            copy.wait()

        @pl.when(r > 0)
        def _():
            sums.forward(r - 1)

        row, slope = qkv.at[r], dqkv.at[r]
        attend_back_into(
            size,
            hid // DK,
            (row, 0),
            (row, hid),
            (row, 2 * hid),
            (grad, 0),
            (mix.at[r], 0),
            (aug.at[r], 0),
            key_aug.at[r],
            tri_t,
            (slope, 0),
            (slope, hid),
            (slope, 2 * hid),
        )
        for copy in saves(r, range(n, n + 1)):
            copy.start()

        @pl.when(r + 1 < rows)
        def _():
            gather.forward(r + 1)

        for j in reversed(range(n)):
            part = dot(dqkv[r, j * size : (j + 1) * size, :], w_qkv[...], NT)
            if j:
                sums.put(r, j, part)
            else:
                total[r] = part

        @pl.when(r > 0)
        def _():
            total[r - 1] = sums.total(r - 1, total[r - 1])

    sums.forward(rows - 1)
    total[rows - 1] = sums.total(rows - 1, total[rows - 1])

    @pl.loop(0, rows)
    def _(r):
        gather.drain(r)
        sums.drain(r)
        for copy in saves(r, range(n + 1)):
            copy.wait()


def self_back_stage(n, x, w_qkv, w_out, key_aug, tri_t, qkv, mix, aug):
    rows, size, width = x.shape
    length, hid = n * size, w_out.shape[0]
    slots = (rows, n - 1)
    return call_stage(
        functools.partial(self_back_kernel, n),
        "self_back_stage",
        2,
        [(a, True) for a in (x, w_qkv, w_out, key_aug, tri_t)]
        + [(a, False) for a in (qkv, mix, aug)],
        [
            ((rows, size, width), F32, True),
            ((rows, length, width), BF, False),
            ((rows, length, 3 * hid), BF, False),
        ],
        [
            *[pltpu.VMEM((*slots, size, width), BF)] * 3,
            pltpu.VMEM((rows, length, 3 * hid), BF),
            pltpu.VMEM((rows, length, hid), BF),
            pltpu.VMEM((rows, length, hid), BF),
            pltpu.VMEM((length, hid), BF),
            pltpu.VMEM((rows, length, 3 * hid), BF),
            *[pltpu.SemaphoreType.DMA(slots)] * 4,
            pltpu.SemaphoreType.DMA((rows, n + 1)),
            pltpu.SemaphoreType.DMA((rows, 3)),
        ],
        rows * length * width * hid * 8 + rows * length * length * hid * 40,
    )


def middle_kernel(n, *refs):
    (x, cot, mid1, gain, w_gate, w_up, w_down, w_cross, query_aug, key_aug) = refs[:10]
    (mid2, third, full_a, full_b, full_cot, kv_out, q_out, mix_out, aug_out) = refs[10:19]
    (got_a, got_b, got_c, out, back, kv, q, mix, aug) = refs[19:28]
    sems = refs[28:]
    rows, size = x.shape[:2]
    hid = q.shape[2]
    enc = lax.axis_index("section") == 0
    gather_a = Gather(n, x, got_a, *sems[0:2])
    gather_b = Gather(n, third, got_b, *sems[2:4])
    gather_c = Gather(n, cot, got_c, *sems[4:6])
    sums = Sums(n, out, back, *sems[6:8])
    pair_send, pair_recv, save_a, save_b, save_c, save_x = sems[8:]
    greet(n, True)

    def block_saves(gather, dst, sem, r):
        for j in range(n):
            yield pltpu.make_async_copy(
                gather.block(r, j), dst.at[r, pl.ds(j * size, size)], sem.at[r, j]
            )

    def cross_saves(r):
        for i, (src, dst) in enumerate(
            ((kv, kv_out), (q, q_out), (mix, mix_out), (aug, aug_out))
        ):
            yield pltpu.make_async_copy(src.at[r], dst.at[r], save_x.at[r, i])

    def pair_copy(r):
        return pltpu.make_async_remote_copy(
            src_ref=kv.at[r],
            dst_ref=kv.at[r],
            send_sem=pair_send.at[r],
            recv_sem=pair_recv.at[r],
            device_id={"section": 1 - lax.axis_index("section")},
            device_id_type=MESH,
        )

    def finish(r):
        stream = mid1[r] + sums.total(r, mid2[r])
        mid2[r] = stream
        third[r] = (stream * norm_parts(stream) * gain[...]).astype(BF)

    for r in range(rows):
        gather_a.start(r)
    gather_a.forward(0)

    @pl.when(enc)
    def _():
        @pl.loop(0, rows)
        def _(r):
            gather_a.finish(r)
            for copy in block_saves(gather_a, full_a, save_a, r):
                copy.start()

            @pl.when(r > 0)
            def _():
                sums.forward(r - 1)

            for j in reversed(range(n)):
                block = gather_a.block(r, j)[...]
                gate = dot(block, w_gate[...])
                up = dot(block, w_up[...])
                hidden = (gelu_and_slope(gate)[0] * up).astype(BF)
                part = dot(hidden, w_down[...])
                if j:
                    sums.put(r, j, part)
                else:
                    mid2[r] = part

            @pl.when(r + 1 < rows)
            def _():
                gather_a.forward(r + 1)

            @pl.when(r > 0)
            def _():
                finish(r - 1)
                gather_b.start(r - 1)

        sums.forward(rows - 1)
        gather_b.forward(0)
        finish(rows - 1)
        gather_b.start(rows - 1)

        @pl.loop(0, rows)
        def _(r):
            gather_b.finish(r)
            for j in range(n):
                kv[r, j * size : (j + 1) * size, :] = dot(
                    gather_b.block(r, j)[...], w_cross[...]
                ).astype(BF)
            pair_copy(r).start()
            for copy in block_saves(gather_b, full_b, save_b, r):
                copy.start()

            @pl.when(r + 1 < rows)
            def _():
                gather_b.forward(r + 1)

        @pl.loop(0, rows)
        def _(r):
            gather_b.drain(r)
            pair_copy(r).wait_send()
            for copy in block_saves(gather_b, full_b, save_b, r):
                copy.wait()

    @pl.when(jnp.logical_not(enc))
    def _():
        for r in range(rows):
            gather_c.start(r)

        @pl.loop(0, rows)
        def _(r):
            gather_a.finish(r)
            for copy in block_saves(gather_a, full_a, save_a, r):
                copy.start()
            for j in range(n):
                q[r, j * size : (j + 1) * size, :] = dot(
                    gather_a.block(r, j)[...], w_cross[:, :hid]
                ).astype(BF)

            @pl.when(r + 1 < rows)
            def _():
                gather_a.forward(r + 1)

        @pl.loop(0, rows)
        def _(r):
            gather_c.forward(r)
            gather_c.finish(r)
            for copy in block_saves(gather_c, full_cot, save_c, r):
                copy.start()

        @pl.loop(0, rows)
        def _(r):
            pair_copy(r).wait_recv()

            @pl.when(r > 0)
            def _():
                sums.forward(r - 1)

            row = kv.at[r]
            attend_into(
                size,
                hid // DK,
                (q.at[r], 0),
                (row, 0),
                (row, hid),
                query_aug.at[r],
                key_aug.at[r],
                None,
                mix.at[r],
                aug.at[r],
            )
            for copy in cross_saves(r):
                copy.start()
            for j in reversed(range(n)):
                part = dot(mix[r, j * size : (j + 1) * size, :], w_cross[:, hid:], NT)
                if j:
                    sums.put(r, j, part)
                else:
                    mid2[r] = part

            @pl.when(r > 0)
            def _():
                finish(r - 1)

        sums.forward(rows - 1)
        finish(rows - 1)

        @pl.loop(0, rows)
        def _(r):
            gather_c.drain(r)
            for copy in block_saves(gather_c, full_cot, save_c, r):
                copy.wait()
            for copy in cross_saves(r):
                copy.wait()

    @pl.loop(0, rows)
    def _(r):
        gather_a.drain(r)
        sums.drain(r)
        for copy in block_saves(gather_a, full_a, save_a, r):
            copy.wait()


def middle_stage(n, x, cot, mid1, gain, w_gate, w_up, w_down, w_cross, query_aug, key_aug):
    rows, size, width = x.shape
    length, hid, ffd = n * size, w_cross.shape[1] // 2, w_gate.shape[1]
    slots = (rows, n - 1)
    full = ((rows, length, width), BF, False)
    head = ((rows, length, hid), BF, False)
    near = (x, cot, mid1, gain, w_gate, w_up, w_down, w_cross, query_aug, key_aug)
    return call_stage(
        functools.partial(middle_kernel, n),
        "middle_stage",
        3,
        [(a, True) for a in near],
        [
            ((rows, size, width), F32, True),
            ((rows, size, width), BF, True),
            full,
            full,
            full,
            ((rows, length, 2 * hid), BF, False),
            head,
            head,
            head,
        ],
        [
            *[pltpu.VMEM((*slots, size, width), BF)] * 5,
            pltpu.VMEM((rows, length, 2 * hid), BF),
            *[pltpu.VMEM((rows, length, hid), BF)] * 3,
            *[pltpu.SemaphoreType.DMA(slots)] * 8,
            *[pltpu.SemaphoreType.DMA((rows,))] * 2,
            *[pltpu.SemaphoreType.DMA((rows, n))] * 3,
            pltpu.SemaphoreType.DMA((rows, 4)),
        ],
        rows * length * width * ffd * 6 + rows * length * length * hid * 16,
    )


def middle_back_kernel(n, *refs):
    (third, cot, gain2, gain1, w_gate, w_up, w_down, w_cross, key_aug) = refs[:9]
    (mid1_in, mid2_in, fwd_in, cot_in, kv_in, q_in, mix_in, aug_in) = refs[9:17]
    (grad, gain_out, parts_out, full_3, full_g) = refs[17:22]
    (hidden_out, dgate_out, dup_out, dkv_out, dq_out) = refs[22:27]
    (own, got, out, back, rest, dkv) = refs[27:33]
    (mid, full, kv, q, mix, aug, dq, hidden_s, dgate_s, dup_s, part_s) = refs[33:44]
    sems = refs[44:]
    rows, size = third.shape[:2]
    hid = q.shape[1]
    enc = lax.axis_index("section") == 0
    gather_3 = Gather(n, third, got, *sems[0:2])
    gather_g = Gather(n, own, got, *sems[2:4])
    sums_a = Sums(n, out, back, *sems[4:6])
    sums_b = Sums(n, out, back, *sems[6:8])
    pair_send, pair_recv, save_3, save_g, save_f, save_p, save_d, load_m, load_f, load_x = sems[8:]
    greet(n, True)
    gain_out[...] = jnp.zeros_like(gain_out)

    def block_saves(gather, dst, sem, r):
        for j in range(n):
            yield pltpu.make_async_copy(
                gather.block(r, j), dst.at[r, pl.ds(j * size, size)], sem.at[r, j]
            )

    def pair_copy(r):
        return pltpu.make_async_remote_copy(
            src_ref=dkv.at[r],
            dst_ref=dkv.at[r],
            send_sem=pair_send.at[r],
            recv_sem=pair_recv.at[r],
            device_id={"section": 1 - lax.axis_index("section")},
            device_id_type=MESH,
        )

    def mid_load(i, source, r):
        return pltpu.make_async_copy(source.at[r], mid.at[i], load_m.at[i])

    def full_load(source, r):
        return pltpu.make_async_copy(source.at[r], full, load_f.at[0])

    def cross_loads(r):
        for i, (src, dst) in enumerate(((kv_in, kv), (q_in, q), (mix_in, mix), (aug_in, aug))):
            yield pltpu.make_async_copy(src.at[r], dst, load_x.at[i])

    def ffn_saves(r):
        for i, (src, dst) in enumerate(
            ((hidden_s, hidden_out), (dgate_s, dgate_out), (dup_s, dup_out))
        ):
            yield pltpu.make_async_copy(src, dst.at[r], save_f.at[r, i])

    def part_save(r, j):
        return pltpu.make_async_copy(
            part_s.at[j], parts_out.at[r, pl.ds(j * size, size)], save_p.at[j]
        )

    def feed_forward(r, normed_of, grad_of, sums, with_out):
        @pl.when(r > 0)
        def _():
            for copy in ffn_saves(r - 1):
                copy.wait()

        for j in reversed(range(n)):
            at = slice(j * size, (j + 1) * size)
            normed, slope_in = normed_of(j), grad_of(j)
            gate = dot(normed, w_gate[...])
            up = dot(normed, w_up[...])
            active, slope = gelu_and_slope(gate)
            hidden = (active * up).astype(BF)
            hidden_s[at, :] = hidden
            back_hidden = dot(slope_in, w_down[...], NT)
            dgate = (back_hidden * up * slope).astype(BF)
            dup = (back_hidden * active).astype(BF)
            dgate_s[at, :] = dgate
            dup_s[at, :] = dup
            part = dot(dgate, w_gate[...], NT) + dot(dup, w_up[...], NT)
            if j:
                sums.put(r, j, part)
            else:
                rest[r] = part
            if with_out:
                part = dot(hidden, w_down[...]).astype(BF)

                @pl.when(r > 0)
                def _():
                    part_save(r - 1, j).wait()

                part_s[j] = part
                part_save(r, j).start()
        for copy in ffn_saves(r):
            copy.start()

    def finish_third(r, sums, add_cot):
        mid_load(0, mid2_in, r).wait()
        arriving = sums.total(r, rest[r])
        if add_cot:
            arriving = arriving + cot[r].astype(F32)
        part, terms = norm_back_parts(mid[0], gain2[...], arriving)
        gain_out[0] += gain_terms(terms)
        if not add_cot:
            part = part + cot[r].astype(F32)
        grad[r] = part
        own[r] = part.astype(BF)

    def finish_second(r, sums):
        mid_load(1, mid1_in, r).wait()
        part, terms = norm_back_parts(mid[1], gain1[...], sums.total(r, rest[r]))
        gain_out[1] += gain_terms(terms)
        grad[r] = grad[r] + part

    last = rows - 1

    @pl.when(jnp.logical_not(enc))
    def _():
        for r in range(rows):
            gather_3.start(r)
        full_load(cot_in, 0).start()
        gather_3.forward(0)

        @pl.loop(0, rows)
        def _(r):
            gather_3.finish(r)
            for copy in block_saves(gather_3, full_3, save_3, r):
                copy.start()
            full_load(cot_in, r).wait()

            @pl.when(r > 0)
            def _():
                gather_3.drain(r - 1)
                sums_a.forward(r - 1)
                mid_load(0, mid2_in, r - 1).start()

            for copy in block_saves(gather_3, full_3, save_3, r):
                copy.wait()
            feed_forward(
                r,
                lambda j: gather_3.block(r, j)[...],
                lambda j: full[j * size : (j + 1) * size, :],
                sums_a,
                True,
            )

            @pl.when(r + 1 < rows)
            def _():
                full_load(cot_in, r + 1).start()
                gather_3.forward(r + 1)

            @pl.when(r > 0)
            def _():
                finish_third(r - 1, sums_a, False)
                gather_g.start(r - 1)

        gather_3.drain(last)
        sums_a.forward(last)
        mid_load(0, mid2_in, last).start()
        for copy in cross_loads(0):
            copy.start()
        gather_g.forward(0)
        finish_third(last, sums_a, False)
        gather_g.start(last)

        @pl.loop(0, rows)
        def _(r):
            gather_g.finish(r)
            for copy in block_saves(gather_g, full_g, save_g, r):
                copy.start()
            for j in range(n):
                at = slice(j * size, (j + 1) * size)
                full[at, :hid] = dot(gather_g.block(r, j)[...], w_cross[:, hid:]).astype(BF)
            for copy in cross_loads(r):
                copy.wait()

            @pl.when(r > 0)
            def _():
                pltpu.make_async_copy(dq, dq_out.at[r - 1], save_d.at[0]).wait()
                sums_b.forward(r - 1)
                mid_load(1, mid1_in, r - 1).start()

            attend_back_into(
                size,
                hid // DK,
                (q, 0),
                (kv, 0),
                (kv, hid),
                (full, 0),
                (mix, 0),
                (aug, 0),
                key_aug.at[r],
                None,
                (dq, 0),
                (dkv.at[r], 0),
                (dkv.at[r], hid),
            )
            pair_copy(r).start()
            pltpu.make_async_copy(dq, dq_out.at[r], save_d.at[0]).start()

            @pl.when(r + 1 < rows)
            def _():
                for copy in cross_loads(r + 1):
                    copy.start()
                gather_g.forward(r + 1)

            sums_a.drain(r)
            for j in reversed(range(n)):
                part = dot(dq[j * size : (j + 1) * size, :], w_cross[:, :hid], NT)
                if j:
                    sums_b.put(r, j, part)
                else:
                    rest[r] = part

            @pl.when(r > 0)
            def _():
                finish_second(r - 1, sums_b)

        sums_b.forward(last)
        mid_load(1, mid1_in, last).start()
        finish_second(last, sums_b)

        @pl.loop(0, rows)
        def _(r):
            pair_copy(r).wait_send()

        for j in range(n):
            part_save(last, j).wait()
        pltpu.make_async_copy(dq, dq_out.at[last], save_d.at[0]).wait()

    @pl.when(enc)
    def _():
        full_load(fwd_in, 0).start()

        @pl.loop(0, rows + 1)
        def _(t):
            @pl.when(t < rows)
            def _():
                mid_load(0, mid2_in, t).start()
                pair_copy(t).wait_recv()
                pltpu.make_async_copy(dkv.at[t], dkv_out.at[t], save_d.at[1 + t]).start()
                for j in reversed(range(n)):
                    at = slice(j * size, (j + 1) * size)
                    part = dot(dkv[t, at, :], w_cross[...], NT)
                    if j:
                        sums_a.put(t, j, part)
                    else:
                        rest[t] = part
                sums_a.forward(t)

            @pl.when(t > 0)
            def _():
                r = t - 1
                mid_load(1, mid1_in, r).start()
                gather_g.forward(r)
                gather_g.finish(r)
                for copy in block_saves(gather_g, full_g, save_g, r):
                    copy.start()
                full_load(fwd_in, r).wait()
                sums_a.drain(r)
                feed_forward(
                    r,
                    lambda j: full[j * size : (j + 1) * size, :],
                    lambda j: gather_g.block(r, j)[...],
                    sums_b,
                    False,
                )

                @pl.when(r + 1 < rows)
                def _():
                    full_load(fwd_in, r + 1).start()

            @pl.when(t < rows)
            def _():
                finish_third(t, sums_a, True)
                gather_g.start(t)

            @pl.when(t > 0)
            def _():
                sums_b.forward(t - 1)
                finish_second(t - 1, sums_b)

        @pl.loop(0, rows)
        def _(r):
            pltpu.make_async_copy(dkv.at[r], dkv_out.at[r], save_d.at[1 + r]).wait()

    for copy in ffn_saves(last):
        copy.wait()

    @pl.loop(0, rows)
    def _(r):
        gather_g.drain(r)
        sums_b.drain(r)
        for copy in block_saves(gather_g, full_g, save_g, r):
            copy.wait()


def middle_back_stage(
    n,
    third,
    cot,
    gain2,
    gain1,
    w_gate,
    w_up,
    w_down,
    w_cross,
    key_aug,
    mid1,
    mid2,
    fwd,
    full_cot,
    kv,
    q,
    mix,
    aug,
):
    rows, size, width = third.shape
    length, hid, ffd = n * size, w_cross.shape[1] // 2, w_gate.shape[1]
    slots = (rows, n - 1)
    full = ((rows, length, width), BF, False)
    unit = ((rows, length, ffd), BF, False)
    near = (third, cot, gain2, gain1, w_gate, w_up, w_down, w_cross, key_aug)
    return call_stage(
        functools.partial(middle_back_kernel, n),
        "middle_back_stage",
        4,
        [(a, True) for a in near]
        + [(a, False) for a in (mid1, mid2, fwd, full_cot, kv, q, mix, aug)],
        [
            ((rows, size, width), F32, True),
            ((2, 8, width), F32, True),
            full,
            full,
            full,
            unit,
            unit,
            unit,
            ((rows, length, 2 * hid), BF, False),
            ((rows, length, hid), BF, False),
        ],
        [
            pltpu.VMEM((rows, size, width), BF),
            *[pltpu.VMEM((*slots, size, width), BF)] * 3,
            pltpu.VMEM((rows, size, width), F32),
            pltpu.VMEM((rows, length, 2 * hid), BF),
            pltpu.VMEM((2, size, width), F32),
            pltpu.VMEM((length, width), BF),
            pltpu.VMEM((length, 2 * hid), BF),
            *[pltpu.VMEM((length, hid), BF)] * 4,
            *[pltpu.VMEM((length, ffd), BF)] * 3,
            pltpu.VMEM((n, size, width), BF),
            *[pltpu.SemaphoreType.DMA(slots)] * 8,
            *[pltpu.SemaphoreType.DMA((rows,))] * 2,
            *[pltpu.SemaphoreType.DMA((rows, n))] * 2,
            pltpu.SemaphoreType.DMA((rows, 3)),
            pltpu.SemaphoreType.DMA((n,)),
            pltpu.SemaphoreType.DMA((rows + 1,)),
            pltpu.SemaphoreType.DMA((2,)),
            pltpu.SemaphoreType.DMA((1,)),
            pltpu.SemaphoreType.DMA((4,)),
        ],
        rows * length * width * ffd * 16 + rows * length * length * hid * 40,
    )


def body(
    block_input, cotangent, segments, attn_weight, attn_out, ffn_in, ffn_out, cross_weight, gains
):
    enc = lax.axis_index("section") == 0
    idx = lax.axis_index("mp")
    n = lax.axis_size("mp")
    dp_size = lax.axis_size("dp")
    bits = [1 << b for b in range(n.bit_length() - 1)]
    size, row_count, width = block_input.shape[1:]
    length = size * n
    hid = attn_weight.shape[3]
    ffd = ffn_in.shape[3]
    rows = range(row_count)

    w_qkv = attn_weight[0].reshape(width, 3 * hid)
    w_out = attn_out[0]
    w_gate, w_up = ffn_in[0, :, 0], ffn_in[0, :, 1]
    w_down = ffn_out[0]
    w_cross = cross_weight[0].reshape(width, 2 * hid)
    gain = gains[0]
    x_low = jnp.swapaxes(block_input[0], 0, 1)
    x = x_low.astype(F32)
    cot = jnp.swapaxes(cotangent[0], 0, 1)

    order = jnp.arange(n, dtype=jnp.int32) ^ idx
    block_of = jnp.repeat(order, size)[:, None]
    lane = jnp.arange(DK, dtype=jnp.int32)
    local = jnp.concatenate(
        [lax.dynamic_slice_in_dim(segments, (idx ^ j) * size, size, axis=2) for j in range(n)],
        axis=2,
    )[..., None]
    own = jnp.where(enc, local[0], local[1])

    def query_features(seg, causal):
        doc = (lane < DOC_LANES) & (lane != seg)
        later = (lane >= BLOCK_LANE) & (lane < BLOCK_LANE + n)
        later = later & (lane - BLOCK_LANE > block_of) & causal
        return jnp.where(doc | later, BIG, 0.0).astype(BF)

    def key_features(seg):
        doc = (lane < DOC_LANES) & (lane == seg)
        ones = (lane >= OFFSET_LANE) & (lane < OFFSET_LANE + 3)
        place = lane - BLOCK_LANE == block_of
        return jnp.where(doc | ones | place, 1.0, 0.0).astype(BF)

    above = jnp.arange(size)[None, :] > jnp.arange(size)[:, None]
    tri = jnp.where(above & ~enc, BIG, 0.0).astype(F32)
    key_own, key_enc = key_features(own), key_features(local[0])

    sum1, full1, qkv1, mix1, aug1 = self_stage(
        n,
        norm_scale(x, gain[0]).astype(BF),
        w_qkv,
        w_out,
        query_features(own, ~enc),
        key_own,
        tri,
    )
    mid1 = x + sum1
    mid2, third, full_a, full_b, full_cot, kv, q, mix, aug = middle_stage(
        n,
        norm_scale(mid1, gain[1]).astype(BF),
        cot,
        mid1,
        gain[2:3],
        w_gate,
        w_up,
        w_down,
        w_cross,
        query_features(local[1], False),
        key_enc,
    )

    grad1, gain_parts, parts, full_3, full_g, hidden, dgate, dup, dkv, dq = middle_back_stage(
        n,
        third,
        cot,
        gain[2:3],
        gain[1:2],
        w_gate,
        w_up,
        w_down,
        w_cross,
        key_enc,
        mid1,
        mid2,
        full_a,
        full_cot,
        kv,
        q,
        mix,
        aug,
    )

    def contract(left, right):
        return lax.dot_general(
            left, right, (((0, 1), (0, 1)), ((), ())), preferred_element_type=F32
        ).astype(BF)

    def over_rows(total):
        return lax.psum_scatter(total, "dp", scatter_dimension=0, tiled=True).astype(F32)

    sum_ffn = lax.cond(
        enc,
        lambda: jnp.concatenate(
            [contract(full_a, dgate), contract(full_a, dup), contract(full_g, hidden)], axis=1
        ),
        lambda: jnp.concatenate(
            [contract(full_3, dgate), contract(full_3, dup), contract(full_cot, hidden)], axis=1
        ),
    )
    sum_cross = lax.cond(
        enc,
        lambda: contract(full_b, dkv),
        lambda: jnp.concatenate([contract(full_a, dq), contract(full_g, mix)], axis=1),
    )
    sum2, full_s, dqkv = self_back_stage(
        n, grad1.astype(BF), w_qkv, w_out, key_own, tri.T, qkv1, mix1, aug1
    )
    part, gain_first = norm_back(x, gain[0], sum2)
    input_grad = grad1 + part

    def across(tensor, bit):
        return lax.ppermute(tensor, "mp", [(i, i ^ bit) for i in range(n)])

    have = {j: parts[:, j * size : (j + 1) * size] for j in range(n)}
    for bit in bits:
        for j in sorted((j for j in have if j & bit), reverse=True):
            came = across(have.pop(j), bit)
            total = have[j ^ bit].astype(F32) + came.astype(F32)
            have[j ^ bit] = total if len(have) == 1 else total.astype(BF)
    block_out = jnp.where(enc, third, (mid2 + have[0].astype(F32)).astype(BF))

    sum_attn = jnp.concatenate([contract(full1, dqkv), contract(full_s, mix1), sum_cross], axis=1)
    quarter = width // dp_size
    got_ffn = over_rows(sum_ffn)
    got_attn = over_rows(sum_attn)
    out_in = jnp.stack([got_ffn[:, :ffd], got_ffn[:, ffd : 2 * ffd]], axis=1)
    out_down = got_ffn[:, 2 * ffd :].T
    out_qkv = got_attn[:, : 3 * hid].reshape(quarter, 3, hid)
    out_out = got_attn[:, 3 * hid : 4 * hid].T
    out_cross = got_attn[:, 4 * hid :].reshape(quarter, 2, hid)
    gain_parts = jnp.sum(gain_parts, axis=1)
    gain_total = lax.psum_scatter(
        jnp.stack([gain_first, gain_parts[1], gain_parts[0]]),
        ("dp", "mp"),
        scatter_dimension=1,
        tiled=True,
    )
    return (
        jnp.swapaxes(block_out, 0, 1)[None],
        jnp.swapaxes(input_grad, 0, 1)[None],
        out_qkv[None],
        out_out[None],
        out_in[None],
        out_down[None],
        out_cross[None],
        gain_total[None],
    )


def solution(mesh):
    in_specs = (
        P("section", "mp", "dp", None),
        P("section", "mp", "dp", None),
        P(None, "dp", None),
        P("section", None, None, "mp"),
        P("section", "mp", None),
        P("section", None, None, "mp"),
        P("section", "mp", None),
        P("section", None, None, "mp"),
        P("section", None, None),
    )
    out_specs = (
        P("section", "mp", "dp", None),
        P("section", "mp", "dp", None),
        P("section", "dp", None, "mp"),
        P("section", "mp", "dp"),
        P("section", "dp", None, "mp"),
        P("section", "mp", "dp"),
        P("section", "dp", None, "mp"),
        P("section", None, ("dp", "mp")),
    )
    return jax.shard_map(body, mesh=mesh, in_specs=in_specs, out_specs=out_specs, check_vma=False)
```

```python
import functools
import math

import jax
import jax.numpy as jnp
from jax import lax
from jax.experimental import pallas as pl
from jax.experimental.pallas import tpu as pltpu
from jax.sharding import PartitionSpec as P

DK = 64
EPS = 1e-06
BIG = -1e30
SCALE = DK**-0.5
LOG_SCALE = SCALE * math.log2(math.e)
BF, F32 = jnp.bfloat16, jnp.float32

DOC_LANES = 3
OFFSET_LANE = 3
BLOCK_LANE = 8

MESH = pl.DeviceIdType.MESH

NT = (((1,), (1,)), ((), ()))
NN = (((1,), (0,)), ((), ()))
TN = (((0,), (0,)), ((), ()))


def dot(a, b, dims=NN):
    return lax.dot_general(a, b, dims, preferred_element_type=F32)


def norm_scale(tensor, gain):
    return tensor * lax.rsqrt(jnp.mean(tensor * tensor, axis=-1, keepdims=True) + EPS) * gain


def norm_back(tensor, gain, gradient):
    _, pull_back = jax.vjp(norm_scale, tensor, gain)
    return pull_back(gradient)


def split_three(column):
    high = column.astype(BF)
    rest = column - high.astype(F32)
    middle = rest.astype(BF)
    low = (rest - middle.astype(F32)).astype(BF)
    return high, middle, low


def with_offsets(base, column):
    lane = lax.broadcasted_iota(jnp.int32, base.shape, 1)
    out = base.astype(F32)
    for i, piece in enumerate(split_three(column)):
        out = jnp.where(lane == OFFSET_LANE + i, piece.astype(F32), out)
    return out.astype(BF)


def low_bit(j):
    return j & -j


def flipped(index, bit):
    return index + bit - 2 * bit * lax.rem(index // bit, 2)


def greet(n, section=False):
    barrier = pltpu.get_barrier_semaphore()
    idx = lax.axis_index("mp")
    bits = [j for j in range(1, n) if j == low_bit(j)]
    for bit in bits:
        pl.semaphore_signal(
            barrier, inc=1, device_id={"mp": flipped(idx, bit)}, device_id_type=MESH
        )
    if section:
        other = 1 - lax.axis_index("section")
        pl.semaphore_signal(barrier, inc=1, device_id={"section": other}, device_id_type=MESH)
    pl.semaphore_wait(barrier, len(bits) + (1 if section else 0))


class Gather:
    def __init__(self, n, own, got, send, recv):
        self.n, self.own, self.got, self.send, self.recv = n, own, got, send, recv
        self.idx = lax.axis_index("mp")
        self.slots = range(1, n)
        self.parents = sorted({j ^ low_bit(j) for j in self.slots} - {0}, key=int.bit_count)

    def block(self, r, j):
        return self.own.at[r] if j == 0 else self.got.at[r, j - 1]

    def copy(self, r, j):
        return pltpu.make_async_remote_copy(
            src_ref=self.block(r, j ^ low_bit(j)),
            dst_ref=self.got.at[r, j - 1],
            send_sem=self.send.at[r, j - 1],
            recv_sem=self.recv.at[r, j - 1],
            device_id={"mp": flipped(self.idx, low_bit(j))},
            device_id_type=MESH,
        )

    def start(self, r):
        for j in sorted(self.slots, reverse=True):
            if j == low_bit(j):
                self.copy(r, j).start()

    def forward(self, r):
        for parent in self.parents:
            self.copy(r, parent).wait_recv()
            for j in self.slots:
                if j ^ low_bit(j) == parent:
                    self.copy(r, j).start()

    def finish(self, r):
        for j in self.slots:
            if j not in self.parents:
                self.copy(r, j).wait_recv()

    def drain(self, r):
        for j in self.slots:
            self.copy(r, j).wait_send()


class Sums:
    def __init__(self, n, out, back, send, recv):
        self.n, self.out, self.back, self.send, self.recv = n, out, back, send, recv
        self.idx = lax.axis_index("mp")
        self.slots = range(1, n)

    def copy(self, r, j):
        return pltpu.make_async_remote_copy(
            src_ref=self.out.at[r, j - 1],
            dst_ref=self.back.at[r, j - 1],
            send_sem=self.send.at[r, j - 1],
            recv_sem=self.recv.at[r, j - 1],
            device_id={"mp": flipped(self.idx, low_bit(j))},
            device_id_type=MESH,
        )

    def terms(self, j):
        limit = low_bit(j) if j else self.n
        return [j | 1 << b for b in range(self.n.bit_length()) if 1 << b < limit]

    def put(self, r, j, part):
        self.out[r, j - 1] = part.astype(BF)
        if low_bit(j) == 1:
            self.copy(r, j).start()

    def forward(self, r):
        for j in sorted(self.slots, key=low_bit):
            if low_bit(j) == 1:
                continue
            total = self.out[r, j - 1].astype(F32)
            for k in self.terms(j):
                self.copy(r, k).wait_recv()
                total = total + self.back[r, k - 1].astype(F32)
            self.out[r, j - 1] = total.astype(BF)
            self.copy(r, j).start()

    def total(self, r, own):
        for k in self.terms(0):
            self.copy(r, k).wait_recv()
            own = own + self.back[r, k - 1].astype(F32)
        return own

    def drain(self, r):
        for j in self.slots:
            self.copy(r, j).wait_send()


def attend_into(size, heads, q, k, v, query_aug, key_aug, tri, mix, aug):
    keys_aug = key_aug[...]
    blocks = mix.shape[0] // size
    lanes_of = lambda at, head: slice(at + head * DK, at + (head + 1) * DK)
    for head in range(heads):
        lanes = lanes_of(0, head)
        keys = jnp.concatenate([k[0][:, lanes_of(k[1], head)], keys_aug], axis=1)
        values = jnp.concatenate([v[0][:, lanes_of(v[1], head)], keys_aug], axis=1)
        for c in range(blocks):
            rows = slice(c * size, (c + 1) * size)
            base = query_aug[rows, :]
            query = jnp.concatenate([q[0][rows, lanes_of(q[1], head)], base], axis=1)
            scores = []
            for j in range(blocks):
                s = dot(query, keys[j * size : (j + 1) * size], NT)
                scores.append(s + tri[...] if tri is not None and j == c else s)
            top = functools.reduce(jnp.maximum, scores)
            top = jnp.max(top, axis=1, keepdims=True)
            total = None
            for j, s in enumerate(scores):
                p = jnp.exp2((s - top) * LOG_SCALE).astype(BF)
                o = dot(p, values[j * size : (j + 1) * size])
                total = o if total is None else total + o
            weight = total[:, DK + OFFSET_LANE : DK + OFFSET_LANE + 1]
            mix[rows, lanes] = (total[:, :DK] / weight).astype(BF)
            log_raw = top + jnp.log2(weight) * (1.0 / LOG_SCALE)
            aug[rows, lanes] = with_offsets(base, -log_raw)


def attend_back_into(size, heads, q, k, v, grad, mix, aug, key_aug, tri, dq, dk, dv):
    keys_aug = key_aug[...]
    length = k[0].shape[0]
    at = lambda ref, head: slice(ref[1] + head * DK, ref[1] + (head + 1) * DK)
    for head in range(heads):
        key = k[0][:, at(k, head)]
        keys = jnp.concatenate([key, keys_aug], axis=1)
        values = jnp.concatenate([v[0][:, at(v, head)], keys_aug], axis=1)
        grad_k = jnp.zeros((length, DK), F32)
        grad_v = jnp.zeros((length, DK), F32)
        for c in range(length // size):
            rows = slice(c * size, (c + 1) * size)
            query = q[0][rows, at(q, head)]
            slope_in = grad[0][rows, at(grad, head)]
            delta = jnp.sum(
                slope_in.astype(F32) * mix[0][rows, at(mix, head)].astype(F32),
                axis=1,
                keepdims=True,
            )
            queries = jnp.concatenate([query, aug[0][rows, at(aug, head)]], axis=1)
            grads = jnp.concatenate(
                [slope_in, with_offsets(jnp.zeros((size, DK), BF), -delta)], axis=1
            )
            weights, slopes = [], []
            for j in range(length // size):
                block = slice(j * size, (j + 1) * size)
                s = dot(keys[block], queries, NT)
                if tri is not None and j == c:
                    s = s + tri[...]
                p = jnp.exp2(s * LOG_SCALE)
                slope = p * dot(values[block], grads, NT)
                weights.append(p.astype(BF))
                slopes.append(slope.astype(BF))
            weights = jnp.concatenate(weights, axis=0)
            slopes = jnp.concatenate(slopes, axis=0)
            grad_v = grad_v + dot(weights, slope_in)
            grad_k = grad_k + dot(slopes, query)
            dq[0][rows, at(dq, head)] = (dot(slopes, key, TN) * SCALE).astype(BF)
        dk[0][:, at(dk, head)] = (grad_k * SCALE).astype(BF)
        dv[0][:, at(dv, head)] = grad_v.astype(BF)


GELU_A, GELU_B = math.sqrt(2.0 / math.pi), 0.044715


def gelu_and_slope(x):
    square = x * x
    t = jnp.tanh(GELU_A * x * (1.0 + GELU_B * square))
    half = 0.5 * (1.0 + t)
    slope = half + 0.5 * x * (1.0 - t * t) * (GELU_A * (1.0 + 3.0 * GELU_B * square))
    return x * half, slope


def norm_parts(stream):
    return lax.rsqrt(jnp.mean(stream * stream, axis=-1, keepdims=True) + EPS)


def norm_back_parts(stream, gain, gradient):
    root = norm_parts(stream)
    unit = stream * root
    scaled = gradient * gain
    inner = jnp.mean(scaled * unit, axis=-1, keepdims=True)
    return root * (scaled - unit * inner), gradient * unit


def gain_terms(terms):
    return jnp.sum(terms.reshape(terms.shape[0] // 8, 8, terms.shape[1]), axis=0)


VMEM_LIMIT = 60 * 1024 * 1024


def call_stage(kernel, name, number, inputs, outputs, scratch, flops):
    vmem = pl.BlockSpec(memory_space=pltpu.VMEM)
    hbm = pl.BlockSpec(memory_space=pl.ANY)
    return pl.pallas_call(
        kernel,
        in_specs=[vmem if near else hbm for _, near in inputs],
        out_specs=[vmem if near else hbm for _, _, near in outputs],
        out_shape=[jax.ShapeDtypeStruct(shape, kind) for shape, kind, _ in outputs],
        scratch_shapes=scratch,
        compiler_params=pltpu.CompilerParams(
            collective_id=number, has_side_effects=True, vmem_limit_bytes=VMEM_LIMIT
        ),
        cost_estimate=pl.CostEstimate(
            flops=flops, bytes_accessed=1 << 25, transcendentals=1 << 24
        ),
        name=name,
    )(*(array for array, _ in inputs))


def self_stage_kernel(n, *refs):
    (x, w_qkv, w_out, query_aug, key_aug, tri) = refs[:6]
    (total, full_out, qkv_out, mix_out, aug_out) = refs[6:11]
    (got, out, back, qkv, mix, aug) = refs[11:17]
    sems = refs[17:]
    rows, size = x.shape[:2]
    hid = w_out.shape[0]
    gather = Gather(n, x, got, *sems[:2])
    sums = Sums(n, out, back, *sems[2:4])
    save = sems[4]
    greet(n)

    def saves(r, which):
        for i in which:
            if i < n:
                pair = (gather.block(r, i), full_out.at[r, pl.ds(i * size, size)])
            else:
                ref, dst = ((qkv, qkv_out), (mix, mix_out), (aug, aug_out))[i - n]
                pair = (ref.at[r], dst.at[r])
            yield pltpu.make_async_copy(*pair, save.at[r, i])

    for r in range(rows):
        gather.start(r)
    gather.forward(0)

    @pl.loop(0, rows)
    def _(r):
        gather.finish(r)
        for j in range(n):
            qkv[r, j * size : (j + 1) * size, :] = dot(
                gather.block(r, j)[...], w_qkv[...]
            ).astype(BF)
        for copy in saves(r, range(n + 1)):
            copy.start()

        @pl.when(r > 0)
        def _():
            sums.forward(r - 1)

        row = qkv.at[r]
        attend_into(
            size,
            hid // DK,
            (row, 0),
            (row, hid),
            (row, 2 * hid),
            query_aug.at[r],
            key_aug.at[r],
            tri,
            mix.at[r],
            aug.at[r],
        )
        for copy in saves(r, range(n + 1, n + 3)):
            copy.start()

        @pl.when(r + 1 < rows)
        def _():
            gather.forward(r + 1)

        for j in reversed(range(n)):
            part = dot(mix[r, j * size : (j + 1) * size, :], w_out[...])
            if j:
                sums.put(r, j, part)
            else:
                total[r] = part

        @pl.when(r > 0)
        def _():
            total[r - 1] = sums.total(r - 1, total[r - 1])

    sums.forward(rows - 1)
    total[rows - 1] = sums.total(rows - 1, total[rows - 1])

    @pl.loop(0, rows)
    def _(r):
        gather.drain(r)
        sums.drain(r)
        for copy in saves(r, range(n + 3)):
            copy.wait()


def self_stage(n, x, w_qkv, w_out, query_aug, key_aug, tri):
    rows, size, width = x.shape
    length, hid = n * size, w_out.shape[0]
    slots = (rows, n - 1)
    return call_stage(
        functools.partial(self_stage_kernel, n),
        "self_stage",
        1,
        [(a, True) for a in (x, w_qkv, w_out, query_aug, key_aug, tri)],
        [
            ((rows, size, width), F32, True),
            ((rows, length, width), BF, False),
            ((rows, length, 3 * hid), BF, False),
            ((rows, length, hid), BF, False),
            ((rows, length, hid), BF, False),
        ],
        [
            *[pltpu.VMEM((*slots, size, width), BF)] * 3,
            pltpu.VMEM((rows, length, 3 * hid), BF),
            pltpu.VMEM((rows, length, hid), BF),
            pltpu.VMEM((rows, length, hid), BF),
            *[pltpu.SemaphoreType.DMA(slots)] * 4,
            pltpu.SemaphoreType.DMA((rows, n + 3)),
        ],
        rows * length * width * hid * 8 + rows * length * length * hid * 16,
    )


def self_back_kernel(n, *refs):
    (x, w_qkv, w_out, key_aug, tri_t, qkv_in, mix_in, aug_in) = refs[:8]
    (total, full_out, dqkv_out) = refs[8:11]
    (got, out, back, qkv, mix, aug, grad, dqkv) = refs[11:19]
    sems = refs[19:]
    rows, size = x.shape[:2]
    hid = w_out.shape[0]
    gather = Gather(n, x, got, *sems[:2])
    sums = Sums(n, out, back, *sems[2:4])
    save, load = sems[4:]
    greet(n)

    def loads(r):
        for i, (src, dst) in enumerate(((qkv_in, qkv), (mix_in, mix), (aug_in, aug))):
            yield pltpu.make_async_copy(src.at[r], dst.at[r], load.at[r, i])

    def saves(r, which):
        for i in which:
            if i < n:
                pair = (gather.block(r, i), full_out.at[r, pl.ds(i * size, size)])
            else:
                pair = (dqkv.at[r], dqkv_out.at[r])
            yield pltpu.make_async_copy(*pair, save.at[r, i])

    for r in range(rows):
        gather.start(r)
        for copy in loads(r):
            copy.start()
    gather.forward(0)

    @pl.loop(0, rows)
    def _(r):
        gather.finish(r)
        for j in range(n):
            grad[j * size : (j + 1) * size, :] = dot(
                gather.block(r, j)[...], w_out[...], NT
            ).astype(BF)
        for copy in saves(r, range(n)):
            copy.start()
        for copy in loads(r):
            copy.wait()

        @pl.when(r > 0)
        def _():
            sums.forward(r - 1)

        row, slope = qkv.at[r], dqkv.at[r]
        attend_back_into(
            size,
            hid // DK,
            (row, 0),
            (row, hid),
            (row, 2 * hid),
            (grad, 0),
            (mix.at[r], 0),
            (aug.at[r], 0),
            key_aug.at[r],
            tri_t,
            (slope, 0),
            (slope, hid),
            (slope, 2 * hid),
        )
        for copy in saves(r, range(n, n + 1)):
            copy.start()

        @pl.when(r + 1 < rows)
        def _():
            gather.forward(r + 1)

        for j in reversed(range(n)):
            part = dot(dqkv[r, j * size : (j + 1) * size, :], w_qkv[...], NT)
            if j:
                sums.put(r, j, part)
            else:
                total[r] = part

        @pl.when(r > 0)
        def _():
            total[r - 1] = sums.total(r - 1, total[r - 1])

    sums.forward(rows - 1)
    total[rows - 1] = sums.total(rows - 1, total[rows - 1])

    @pl.loop(0, rows)
    def _(r):
        gather.drain(r)
        sums.drain(r)
        for copy in saves(r, range(n + 1)):
            copy.wait()


def self_back_stage(n, x, w_qkv, w_out, key_aug, tri_t, qkv, mix, aug):
    rows, size, width = x.shape
    length, hid = n * size, w_out.shape[0]
    slots = (rows, n - 1)
    return call_stage(
        functools.partial(self_back_kernel, n),
        "self_back_stage",
        2,
        [(a, True) for a in (x, w_qkv, w_out, key_aug, tri_t)]
        + [(a, False) for a in (qkv, mix, aug)],
        [
            ((rows, size, width), F32, True),
            ((rows, length, width), BF, False),
            ((rows, length, 3 * hid), BF, False),
        ],
        [
            *[pltpu.VMEM((*slots, size, width), BF)] * 3,
            pltpu.VMEM((rows, length, 3 * hid), BF),
            pltpu.VMEM((rows, length, hid), BF),
            pltpu.VMEM((rows, length, hid), BF),
            pltpu.VMEM((length, hid), BF),
            pltpu.VMEM((rows, length, 3 * hid), BF),
            *[pltpu.SemaphoreType.DMA(slots)] * 4,
            pltpu.SemaphoreType.DMA((rows, n + 1)),
            pltpu.SemaphoreType.DMA((rows, 3)),
        ],
        rows * length * width * hid * 8 + rows * length * length * hid * 40,
    )


def middle_kernel(n, *refs):
    (x, cot, mid1, gain, w_gate, w_up, w_down, w_cross, query_aug, key_aug) = refs[:10]
    (mid2, third, full_a, full_b, full_cot, kv_out, q_out, mix_out, aug_out) = refs[10:19]
    (got_a, got_b, got_c, out, back, kv, q, mix, aug) = refs[19:28]
    sems = refs[28:]
    rows, size = x.shape[:2]
    hid = q.shape[2]
    enc = lax.axis_index("section") == 0
    gather_a = Gather(n, x, got_a, *sems[0:2])
    gather_b = Gather(n, third, got_b, *sems[2:4])
    gather_c = Gather(n, cot, got_c, *sems[4:6])
    sums = Sums(n, out, back, *sems[6:8])
    pair_send, pair_recv, save_a, save_b, save_c, save_x = sems[8:]
    greet(n, True)

    def block_saves(gather, dst, sem, r):
        for j in range(n):
            yield pltpu.make_async_copy(
                gather.block(r, j), dst.at[r, pl.ds(j * size, size)], sem.at[r, j]
            )

    def cross_saves(r):
        for i, (src, dst) in enumerate(
            ((kv, kv_out), (q, q_out), (mix, mix_out), (aug, aug_out))
        ):
            yield pltpu.make_async_copy(src.at[r], dst.at[r], save_x.at[r, i])

    def pair_copy(r):
        return pltpu.make_async_remote_copy(
            src_ref=kv.at[r],
            dst_ref=kv.at[r],
            send_sem=pair_send.at[r],
            recv_sem=pair_recv.at[r],
            device_id={"section": 1 - lax.axis_index("section")},
            device_id_type=MESH,
        )

    def finish(r):
        stream = mid1[r] + sums.total(r, mid2[r])
        mid2[r] = stream
        third[r] = (stream * norm_parts(stream) * gain[...]).astype(BF)

    for r in range(rows):
        gather_a.start(r)
    gather_a.forward(0)

    @pl.when(enc)
    def _():
        @pl.loop(0, rows)
        def _(r):
            gather_a.finish(r)
            for copy in block_saves(gather_a, full_a, save_a, r):
                copy.start()

            @pl.when(r > 0)
            def _():
                sums.forward(r - 1)

            for j in reversed(range(n)):
                block = gather_a.block(r, j)[...]
                gate = dot(block, w_gate[...])
                up = dot(block, w_up[...])
                hidden = (gelu_and_slope(gate)[0] * up).astype(BF)
                part = dot(hidden, w_down[...])
                if j:
                    sums.put(r, j, part)
                else:
                    mid2[r] = part

            @pl.when(r + 1 < rows)
            def _():
                gather_a.forward(r + 1)

            @pl.when(r > 0)
            def _():
                finish(r - 1)
                gather_b.start(r - 1)

        sums.forward(rows - 1)
        gather_b.forward(0)
        finish(rows - 1)
        gather_b.start(rows - 1)

        @pl.loop(0, rows)
        def _(r):
            gather_b.finish(r)
            for j in range(n):
                kv[r, j * size : (j + 1) * size, :] = dot(
                    gather_b.block(r, j)[...], w_cross[...]
                ).astype(BF)
            pair_copy(r).start()
            for copy in block_saves(gather_b, full_b, save_b, r):
                copy.start()

            @pl.when(r + 1 < rows)
            def _():
                gather_b.forward(r + 1)

        @pl.loop(0, rows)
        def _(r):
            gather_b.drain(r)
            pair_copy(r).wait_send()
            for copy in block_saves(gather_b, full_b, save_b, r):
                copy.wait()

    @pl.when(jnp.logical_not(enc))
    def _():
        for r in range(rows):
            gather_c.start(r)

        @pl.loop(0, rows)
        def _(r):
            gather_a.finish(r)
            for copy in block_saves(gather_a, full_a, save_a, r):
                copy.start()
            for j in range(n):
                q[r, j * size : (j + 1) * size, :] = dot(
                    gather_a.block(r, j)[...], w_cross[:, :hid]
                ).astype(BF)

            @pl.when(r + 1 < rows)
            def _():
                gather_a.forward(r + 1)

        @pl.loop(0, rows)
        def _(r):
            gather_c.forward(r)
            gather_c.finish(r)
            for copy in block_saves(gather_c, full_cot, save_c, r):
                copy.start()

        @pl.loop(0, rows)
        def _(r):
            pair_copy(r).wait_recv()

            @pl.when(r > 0)
            def _():
                sums.forward(r - 1)

            row = kv.at[r]
            attend_into(
                size,
                hid // DK,
                (q.at[r], 0),
                (row, 0),
                (row, hid),
                query_aug.at[r],
                key_aug.at[r],
                None,
                mix.at[r],
                aug.at[r],
            )
            for copy in cross_saves(r):
                copy.start()
            for j in reversed(range(n)):
                part = dot(mix[r, j * size : (j + 1) * size, :], w_cross[:, hid:], NT)
                if j:
                    sums.put(r, j, part)
                else:
                    mid2[r] = part

            @pl.when(r > 0)
            def _():
                finish(r - 1)

        sums.forward(rows - 1)
        finish(rows - 1)

        @pl.loop(0, rows)
        def _(r):
            gather_c.drain(r)
            for copy in block_saves(gather_c, full_cot, save_c, r):
                copy.wait()
            for copy in cross_saves(r):
                copy.wait()

    @pl.loop(0, rows)
    def _(r):
        gather_a.drain(r)
        sums.drain(r)
        for copy in block_saves(gather_a, full_a, save_a, r):
            copy.wait()


def middle_stage(n, x, cot, mid1, gain, w_gate, w_up, w_down, w_cross, query_aug, key_aug):
    rows, size, width = x.shape
    length, hid, ffd = n * size, w_cross.shape[1] // 2, w_gate.shape[1]
    slots = (rows, n - 1)
    full = ((rows, length, width), BF, False)
    head = ((rows, length, hid), BF, False)
    near = (x, cot, mid1, gain, w_gate, w_up, w_down, w_cross, query_aug, key_aug)
    return call_stage(
        functools.partial(middle_kernel, n),
        "middle_stage",
        3,
        [(a, True) for a in near],
        [
            ((rows, size, width), F32, True),
            ((rows, size, width), BF, True),
            full,
            full,
            full,
            ((rows, length, 2 * hid), BF, False),
            head,
            head,
            head,
        ],
        [
            *[pltpu.VMEM((*slots, size, width), BF)] * 5,
            pltpu.VMEM((rows, length, 2 * hid), BF),
            *[pltpu.VMEM((rows, length, hid), BF)] * 3,
            *[pltpu.SemaphoreType.DMA(slots)] * 8,
            *[pltpu.SemaphoreType.DMA((rows,))] * 2,
            *[pltpu.SemaphoreType.DMA((rows, n))] * 3,
            pltpu.SemaphoreType.DMA((rows, 4)),
        ],
        rows * length * width * ffd * 6 + rows * length * length * hid * 16,
    )


def middle_back_kernel(n, *refs):
    (third, cot, gain2, gain1, w_gate, w_up, w_down, w_cross, key_aug) = refs[:9]
    (mid1_in, mid2_in, fwd_in, cot_in, kv_in, q_in, mix_in, aug_in) = refs[9:17]
    (grad, gain_out, parts_out, full_3, full_g) = refs[17:22]
    (hidden_out, dgate_out, dup_out, dkv_out, dq_out) = refs[22:27]
    (own, got, out, back, rest, dkv) = refs[27:33]
    (mid, full, kv, q, mix, aug, dq, hidden_s, dgate_s, dup_s, part_s) = refs[33:44]
    sems = refs[44:]
    rows, size = third.shape[:2]
    hid = q.shape[1]
    enc = lax.axis_index("section") == 0
    gather_3 = Gather(n, third, got, *sems[0:2])
    gather_g = Gather(n, own, got, *sems[2:4])
    sums_a = Sums(n, out, back, *sems[4:6])
    sums_b = Sums(n, out, back, *sems[6:8])
    pair_send, pair_recv, save_3, save_g, save_f, save_p, save_d, load_m, load_f, load_x = sems[8:]
    greet(n, True)
    gain_out[...] = jnp.zeros_like(gain_out)

    def block_saves(gather, dst, sem, r):
        for j in range(n):
            yield pltpu.make_async_copy(
                gather.block(r, j), dst.at[r, pl.ds(j * size, size)], sem.at[r, j]
            )

    def pair_copy(r):
        return pltpu.make_async_remote_copy(
            src_ref=dkv.at[r],
            dst_ref=dkv.at[r],
            send_sem=pair_send.at[r],
            recv_sem=pair_recv.at[r],
            device_id={"section": 1 - lax.axis_index("section")},
            device_id_type=MESH,
        )

    def mid_load(i, source, r):
        return pltpu.make_async_copy(source.at[r], mid.at[i], load_m.at[i])

    def full_load(source, r):
        return pltpu.make_async_copy(source.at[r], full, load_f.at[0])

    def cross_loads(r):
        for i, (src, dst) in enumerate(((kv_in, kv), (q_in, q), (mix_in, mix), (aug_in, aug))):
            yield pltpu.make_async_copy(src.at[r], dst, load_x.at[i])

    def ffn_saves(r):
        for i, (src, dst) in enumerate(
            ((hidden_s, hidden_out), (dgate_s, dgate_out), (dup_s, dup_out))
        ):
            yield pltpu.make_async_copy(src, dst.at[r], save_f.at[r, i])

    def part_save(r, j):
        return pltpu.make_async_copy(
            part_s.at[j], parts_out.at[r, pl.ds(j * size, size)], save_p.at[j]
        )

    def feed_forward(r, normed_of, grad_of, sums, with_out):
        @pl.when(r > 0)
        def _():
            for copy in ffn_saves(r - 1):
                copy.wait()

        for j in reversed(range(n)):
            at = slice(j * size, (j + 1) * size)
            normed, slope_in = normed_of(j), grad_of(j)
            gate = dot(normed, w_gate[...])
            up = dot(normed, w_up[...])
            active, slope = gelu_and_slope(gate)
            hidden = (active * up).astype(BF)
            hidden_s[at, :] = hidden
            back_hidden = dot(slope_in, w_down[...], NT)
            dgate = (back_hidden * up * slope).astype(BF)
            dup = (back_hidden * active).astype(BF)
            dgate_s[at, :] = dgate
            dup_s[at, :] = dup
            part = dot(dgate, w_gate[...], NT) + dot(dup, w_up[...], NT)
            if j:
                sums.put(r, j, part)
            else:
                rest[r] = part
            if with_out:
                part = dot(hidden, w_down[...]).astype(BF)

                @pl.when(r > 0)
                def _():
                    part_save(r - 1, j).wait()

                part_s[j] = part
                part_save(r, j).start()
        for copy in ffn_saves(r):
            copy.start()

    def finish_third(r, sums, add_cot):
        mid_load(0, mid2_in, r).wait()
        arriving = sums.total(r, rest[r])
        if add_cot:
            arriving = arriving + cot[r].astype(F32)
        part, terms = norm_back_parts(mid[0], gain2[...], arriving)
        gain_out[0] += gain_terms(terms)
        if not add_cot:
            part = part + cot[r].astype(F32)
        grad[r] = part
        own[r] = part.astype(BF)

    def finish_second(r, sums):
        mid_load(1, mid1_in, r).wait()
        part, terms = norm_back_parts(mid[1], gain1[...], sums.total(r, rest[r]))
        gain_out[1] += gain_terms(terms)
        grad[r] = grad[r] + part

    last = rows - 1

    @pl.when(jnp.logical_not(enc))
    def _():
        for r in range(rows):
            gather_3.start(r)
        full_load(cot_in, 0).start()
        gather_3.forward(0)

        @pl.loop(0, rows)
        def _(r):
            gather_3.finish(r)
            for copy in block_saves(gather_3, full_3, save_3, r):
                copy.start()
            full_load(cot_in, r).wait()

            @pl.when(r > 0)
            def _():
                gather_3.drain(r - 1)
                sums_a.forward(r - 1)
                mid_load(0, mid2_in, r - 1).start()

            for copy in block_saves(gather_3, full_3, save_3, r):
                copy.wait()
            feed_forward(
                r,
                lambda j: gather_3.block(r, j)[...],
                lambda j: full[j * size : (j + 1) * size, :],
                sums_a,
                True,
            )

            @pl.when(r + 1 < rows)
            def _():
                full_load(cot_in, r + 1).start()
                gather_3.forward(r + 1)

            @pl.when(r > 0)
            def _():
                finish_third(r - 1, sums_a, False)
                gather_g.start(r - 1)

        gather_3.drain(last)
        sums_a.forward(last)
        mid_load(0, mid2_in, last).start()
        for copy in cross_loads(0):
            copy.start()
        gather_g.forward(0)
        finish_third(last, sums_a, False)
        gather_g.start(last)

        @pl.loop(0, rows)
        def _(r):
            gather_g.finish(r)
            for copy in block_saves(gather_g, full_g, save_g, r):
                copy.start()
            for j in range(n):
                at = slice(j * size, (j + 1) * size)
                full[at, :hid] = dot(gather_g.block(r, j)[...], w_cross[:, hid:]).astype(BF)
            for copy in cross_loads(r):
                copy.wait()

            @pl.when(r > 0)
            def _():
                pltpu.make_async_copy(dq, dq_out.at[r - 1], save_d.at[0]).wait()
                sums_b.forward(r - 1)
                mid_load(1, mid1_in, r - 1).start()

            attend_back_into(
                size,
                hid // DK,
                (q, 0),
                (kv, 0),
                (kv, hid),
                (full, 0),
                (mix, 0),
                (aug, 0),
                key_aug.at[r],
                None,
                (dq, 0),
                (dkv.at[r], 0),
                (dkv.at[r], hid),
            )
            pair_copy(r).start()
            pltpu.make_async_copy(dq, dq_out.at[r], save_d.at[0]).start()

            @pl.when(r + 1 < rows)
            def _():
                for copy in cross_loads(r + 1):
                    copy.start()
                gather_g.forward(r + 1)

            sums_a.drain(r)
            for j in reversed(range(n)):
                part = dot(dq[j * size : (j + 1) * size, :], w_cross[:, :hid], NT)
                if j:
                    sums_b.put(r, j, part)
                else:
                    rest[r] = part

            @pl.when(r > 0)
            def _():
                finish_second(r - 1, sums_b)

        sums_b.forward(last)
        mid_load(1, mid1_in, last).start()
        finish_second(last, sums_b)

        @pl.loop(0, rows)
        def _(r):
            pair_copy(r).wait_send()

        for j in range(n):
            part_save(last, j).wait()
        pltpu.make_async_copy(dq, dq_out.at[last], save_d.at[0]).wait()

    @pl.when(enc)
    def _():
        full_load(fwd_in, 0).start()

        @pl.loop(0, rows + 1)
        def _(t):
            @pl.when(t < rows)
            def _():
                mid_load(0, mid2_in, t).start()
                pair_copy(t).wait_recv()
                pltpu.make_async_copy(dkv.at[t], dkv_out.at[t], save_d.at[1 + t]).start()
                for j in reversed(range(n)):
                    at = slice(j * size, (j + 1) * size)
                    part = dot(dkv[t, at, :], w_cross[...], NT)
                    if j:
                        sums_a.put(t, j, part)
                    else:
                        rest[t] = part
                sums_a.forward(t)

            @pl.when(t > 0)
            def _():
                r = t - 1
                mid_load(1, mid1_in, r).start()
                gather_g.forward(r)
                gather_g.finish(r)
                for copy in block_saves(gather_g, full_g, save_g, r):
                    copy.start()
                full_load(fwd_in, r).wait()
                sums_a.drain(r)
                feed_forward(
                    r,
                    lambda j: full[j * size : (j + 1) * size, :],
                    lambda j: gather_g.block(r, j)[...],
                    sums_b,
                    False,
                )

                @pl.when(r + 1 < rows)
                def _():
                    full_load(fwd_in, r + 1).start()

            @pl.when(t < rows)
            def _():
                finish_third(t, sums_a, True)
                gather_g.start(t)

            @pl.when(t > 0)
            def _():
                sums_b.forward(t - 1)
                finish_second(t - 1, sums_b)

        @pl.loop(0, rows)
        def _(r):
            pltpu.make_async_copy(dkv.at[r], dkv_out.at[r], save_d.at[1 + r]).wait()

    for copy in ffn_saves(last):
        copy.wait()

    @pl.loop(0, rows)
    def _(r):
        gather_g.drain(r)
        sums_b.drain(r)
        for copy in block_saves(gather_g, full_g, save_g, r):
            copy.wait()


def middle_back_stage(
    n,
    third,
    cot,
    gain2,
    gain1,
    w_gate,
    w_up,
    w_down,
    w_cross,
    key_aug,
    mid1,
    mid2,
    fwd,
    full_cot,
    kv,
    q,
    mix,
    aug,
):
    rows, size, width = third.shape
    length, hid, ffd = n * size, w_cross.shape[1] // 2, w_gate.shape[1]
    slots = (rows, n - 1)
    full = ((rows, length, width), BF, False)
    unit = ((rows, length, ffd), BF, False)
    near = (third, cot, gain2, gain1, w_gate, w_up, w_down, w_cross, key_aug)
    return call_stage(
        functools.partial(middle_back_kernel, n),
        "middle_back_stage",
        4,
        [(a, True) for a in near]
        + [(a, False) for a in (mid1, mid2, fwd, full_cot, kv, q, mix, aug)],
        [
            ((rows, size, width), F32, True),
            ((2, 8, width), F32, True),
            full,
            full,
            full,
            unit,
            unit,
            unit,
            ((rows, length, 2 * hid), BF, False),
            ((rows, length, hid), BF, False),
        ],
        [
            pltpu.VMEM((rows, size, width), BF),
            *[pltpu.VMEM((*slots, size, width), BF)] * 3,
            pltpu.VMEM((rows, size, width), F32),
            pltpu.VMEM((rows, length, 2 * hid), BF),
            pltpu.VMEM((2, size, width), F32),
            pltpu.VMEM((length, width), BF),
            pltpu.VMEM((length, 2 * hid), BF),
            *[pltpu.VMEM((length, hid), BF)] * 4,
            *[pltpu.VMEM((length, ffd), BF)] * 3,
            pltpu.VMEM((n, size, width), BF),
            *[pltpu.SemaphoreType.DMA(slots)] * 8,
            *[pltpu.SemaphoreType.DMA((rows,))] * 2,
            *[pltpu.SemaphoreType.DMA((rows, n))] * 2,
            pltpu.SemaphoreType.DMA((rows, 3)),
            pltpu.SemaphoreType.DMA((n,)),
            pltpu.SemaphoreType.DMA((rows + 1,)),
            pltpu.SemaphoreType.DMA((2,)),
            pltpu.SemaphoreType.DMA((1,)),
            pltpu.SemaphoreType.DMA((4,)),
        ],
        rows * length * width * ffd * 16 + rows * length * length * hid * 40,
    )


def weight_kernel(places, stacked, *refs):
    out, acc = refs[-2:]
    at = pl.program_id(0)

    @pl.when(at == 0)
    def _():
        acc[...] = jnp.zeros_like(acc)

    for i, j, start, count in places:
        where = pl.ds(start, count)
        part = dot(refs[i][...], refs[j][...], TN)
        if stacked:
            acc[where, :] += part
        else:
            acc[:, where] += part

    @pl.when(at == pl.num_programs(0) - 1)
    def _():
        out[...] = acc[...].astype(BF)


def weight_sums(pairs, stacked):
    arrays, places, start = [], [], 0

    def index(array):
        for i, known in enumerate(arrays):
            if known is array:
                return i
        arrays.append(array)
        return len(arrays) - 1

    for a, b in pairs:
        count = (a if stacked else b).shape[-1]
        places.append((index(a), index(b), start, count))
        start += count
    flat = [a.reshape(-1, a.shape[-1]) for a in arrays]
    other = pairs[0][1 if stacked else 0].shape[-1]
    shape = (start, other) if stacked else (other, start)
    tokens, step = flat[0].shape[0], 512
    return pl.pallas_call(
        functools.partial(weight_kernel, places, stacked),
        grid=(tokens // step,),
        in_specs=[pl.BlockSpec((step, a.shape[1]), lambda i: (i, 0)) for a in flat],
        out_specs=pl.BlockSpec(shape, lambda i: (0, 0)),
        out_shape=jax.ShapeDtypeStruct(shape, BF),
        scratch_shapes=[pltpu.VMEM(shape, F32)],
        compiler_params=pltpu.CompilerParams(vmem_limit_bytes=VMEM_LIMIT),
        cost_estimate=pl.CostEstimate(
            flops=2 * tokens * start * other,
            bytes_accessed=sum(a.size for a in flat) * 2,
            transcendentals=0,
        ),
        name="weight_sums",
    )(*flat)


def body(
    block_input, cotangent, segments, attn_weight, attn_out, ffn_in, ffn_out, cross_weight, gains
):
    enc = lax.axis_index("section") == 0
    idx = lax.axis_index("mp")
    n = lax.axis_size("mp")
    dp_size = lax.axis_size("dp")
    bits = [1 << b for b in range(n.bit_length() - 1)]
    size, row_count, width = block_input.shape[1:]
    length = size * n
    hid = attn_weight.shape[3]
    ffd = ffn_in.shape[3]
    rows = range(row_count)

    w_qkv = attn_weight[0].reshape(width, 3 * hid)
    w_out = attn_out[0]
    w_gate, w_up = ffn_in[0, :, 0], ffn_in[0, :, 1]
    w_down = ffn_out[0]
    w_cross = cross_weight[0].reshape(width, 2 * hid)
    gain = gains[0]
    x_low = jnp.swapaxes(block_input[0], 0, 1)
    x = x_low.astype(F32)
    cot = jnp.swapaxes(cotangent[0], 0, 1)

    order = jnp.arange(n, dtype=jnp.int32) ^ idx
    block_of = jnp.repeat(order, size)[:, None]
    lane = jnp.arange(DK, dtype=jnp.int32)
    local = jnp.concatenate(
        [lax.dynamic_slice_in_dim(segments, (idx ^ j) * size, size, axis=2) for j in range(n)],
        axis=2,
    )[..., None]
    own = jnp.where(enc, local[0], local[1])

    def query_features(seg, causal):
        doc = (lane < DOC_LANES) & (lane != seg)
        later = (lane >= BLOCK_LANE) & (lane < BLOCK_LANE + n)
        later = later & (lane - BLOCK_LANE > block_of) & causal
        return jnp.where(doc | later, BIG, 0.0).astype(BF)

    def key_features(seg):
        doc = (lane < DOC_LANES) & (lane == seg)
        ones = (lane >= OFFSET_LANE) & (lane < OFFSET_LANE + 3)
        place = lane - BLOCK_LANE == block_of
        return jnp.where(doc | ones | place, 1.0, 0.0).astype(BF)

    above = jnp.arange(size)[None, :] > jnp.arange(size)[:, None]
    tri = jnp.where(above & ~enc, BIG, 0.0).astype(F32)
    key_own, key_enc = key_features(own), key_features(local[0])

    sum1, full1, qkv1, mix1, aug1 = self_stage(
        n,
        norm_scale(x, gain[0]).astype(BF),
        w_qkv,
        w_out,
        query_features(own, ~enc),
        key_own,
        tri,
    )
    mid1 = x + sum1
    mid2, third, full_a, full_b, full_cot, kv, q, mix, aug = middle_stage(
        n,
        norm_scale(mid1, gain[1]).astype(BF),
        cot,
        mid1,
        gain[2:3],
        w_gate,
        w_up,
        w_down,
        w_cross,
        query_features(local[1], False),
        key_enc,
    )

    grad1, gain_parts, parts, full_3, full_g, hidden, dgate, dup, dkv, dq = middle_back_stage(
        n,
        third,
        cot,
        gain[2:3],
        gain[1:2],
        w_gate,
        w_up,
        w_down,
        w_cross,
        key_enc,
        mid1,
        mid2,
        full_a,
        full_cot,
        kv,
        q,
        mix,
        aug,
    )

    def over_rows(total, dim):
        return lax.psum_scatter(total, "dp", scatter_dimension=dim, tiled=True)

    early = lax.cond(
        enc,
        lambda: weight_sums(
            [(dgate, full_a), (dup, full_a), (hidden, full_g), (dkv, full_b)], True
        ),
        lambda: weight_sums(
            [(dgate, full_3), (dup, full_3), (hidden, full_cot), (dq, full_a), (mix, full_g)],
            True,
        ),
    )
    got_early = over_rows(early, 1)

    def across(tensor, bit):
        decoder = [(n + i, n + (i ^ bit)) for i in range(n)]
        return lax.ppermute(tensor, ("section", "mp"), decoder)

    have = {j: parts[:, j * size : (j + 1) * size] for j in range(n)}
    first = None
    for bit in bits:
        for j in sorted((j for j in have if j & bit), reverse=True):
            came = across(have.pop(j), bit)
            total = have[j ^ bit].astype(F32) + came.astype(F32)
            have[j ^ bit] = total if len(have) == 1 else total.astype(BF)
        if bit == 1:
            first = have[max(have)]
    dec_out = mid2 + have[0].astype(F32)
    block_out = jnp.where(enc, third, dec_out.astype(BF))

    grad1_low, _, _ = lax.optimization_barrier((grad1.astype(BF), early, first))
    sum2, full_s, dqkv = self_back_stage(
        n, grad1_low, w_qkv, w_out, key_own, tri.T, qkv1, mix1, aug1
    )
    part, gain_first = norm_back(x, gain[0], sum2)
    input_grad = grad1 + part

    late = weight_sums([(full1, dqkv), (full_s, mix1)], False)
    late, got_early = lax.optimization_barrier((late, got_early))
    got_late = over_rows(late, 0).astype(F32)
    got_early = got_early.astype(F32)
    quarter = width // dp_size
    out_in = jnp.stack([got_early[:ffd].T, got_early[ffd : 2 * ffd].T], axis=1)
    out_down = got_early[2 * ffd : 3 * ffd]
    out_cross = got_early[3 * ffd :].T.reshape(quarter, 2, hid)
    out_qkv = got_late[:, : 3 * hid].reshape(quarter, 3, hid)
    out_out = got_late[:, 3 * hid :].T
    gain_parts = jnp.sum(gain_parts, axis=1)
    gain_total = jnp.stack([gain_first, gain_parts[1], gain_parts[0]])
    for axis, count in (("mp", n), ("dp", dp_size)):
        for bit in (1 << b for b in range(count.bit_length() - 1)):
            other = lax.ppermute(gain_total, axis, [(i, i ^ bit) for i in range(count)])
            gain_total = gain_total + other
    share = width // (n * dp_size)
    place = (lax.axis_index("dp") * n + idx) * share
    gain_total = lax.dynamic_slice_in_dim(gain_total, place, share, axis=1)
    return (
        jnp.swapaxes(block_out, 0, 1)[None],
        jnp.swapaxes(input_grad, 0, 1)[None],
        out_qkv[None],
        out_out[None],
        out_in[None],
        out_down[None],
        out_cross[None],
        gain_total[None],
    )


def solution(mesh):
    in_specs = (
        P("section", "mp", "dp", None),
        P("section", "mp", "dp", None),
        P(None, "dp", None),
        P("section", None, None, "mp"),
        P("section", "mp", None),
        P("section", None, None, "mp"),
        P("section", "mp", None),
        P("section", None, None, "mp"),
        P("section", None, None),
    )
    out_specs = (
        P("section", "mp", "dp", None),
        P("section", "mp", "dp", None),
        P("section", "dp", None, "mp"),
        P("section", "mp", "dp"),
        P("section", "dp", None, "mp"),
        P("section", "mp", "dp"),
        P("section", "dp", None, "mp"),
        P("section", None, ("dp", "mp")),
    )
    return jax.shard_map(body, mesh=mesh, in_specs=in_specs, out_specs=out_specs, check_vma=False)
```

```python
import functools
import math

import jax
import jax.numpy as jnp
from jax import lax
from jax.experimental import pallas as pl
from jax.experimental.pallas import tpu as pltpu
from jax.sharding import PartitionSpec as P

DK = 64
EPS = 1e-06
BIG = -1e30
SCALE = DK**-0.5
LOG_SCALE = SCALE * math.log2(math.e)
BF, F32 = jnp.bfloat16, jnp.float32

DOC_LANES = 3
OFFSET_LANE = 3
BLOCK_LANE = 8

MESH = pl.DeviceIdType.MESH

NT = (((1,), (1,)), ((), ()))
NN = (((1,), (0,)), ((), ()))
TN = (((0,), (0,)), ((), ()))


def dot(a, b, dims=NN):
    return lax.dot_general(a, b, dims, preferred_element_type=F32)


def norm_scale(tensor, gain):
    return tensor * lax.rsqrt(jnp.mean(tensor * tensor, axis=-1, keepdims=True) + EPS) * gain


def norm_back(tensor, gain, gradient):
    _, pull_back = jax.vjp(norm_scale, tensor, gain)
    return pull_back(gradient)


def split_three(column):
    high = column.astype(BF)
    rest = column - high.astype(F32)
    middle = rest.astype(BF)
    low = (rest - middle.astype(F32)).astype(BF)
    return high, middle, low


def with_offsets(base, column):
    lane = lax.broadcasted_iota(jnp.int32, base.shape, 1)
    out = base.astype(F32)
    for i, piece in enumerate(split_three(column)):
        out = jnp.where(lane == OFFSET_LANE + i, piece.astype(F32), out)
    return out.astype(BF)


def low_bit(j):
    return j & -j


def flipped(index, bit):
    return index + bit - 2 * bit * lax.rem(index // bit, 2)


def greet(n, section=False):
    barrier = pltpu.get_barrier_semaphore()
    idx = lax.axis_index("mp")
    bits = [j for j in range(1, n) if j == low_bit(j)]
    for bit in bits:
        pl.semaphore_signal(
            barrier, inc=1, device_id={"mp": flipped(idx, bit)}, device_id_type=MESH
        )
    if section:
        other = 1 - lax.axis_index("section")
        pl.semaphore_signal(barrier, inc=1, device_id={"section": other}, device_id_type=MESH)
    pl.semaphore_wait(barrier, len(bits) + (1 if section else 0))


class Gather:
    def __init__(self, n, own, got, send, recv):
        self.n, self.own, self.got, self.send, self.recv = n, own, got, send, recv
        self.idx = lax.axis_index("mp")
        self.slots = range(1, n)
        self.parents = sorted({j ^ low_bit(j) for j in self.slots} - {0}, key=int.bit_count)

    def block(self, r, j):
        return self.own.at[r] if j == 0 else self.got.at[r, j - 1]

    def copy(self, r, j):
        return pltpu.make_async_remote_copy(
            src_ref=self.block(r, j ^ low_bit(j)),
            dst_ref=self.got.at[r, j - 1],
            send_sem=self.send.at[r, j - 1],
            recv_sem=self.recv.at[r, j - 1],
            device_id={"mp": flipped(self.idx, low_bit(j))},
            device_id_type=MESH,
        )

    def start(self, r):
        for j in sorted(self.slots, reverse=True):
            if j == low_bit(j):
                self.copy(r, j).start()

    def forward(self, r):
        for parent in self.parents:
            self.copy(r, parent).wait_recv()
            for j in self.slots:
                if j ^ low_bit(j) == parent:
                    self.copy(r, j).start()

    def finish(self, r):
        for j in self.slots:
            if j not in self.parents:
                self.copy(r, j).wait_recv()

    def drain(self, r):
        for j in self.slots:
            self.copy(r, j).wait_send()


class Sums:
    def __init__(self, n, out, back, send, recv):
        self.n, self.out, self.back, self.send, self.recv = n, out, back, send, recv
        self.idx = lax.axis_index("mp")
        self.slots = range(1, n)

    def copy(self, r, j):
        return pltpu.make_async_remote_copy(
            src_ref=self.out.at[r, j - 1],
            dst_ref=self.back.at[r, j - 1],
            send_sem=self.send.at[r, j - 1],
            recv_sem=self.recv.at[r, j - 1],
            device_id={"mp": flipped(self.idx, low_bit(j))},
            device_id_type=MESH,
        )

    def terms(self, j):
        limit = low_bit(j) if j else self.n
        return [j | 1 << b for b in range(self.n.bit_length()) if 1 << b < limit]

    def put(self, r, j, part):
        self.out[r, j - 1] = part.astype(BF)
        if low_bit(j) == 1:
            self.copy(r, j).start()

    def forward(self, r):
        for j in sorted(self.slots, key=low_bit):
            if low_bit(j) == 1:
                continue
            total = self.out[r, j - 1].astype(F32)
            for k in self.terms(j):
                self.copy(r, k).wait_recv()
                total = total + self.back[r, k - 1].astype(F32)
            self.out[r, j - 1] = total.astype(BF)
            self.copy(r, j).start()

    def total(self, r, own):
        for k in self.terms(0):
            self.copy(r, k).wait_recv()
            own = own + self.back[r, k - 1].astype(F32)
        return own

    def drain(self, r):
        for j in self.slots:
            self.copy(r, j).wait_send()


def attend_into(size, heads, q, k, v, query_aug, key_aug, tri, mix, aug):
    keys_aug = key_aug[...]
    blocks = mix.shape[0] // size
    lanes_of = lambda at, head: slice(at + head * DK, at + (head + 1) * DK)
    for head in range(heads):
        lanes = lanes_of(0, head)
        keys = jnp.concatenate([k[0][:, lanes_of(k[1], head)], keys_aug], axis=1)
        values = jnp.concatenate([v[0][:, lanes_of(v[1], head)], keys_aug], axis=1)
        for c in range(blocks):
            rows = slice(c * size, (c + 1) * size)
            base = query_aug[rows, :]
            query = jnp.concatenate([q[0][rows, lanes_of(q[1], head)], base], axis=1)
            scores = []
            for j in range(blocks):
                s = dot(query, keys[j * size : (j + 1) * size], NT)
                scores.append(s + tri[...] if tri is not None and j == c else s)
            top = functools.reduce(jnp.maximum, scores)
            top = jnp.max(top, axis=1, keepdims=True)
            total = None
            for j, s in enumerate(scores):
                p = jnp.exp2((s - top) * LOG_SCALE).astype(BF)
                o = dot(p, values[j * size : (j + 1) * size])
                total = o if total is None else total + o
            weight = total[:, DK + OFFSET_LANE : DK + OFFSET_LANE + 1]
            mix[rows, lanes] = (total[:, :DK] / weight).astype(BF)
            log_raw = top + jnp.log2(weight) * (1.0 / LOG_SCALE)
            aug[rows, lanes] = with_offsets(base, -log_raw)


def attend_back_into(size, heads, q, k, v, grad, mix, aug, key_aug, tri, dq, dk, dv):
    keys_aug = key_aug[...]
    length = k[0].shape[0]
    at = lambda ref, head: slice(ref[1] + head * DK, ref[1] + (head + 1) * DK)
    for head in range(heads):
        key = k[0][:, at(k, head)]
        keys = jnp.concatenate([key, keys_aug], axis=1)
        values = jnp.concatenate([v[0][:, at(v, head)], keys_aug], axis=1)
        grad_k = jnp.zeros((length, DK), F32)
        grad_v = jnp.zeros((length, DK), F32)
        for c in range(length // size):
            rows = slice(c * size, (c + 1) * size)
            query = q[0][rows, at(q, head)]
            slope_in = grad[0][rows, at(grad, head)]
            delta = jnp.sum(
                slope_in.astype(F32) * mix[0][rows, at(mix, head)].astype(F32),
                axis=1,
                keepdims=True,
            )
            queries = jnp.concatenate([query, aug[0][rows, at(aug, head)]], axis=1)
            grads = jnp.concatenate(
                [slope_in, with_offsets(jnp.zeros((size, DK), BF), -delta)], axis=1
            )
            weights, slopes = [], []
            for j in range(length // size):
                block = slice(j * size, (j + 1) * size)
                s = dot(keys[block], queries, NT)
                if tri is not None and j == c:
                    s = s + tri[...]
                p = jnp.exp2(s * LOG_SCALE)
                slope = p * dot(values[block], grads, NT)
                weights.append(p.astype(BF))
                slopes.append(slope.astype(BF))
            weights = jnp.concatenate(weights, axis=0)
            slopes = jnp.concatenate(slopes, axis=0)
            grad_v = grad_v + dot(weights, slope_in)
            grad_k = grad_k + dot(slopes, query)
            dq[0][rows, at(dq, head)] = (dot(slopes, key, TN) * SCALE).astype(BF)
        dk[0][:, at(dk, head)] = (grad_k * SCALE).astype(BF)
        dv[0][:, at(dv, head)] = grad_v.astype(BF)


GELU_A, GELU_B = math.sqrt(2.0 / math.pi), 0.044715


def gelu_and_slope(x):
    square = x * x
    t = jnp.tanh(GELU_A * x * (1.0 + GELU_B * square))
    half = 0.5 * (1.0 + t)
    slope = half + 0.5 * x * (1.0 - t * t) * (GELU_A * (1.0 + 3.0 * GELU_B * square))
    return x * half, slope


def norm_parts(stream):
    return lax.rsqrt(jnp.mean(stream * stream, axis=-1, keepdims=True) + EPS)


def norm_back_parts(stream, gain, gradient):
    root = norm_parts(stream)
    unit = stream * root
    scaled = gradient * gain
    inner = jnp.mean(scaled * unit, axis=-1, keepdims=True)
    return root * (scaled - unit * inner), gradient * unit


def gain_terms(terms):
    return jnp.sum(terms.reshape(terms.shape[0] // 8, 8, terms.shape[1]), axis=0)


VMEM_LIMIT = 60 * 1024 * 1024


def call_stage(kernel, name, number, inputs, outputs, scratch, flops):
    vmem = pl.BlockSpec(memory_space=pltpu.VMEM)
    hbm = pl.BlockSpec(memory_space=pl.ANY)
    return pl.pallas_call(
        kernel,
        in_specs=[vmem if near else hbm for _, near in inputs],
        out_specs=[vmem if near else hbm for _, _, near in outputs],
        out_shape=[jax.ShapeDtypeStruct(shape, kind) for shape, kind, _ in outputs],
        scratch_shapes=scratch,
        compiler_params=pltpu.CompilerParams(
            collective_id=number, has_side_effects=True, vmem_limit_bytes=VMEM_LIMIT
        ),
        cost_estimate=pl.CostEstimate(
            flops=flops, bytes_accessed=1 << 25, transcendentals=1 << 24
        ),
        name=name,
    )(*(array for array, _ in inputs))


def self_stage_kernel(n, *refs):
    (x, gain, w_qkv, w_out, query_aug, key_aug, tri) = refs[:7]
    (total, normed, full_out, qkv_out, mix_out, aug_out) = refs[7:13]
    (own, got, out, back, qkv, mix, aug) = refs[13:20]
    sems = refs[20:]
    rows, size = x.shape[:2]
    hid = w_out.shape[0]
    gather = Gather(n, own, got, *sems[:2])
    sums = Sums(n, out, back, *sems[2:4])
    save = sems[4]
    greet(n)

    def saves(r, which):
        for i in which:
            if i < n:
                pair = (gather.block(r, i), full_out.at[r, pl.ds(i * size, size)])
            else:
                ref, dst = ((qkv, qkv_out), (mix, mix_out), (aug, aug_out))[i - n]
                pair = (ref.at[r], dst.at[r])
            yield pltpu.make_async_copy(*pair, save.at[r, i])

    def finish(r):
        stream = x[r].astype(F32) + sums.total(r, total[r])
        total[r] = stream
        normed[r] = (stream * norm_parts(stream) * gain[1:2]).astype(BF)

    for r in range(rows):
        stream = x[r].astype(F32)
        own[r] = (stream * norm_parts(stream) * gain[0:1]).astype(BF)
        gather.start(r)
    gather.forward(0)

    @pl.loop(0, rows)
    def _(r):
        gather.finish(r)
        for j in range(n):
            qkv[r, j * size : (j + 1) * size, :] = dot(
                gather.block(r, j)[...], w_qkv[...]
            ).astype(BF)
        for copy in saves(r, range(n + 1)):
            copy.start()

        @pl.when(r > 0)
        def _():
            sums.forward(r - 1)

        row = qkv.at[r]
        attend_into(
            size,
            hid // DK,
            (row, 0),
            (row, hid),
            (row, 2 * hid),
            query_aug.at[r],
            key_aug.at[r],
            tri,
            mix.at[r],
            aug.at[r],
        )
        for copy in saves(r, range(n + 1, n + 3)):
            copy.start()

        @pl.when(r + 1 < rows)
        def _():
            gather.forward(r + 1)

        for j in reversed(range(n)):
            part = dot(mix[r, j * size : (j + 1) * size, :], w_out[...])
            if j:
                sums.put(r, j, part)
            else:
                total[r] = part

        @pl.when(r > 0)
        def _():
            finish(r - 1)

    sums.forward(rows - 1)
    finish(rows - 1)

    @pl.loop(0, rows)
    def _(r):
        gather.drain(r)
        sums.drain(r)
        for copy in saves(r, range(n + 3)):
            copy.wait()


def self_stage(n, x, gain, w_qkv, w_out, query_aug, key_aug, tri):
    rows, size, width = x.shape
    length, hid = n * size, w_out.shape[0]
    slots = (rows, n - 1)
    return call_stage(
        functools.partial(self_stage_kernel, n),
        "self_stage",
        1,
        [(a, True) for a in (x, gain, w_qkv, w_out, query_aug, key_aug, tri)],
        [
            ((rows, size, width), F32, True),
            ((rows, size, width), BF, True),
            ((rows, length, width), BF, False),
            ((rows, length, 3 * hid), BF, False),
            ((rows, length, hid), BF, False),
            ((rows, length, hid), BF, False),
        ],
        [
            pltpu.VMEM((rows, size, width), BF),
            *[pltpu.VMEM((*slots, size, width), BF)] * 3,
            pltpu.VMEM((rows, length, 3 * hid), BF),
            pltpu.VMEM((rows, length, hid), BF),
            pltpu.VMEM((rows, length, hid), BF),
            *[pltpu.SemaphoreType.DMA(slots)] * 4,
            pltpu.SemaphoreType.DMA((rows, n + 3)),
        ],
        rows * length * width * hid * 8 + rows * length * length * hid * 16,
    )


def self_back_kernel(n, *refs):
    (x, gain, slope, w_qkv, w_out, key_aug, tri_t, qkv_in, mix_in, aug_in, full_in) = refs[:11]
    (total, gain_out, weights) = refs[11:14]
    (own, got, out, back, qkv, mix, aug, grad, dqkv, full, acc) = refs[14:25]
    sems = refs[25:]
    rows, size = x.shape[:2]
    hid = w_out.shape[0]
    gather = Gather(n, own, got, *sems[:2])
    sums = Sums(n, out, back, *sems[2:4])
    load, load_full = sems[4:]
    greet(n)

    def loads(r):
        for i, (src, dst) in enumerate(((qkv_in, qkv), (mix_in, mix), (aug_in, aug))):
            yield pltpu.make_async_copy(src.at[r], dst.at[r], load.at[r, i])

    def full_load(r):
        return pltpu.make_async_copy(full_in.at[r], full, load_full.at[0])

    def add_weights(r):
        full_load(r).wait()
        acc[:, : 3 * hid] += dot(full[...], dqkv[r], TN)
        acc[:, 3 * hid :] += functools.reduce(
            jnp.add,
            [
                dot(gather.block(r, j)[...], mix[r, j * size : (j + 1) * size, :], TN)
                for j in range(n)
            ],
        )

    def finish(r):
        part, terms = norm_back_parts(
            x[r].astype(F32), gain[0:1], sums.total(r, total[r])
        )
        gain_out[...] += gain_terms(terms)
        total[r] = slope[r] + part

    for r in range(rows):
        own[r] = slope[r].astype(BF)
        gather.start(r)
        for copy in loads(r):
            copy.start()
    full_load(0).start()
    gain_out[...] = jnp.zeros_like(gain_out)
    acc[...] = jnp.zeros_like(acc)
    gather.forward(0)

    @pl.loop(0, rows)
    def _(r):
        gather.finish(r)
        for j in range(n):
            grad[j * size : (j + 1) * size, :] = dot(
                gather.block(r, j)[...], w_out[...], NT
            ).astype(BF)
        for copy in loads(r):
            copy.wait()

        @pl.when(r > 0)
        def _():
            sums.forward(r - 1)

        row, result = qkv.at[r], dqkv.at[r]
        attend_back_into(
            size,
            hid // DK,
            (row, 0),
            (row, hid),
            (row, 2 * hid),
            (grad, 0),
            (mix.at[r], 0),
            (aug.at[r], 0),
            key_aug.at[r],
            tri_t,
            (result, 0),
            (result, hid),
            (result, 2 * hid),
        )

        @pl.when(r + 1 < rows)
        def _():
            gather.forward(r + 1)

        for j in reversed(range(n)):
            part = dot(dqkv[r, j * size : (j + 1) * size, :], w_qkv[...], NT)
            if j:
                sums.put(r, j, part)
            else:
                total[r] = part

        @pl.when(r > 0)
        def _():
            add_weights(r - 1)
            full_load(r).start()
            finish(r - 1)

    sums.forward(rows - 1)
    add_weights(rows - 1)
    weights[...] = acc[...].astype(BF)
    finish(rows - 1)

    @pl.loop(0, rows)
    def _(r):
        gather.drain(r)
        sums.drain(r)


def self_back_stage(n, x, gain, slope, w_qkv, w_out, key_aug, tri_t, qkv, mix, aug, full):
    rows, size, width = x.shape
    length, hid = n * size, w_out.shape[0]
    slots = (rows, n - 1)
    return call_stage(
        functools.partial(self_back_kernel, n),
        "self_back_stage",
        2,
        [(a, True) for a in (x, gain, slope, w_qkv, w_out, key_aug, tri_t)]
        + [(a, False) for a in (qkv, mix, aug, full)],
        [
            ((rows, size, width), F32, True),
            ((8, width), F32, True),
            ((width, 4 * hid), BF, True),
        ],
        [
            pltpu.VMEM((rows, size, width), BF),
            *[pltpu.VMEM((*slots, size, width), BF)] * 3,
            pltpu.VMEM((rows, length, 3 * hid), BF),
            pltpu.VMEM((rows, length, hid), BF),
            pltpu.VMEM((rows, length, hid), BF),
            pltpu.VMEM((length, hid), BF),
            pltpu.VMEM((rows, length, 3 * hid), BF),
            pltpu.VMEM((length, width), BF),
            pltpu.VMEM((width, 4 * hid), F32),
            *[pltpu.SemaphoreType.DMA(slots)] * 4,
            pltpu.SemaphoreType.DMA((rows, 3)),
            pltpu.SemaphoreType.DMA((1,)),
        ],
        rows * length * width * hid * 8 + rows * length * length * hid * 40,
    )


def middle_kernel(n, *refs):
    (x, cot, mid1, gain, w_gate, w_up, w_down, w_cross, query_aug, key_aug) = refs[:10]
    (mid2, third, full_a, full_b, full_cot, full_t, w_kv_out) = refs[10:17]
    (kv_out, q_out, mix_out, aug_out) = refs[17:21]
    (got_a, got_b, got_c, out, back, memory, w_kv, kv, q, mix, aug) = refs[21:32]
    sems = refs[32:]
    rows, size = x.shape[:2]
    hid = q.shape[2]
    enc = lax.axis_index("section") == 0
    gather_a = Gather(n, x, got_a, *sems[0:2])
    gather_b = Gather(n, memory, got_b, *sems[2:4])
    gather_c = Gather(n, cot, got_c, *sems[4:6])
    sums = Sums(n, out, back, *sems[6:8])
    gather_t = Gather(n, third, got_a, *sems[8:10])
    pair_send, pair_recv, save_a, save_b, save_c, save_t, save_x, weight_sems = sems[10:]
    greet(n, True)
    weight_copy = pltpu.make_async_remote_copy(
        src_ref=w_cross,
        dst_ref=w_kv,
        send_sem=weight_sems.at[0],
        recv_sem=weight_sems.at[1],
        device_id={"section": 1 - lax.axis_index("section")},
        device_id_type=MESH,
    )
    weight_save = pltpu.make_async_copy(w_kv, w_kv_out, weight_sems.at[2])

    def block_saves(gather, dst, sem, r):
        for j in range(n):
            yield pltpu.make_async_copy(
                gather.block(r, j), dst.at[r, pl.ds(j * size, size)], sem.at[r, j]
            )

    def cross_saves(r):
        for i, (src, dst) in enumerate(
            ((kv, kv_out), (q, q_out), (mix, mix_out), (aug, aug_out))
        ):
            yield pltpu.make_async_copy(src.at[r], dst.at[r], save_x.at[r, i])

    def pair_copy(r):
        return pltpu.make_async_remote_copy(
            src_ref=third.at[r],
            dst_ref=memory.at[r],
            send_sem=pair_send.at[r],
            recv_sem=pair_recv.at[r],
            device_id={"section": 1 - lax.axis_index("section")},
            device_id_type=MESH,
        )

    def finish(r):
        stream = mid1[r] + sums.total(r, mid2[r])
        mid2[r] = stream
        third[r] = (stream * norm_parts(stream) * gain[...]).astype(BF)

    for r in range(rows):
        gather_a.start(r)
    gather_a.forward(0)

    @pl.when(enc)
    def _():
        weight_copy.start()

        @pl.loop(0, rows)
        def _(r):
            gather_a.finish(r)
            for copy in block_saves(gather_a, full_a, save_a, r):
                copy.start()

            @pl.when(r > 0)
            def _():
                sums.forward(r - 1)

            for j in reversed(range(n)):
                block = gather_a.block(r, j)[...]
                gate = dot(block, w_gate[...])
                up = dot(block, w_up[...])
                hidden = (gelu_and_slope(gate)[0] * up).astype(BF)
                part = dot(hidden, w_down[...])
                if j:
                    sums.put(r, j, part)
                else:
                    mid2[r] = part

            @pl.when(r + 1 < rows)
            def _():
                gather_a.forward(r + 1)

            @pl.when(r > 0)
            def _():
                finish(r - 1)
                pair_copy(r - 1).start()

        sums.forward(rows - 1)
        finish(rows - 1)
        pair_copy(rows - 1).start()

        @pl.loop(0, rows)
        def _(r):
            pair_copy(r).wait_send()
            gather_a.drain(r)
            for copy in block_saves(gather_a, full_a, save_a, r):
                copy.wait()

        weight_copy.wait_send()

    @pl.when(jnp.logical_not(enc))
    def _():
        for r in range(rows):
            gather_c.start(r)

        @pl.loop(0, rows)
        def _(r):
            gather_a.finish(r)
            for copy in block_saves(gather_a, full_a, save_a, r):
                copy.start()
            for j in range(n):
                q[r, j * size : (j + 1) * size, :] = dot(
                    gather_a.block(r, j)[...], w_cross[:, :hid]
                ).astype(BF)

            @pl.when(r + 1 < rows)
            def _():
                gather_a.forward(r + 1)

        @pl.loop(0, rows)
        def _(r):
            gather_c.forward(r)
            gather_c.finish(r)
            for copy in block_saves(gather_c, full_cot, save_c, r):
                copy.start()

        def launch(r):
            pair_copy(r).wait_recv()
            gather_b.start(r)

        weight_copy.wait_recv()
        weight_save.start()
        for r in range(min(2, rows)):
            launch(r)
        gather_b.forward(0)

        @pl.loop(0, rows)
        def _(r):
            gather_b.finish(r)
            for copy in block_saves(gather_b, full_b, save_b, r):
                copy.start()
            for j in range(n):
                kv[r, j * size : (j + 1) * size, :] = dot(
                    gather_b.block(r, j)[...], w_kv[...]
                ).astype(BF)

            @pl.when(r > 0)
            def _():
                sums.forward(r - 1)

            @pl.when(r + 2 < rows)
            def _():
                launch(r + 2)

            row = kv.at[r]
            attend_into(
                size,
                hid // DK,
                (q.at[r], 0),
                (row, 0),
                (row, hid),
                query_aug.at[r],
                key_aug.at[r],
                None,
                mix.at[r],
                aug.at[r],
            )
            for copy in cross_saves(r):
                copy.start()

            @pl.when(r + 1 < rows)
            def _():
                gather_b.forward(r + 1)

            gather_a.drain(r)
            for copy in block_saves(gather_a, full_a, save_a, r):
                copy.wait()
            for j in reversed(range(n)):
                part = dot(mix[r, j * size : (j + 1) * size, :], w_cross[:, hid:], NT)
                if j:
                    sums.put(r, j, part)
                else:
                    mid2[r] = part

            @pl.when(r > 0)
            def _():
                finish(r - 1)

            @pl.when(r == 1)
            def _():
                gather_t.start(0)

            @pl.when(r == 2)
            def _():
                gather_t.forward(0)

        sums.forward(rows - 1)
        if rows > 1:
            if rows == 2:
                gather_t.forward(0)
            gather_t.finish(0)
            for copy in block_saves(gather_t, full_t, save_t, 0):
                copy.start()
        finish(rows - 1)
        if rows > 1:
            gather_t.drain(0)
            for copy in block_saves(gather_t, full_t, save_t, 0):
                copy.wait()

        weight_save.wait()

        @pl.loop(0, rows)
        def _(r):
            gather_b.drain(r)
            for copy in block_saves(gather_b, full_b, save_b, r):
                copy.wait()
            gather_c.drain(r)
            for copy in block_saves(gather_c, full_cot, save_c, r):
                copy.wait()
            for copy in cross_saves(r):
                copy.wait()

    @pl.loop(0, rows)
    def _(r):
        sums.drain(r)


def middle_stage(n, x, cot, mid1, gain, w_gate, w_up, w_down, w_cross, query_aug, key_aug):
    rows, size, width = x.shape
    length, hid, ffd = n * size, w_cross.shape[1] // 2, w_gate.shape[1]
    slots = (rows, n - 1)
    full = ((rows, length, width), BF, False)
    head = ((rows, length, hid), BF, False)
    near = (x, cot, mid1, gain, w_gate, w_up, w_down, w_cross, query_aug, key_aug)
    return call_stage(
        functools.partial(middle_kernel, n),
        "middle_stage",
        3,
        [(a, True) for a in near],
        [
            ((rows, size, width), F32, True),
            ((rows, size, width), BF, True),
            full,
            full,
            full,
            full,
            ((width, 2 * hid), BF, False),
            ((rows, length, 2 * hid), BF, False),
            head,
            head,
            head,
        ],
        [
            *[pltpu.VMEM((*slots, size, width), BF)] * 5,
            pltpu.VMEM((rows, size, width), BF),
            pltpu.VMEM((width, 2 * hid), BF),
            pltpu.VMEM((rows, length, 2 * hid), BF),
            *[pltpu.VMEM((rows, length, hid), BF)] * 3,
            *[pltpu.SemaphoreType.DMA(slots)] * 10,
            *[pltpu.SemaphoreType.DMA((rows,))] * 2,
            *[pltpu.SemaphoreType.DMA((rows, n))] * 4,
            pltpu.SemaphoreType.DMA((rows, 4)),
            pltpu.SemaphoreType.DMA((3,)),
        ],
        rows * length * width * ffd * 6 + rows * length * length * hid * 16,
    )


def middle_back_kernel(n, *refs):
    (third, cot, gain2, gain1, w_gate, w_up, w_down, w_cross, w_kv, key_aug) = refs[:10]
    (mid1_in, mid2_in, fwd_in, cot_in, third_in) = refs[10:15]
    (kv_in, q_in, mix_in, aug_in) = refs[15:19]
    (grad, gain_out, parts_out, full_3, full_g) = refs[19:24]
    (hidden_out, dgate_out, dup_out, dkv_out, dq_out) = refs[24:29]
    (own, got, out, back, rest, dmem) = refs[29:35]
    (mid, full, kv, q, mix, aug, dq, dkv, hidden_s, dgate_s, dup_s, part_s) = refs[35:47]
    ready = refs[47]
    sems = refs[48:]
    rows, size = third.shape[:2]
    hid = q.shape[1]
    enc = lax.axis_index("section") == 0
    gather_3 = Gather(n, third, got, *sems[0:2])
    gather_g = Gather(n, own, got, *sems[2:4])
    sums_a = Sums(n, out, back, *sems[4:6])
    sums_b = Sums(n, out, back, *sems[6:8])
    sums_m = Sums(n, out, back, *sems[8:10])
    pair_send, pair_recv, save_3, save_g, save_f, save_p, save_d, load_m, load_f, load_x = sems[10:]
    greet(n, True)
    gain_out[...] = jnp.zeros_like(gain_out)

    def block_saves(gather, dst, sem, r):
        for j in range(n):
            yield pltpu.make_async_copy(
                gather.block(r, j), dst.at[r, pl.ds(j * size, size)], sem.at[r, j]
            )

    def pair_copy(r):
        return pltpu.make_async_remote_copy(
            src_ref=dmem.at[r],
            dst_ref=dmem.at[r],
            send_sem=pair_send.at[r],
            recv_sem=pair_recv.at[r],
            device_id={"section": 1 - lax.axis_index("section")},
            device_id_type=MESH,
        )

    def mid_load(i, source, r):
        return pltpu.make_async_copy(source.at[r], mid.at[i], load_m.at[i])

    def full_load(source, r):
        return pltpu.make_async_copy(source.at[r], full, load_f.at[0])

    def cross_loads(r):
        for i, (src, dst) in enumerate(((kv_in, kv), (q_in, q), (mix_in, mix), (aug_in, aug))):
            yield pltpu.make_async_copy(src.at[r], dst, load_x.at[i])

    def ffn_saves(r):
        for i, (src, dst) in enumerate(
            ((hidden_s, hidden_out), (dgate_s, dgate_out), (dup_s, dup_out))
        ):
            yield pltpu.make_async_copy(src, dst.at[r], save_f.at[r, i])

    def part_save(r, j):
        return pltpu.make_async_copy(
            part_s.at[j], parts_out.at[r, pl.ds(j * size, size)], save_p.at[j]
        )

    def feed_forward(r, normed_of, grad_of, sums, with_out):
        @pl.when(r > 0)
        def _():
            for copy in ffn_saves(r - 1):
                copy.wait()

        for j in reversed(range(n)):
            at = slice(j * size, (j + 1) * size)
            normed, slope_in = normed_of(j), grad_of(j)
            gate = dot(normed, w_gate[...])
            up = dot(normed, w_up[...])
            active, slope = gelu_and_slope(gate)
            hidden = (active * up).astype(BF)
            hidden_s[at, :] = hidden
            back_hidden = dot(slope_in, w_down[...], NT)
            dgate = (back_hidden * up * slope).astype(BF)
            dup = (back_hidden * active).astype(BF)
            dgate_s[at, :] = dgate
            dup_s[at, :] = dup
            part = dot(dgate, w_gate[...], NT) + dot(dup, w_up[...], NT)
            if j:
                sums.put(r, j, part)
            else:
                rest[r] = part
            if with_out:
                part = dot(hidden, w_down[...]).astype(BF)

                @pl.when(r > 0)
                def _():
                    part_save(r - 1, j).wait()

                part_s[j] = part
                part_save(r, j).start()
        for copy in ffn_saves(r):
            copy.start()

    def finish_third(r, sums, add_cot):
        mid_load(0, mid2_in, r).wait()
        if add_cot:
            arriving = dmem[r].astype(F32) + cot[r].astype(F32)
        else:
            arriving = sums.total(r, rest[r])
        part, terms = norm_back_parts(mid[0], gain2[...], arriving)
        gain_out[0] += gain_terms(terms)
        if not add_cot:
            part = part + cot[r].astype(F32)
        grad[r] = part
        own[r] = part.astype(BF)

    def dkv_save(r):
        return pltpu.make_async_copy(dkv, dkv_out.at[r], save_d.at[0])

    def dq_save(r):
        return pltpu.make_async_copy(dq.at[r], dq_out.at[r], save_d.at[1 + r])

    def finish_memory(r):
        dmem[r] = sums_m.total(r, rest[r]).astype(BF)
        pair_copy(r).start()

    def finish_second(r, sums):
        mid_load(1, mid1_in, r).wait()
        part, terms = norm_back_parts(mid[1], gain1[...], sums.total(r, rest[r]))
        gain_out[1] += gain_terms(terms)
        grad[r] = grad[r] + part

    last = rows - 1

    @pl.when(jnp.logical_not(enc))
    def _():
        def third_loads(r):
            for j in range(1, n):
                yield pltpu.make_async_copy(
                    third_in.at[r, pl.ds(j * size, size)], got.at[r, j - 1], save_3.at[r, j]
                )

        ahead = 1 if rows > 1 else 0
        for r in range(ahead, rows):
            gather_3.start(r)
        full_load(cot_in, 0).start()
        if ahead:
            for copy in third_loads(0):
                copy.start()
        else:
            gather_3.forward(0)

        @pl.loop(0, rows)
        def _(r):
            @pl.when(r < ahead)
            def _():
                for copy in third_loads(r):
                    copy.wait()

            @pl.when(r >= ahead)
            def _():
                gather_3.finish(r)

            for copy in block_saves(gather_3, full_3, save_3, r):
                copy.start()
            full_load(cot_in, r).wait()

            @pl.when(r > ahead)
            def _():
                gather_3.drain(r - 1)

            @pl.when(r > 0)
            def _():
                sums_a.forward(r - 1)
                mid_load(0, mid2_in, r - 1).start()

            for copy in block_saves(gather_3, full_3, save_3, r):
                copy.wait()
            feed_forward(
                r,
                lambda j: gather_3.block(r, j)[...],
                lambda j: full[j * size : (j + 1) * size, :],
                sums_a,
                True,
            )

            @pl.when(r + 1 < rows)
            def _():
                full_load(cot_in, r + 1).start()
                gather_3.forward(r + 1)

            @pl.when(r > 0)
            def _():
                finish_third(r - 1, sums_a, False)
                gather_g.start(r - 1)

        gather_3.drain(last)
        sums_a.forward(last)
        mid_load(0, mid2_in, last).start()
        for copy in cross_loads(0):
            copy.start()
        gather_g.forward(0)
        finish_third(last, sums_a, False)
        gather_g.start(last)

        @pl.loop(0, rows)
        def _(r):
            gather_g.finish(r)
            for copy in block_saves(gather_g, full_g, save_g, r):
                copy.start()
            for j in range(n):
                at = slice(j * size, (j + 1) * size)
                full[at, :hid] = dot(gather_g.block(r, j)[...], w_cross[:, hid:]).astype(BF)
            for copy in cross_loads(r):
                copy.wait()

            @pl.when(r > 0)
            def _():
                dkv_save(r - 1).wait()
                sums_m.forward(r - 1)

            attend_back_into(
                size,
                hid // DK,
                (q, 0),
                (kv, 0),
                (kv, hid),
                (full, 0),
                (mix, 0),
                (aug, 0),
                key_aug.at[r],
                None,
                (dq.at[r], 0),
                (dkv, 0),
                (dkv, hid),
            )
            dkv_save(r).start()
            dq_save(r).start()

            @pl.when(r + 1 < rows)
            def _():
                for copy in cross_loads(r + 1):
                    copy.start()
                gather_g.forward(r + 1)

            sums_a.drain(r)
            for j in reversed(range(n)):
                part = dot(dkv[j * size : (j + 1) * size, :], w_kv[...], NT)
                if j:
                    sums_m.put(r, j, part)
                else:
                    rest[r] = part

            @pl.when(r > 0)
            def _():
                finish_memory(r - 1)

        sums_m.forward(last)
        finish_memory(last)

        idx = lax.axis_index("mp")
        bits = [j for j in range(1, n) if j == low_bit(j)]
        for bit in bits:
            pl.semaphore_signal(
                ready, inc=1, device_id={"mp": flipped(idx, bit)}, device_id_type=MESH
            )
        pl.semaphore_wait(ready, len(bits))

        @pl.loop(0, rows)
        def _(r):
            sums_m.drain(r)

            @pl.when(r > 0)
            def _():
                mid_load(1, mid1_in, r - 1).start()

            for j in reversed(range(n)):
                part = dot(dq[r, j * size : (j + 1) * size, :], w_cross[:, :hid], NT)
                if j:
                    sums_b.put(r, j, part)
                else:
                    rest[r] = part

            @pl.when(r > 0)
            def _():
                sums_b.forward(r - 1)
                finish_second(r - 1, sums_b)

        sums_b.forward(last)
        mid_load(1, mid1_in, last).start()
        finish_second(last, sums_b)

        @pl.loop(0, rows)
        def _(r):
            pair_copy(r).wait_send()
            dq_save(r).wait()

        for j in range(n):
            part_save(last, j).wait()
        dkv_save(last).wait()

    @pl.when(enc)
    def _():
        full_load(fwd_in, 0).start()

        @pl.loop(0, rows + 1)
        def _(t):
            @pl.when(t < rows)
            def _():
                mid_load(0, mid2_in, t).start()
                pair_copy(t).wait_recv()
                finish_third(t, None, True)
                gather_g.start(t)

            @pl.when(t > 0)
            def _():
                r = t - 1
                mid_load(1, mid1_in, r).start()
                gather_g.forward(r)
                gather_g.finish(r)
                for copy in block_saves(gather_g, full_g, save_g, r):
                    copy.start()
                full_load(fwd_in, r).wait()
                feed_forward(
                    r,
                    lambda j: full[j * size : (j + 1) * size, :],
                    lambda j: gather_g.block(r, j)[...],
                    sums_b,
                    False,
                )

                @pl.when(r + 1 < rows)
                def _():
                    full_load(fwd_in, r + 1).start()

                sums_b.forward(r)
                finish_second(r, sums_b)

    for copy in ffn_saves(last):
        copy.wait()

    @pl.loop(0, rows)
    def _(r):
        gather_g.drain(r)
        sums_b.drain(r)
        for copy in block_saves(gather_g, full_g, save_g, r):
            copy.wait()


def middle_back_stage(
    n,
    third,
    cot,
    gain2,
    gain1,
    w_gate,
    w_up,
    w_down,
    w_cross,
    w_kv,
    key_aug,
    mid1,
    mid2,
    fwd,
    full_cot,
    full_t,
    kv,
    q,
    mix,
    aug,
):
    rows, size, width = third.shape
    length, hid, ffd = n * size, w_cross.shape[1] // 2, w_gate.shape[1]
    slots = (rows, n - 1)
    full = ((rows, length, width), BF, False)
    unit = ((rows, length, ffd), BF, False)
    near = (third, cot, gain2, gain1, w_gate, w_up, w_down, w_cross, w_kv, key_aug)
    return call_stage(
        functools.partial(middle_back_kernel, n),
        "middle_back_stage",
        4,
        [(a, True) for a in near]
        + [(a, False) for a in (mid1, mid2, fwd, full_cot, full_t, kv, q, mix, aug)],
        [
            ((rows, size, width), F32, True),
            ((2, 8, width), F32, True),
            full,
            full,
            full,
            unit,
            unit,
            unit,
            ((rows, length, 2 * hid), BF, False),
            ((rows, length, hid), BF, False),
        ],
        [
            pltpu.VMEM((rows, size, width), BF),
            *[pltpu.VMEM((*slots, size, width), BF)] * 3,
            pltpu.VMEM((rows, size, width), F32),
            pltpu.VMEM((rows, size, width), BF),
            pltpu.VMEM((2, size, width), F32),
            pltpu.VMEM((length, width), BF),
            pltpu.VMEM((length, 2 * hid), BF),
            *[pltpu.VMEM((length, hid), BF)] * 3,
            pltpu.VMEM((rows, length, hid), BF),
            pltpu.VMEM((length, 2 * hid), BF),
            *[pltpu.VMEM((length, ffd), BF)] * 3,
            pltpu.VMEM((n, size, width), BF),
            pltpu.SemaphoreType.REGULAR,
            *[pltpu.SemaphoreType.DMA(slots)] * 10,
            *[pltpu.SemaphoreType.DMA((rows,))] * 2,
            *[pltpu.SemaphoreType.DMA((rows, n))] * 2,
            pltpu.SemaphoreType.DMA((rows, 3)),
            pltpu.SemaphoreType.DMA((n,)),
            pltpu.SemaphoreType.DMA((rows + 1,)),
            pltpu.SemaphoreType.DMA((2,)),
            pltpu.SemaphoreType.DMA((1,)),
            pltpu.SemaphoreType.DMA((4,)),
        ],
        rows * length * width * ffd * 16 + rows * length * length * hid * 40,
    )


def weight_kernel(places, stacked, extra, *refs):
    out, acc = refs[-2:]
    at = pl.program_id(0)

    @pl.when(at == 0)
    def _():
        acc[...] = jnp.zeros_like(acc)

    for i, j, start, count in places:
        where = pl.ds(start, count)
        part = dot(refs[i][...], refs[j][...], TN)
        if stacked:
            acc[where, :] += part
        else:
            acc[:, where] += part

    @pl.when(at == pl.num_programs(0) - 1)
    def _():
        out[: acc.shape[0], :] = acc[...].astype(BF)
        if extra:
            out[acc.shape[0] :, :] = jnp.zeros((extra, acc.shape[1]), BF)


def weight_sums(pairs, stacked, extra=0):
    arrays, places, start = [], [], 0

    def index(array):
        for i, known in enumerate(arrays):
            if known is array:
                return i
        arrays.append(array)
        return len(arrays) - 1

    for a, b in pairs:
        count = (a if stacked else b).shape[-1]
        places.append((index(a), index(b), start, count))
        start += count
    flat = [a.reshape(-1, a.shape[-1]) for a in arrays]
    other = pairs[0][1 if stacked else 0].shape[-1]
    shape = (start, other) if stacked else (other, start)
    tokens, step = flat[0].shape[0], 512
    whole = (shape[0] + extra, shape[1])
    return pl.pallas_call(
        functools.partial(weight_kernel, places, stacked, extra),
        grid=(tokens // step,),
        in_specs=[pl.BlockSpec((step, a.shape[1]), lambda i: (i, 0)) for a in flat],
        out_specs=pl.BlockSpec(whole, lambda i: (0, 0)),
        out_shape=jax.ShapeDtypeStruct(whole, BF),
        scratch_shapes=[pltpu.VMEM(shape, F32)],
        compiler_params=pltpu.CompilerParams(vmem_limit_bytes=VMEM_LIMIT),
        cost_estimate=pl.CostEstimate(
            flops=2 * tokens * start * other,
            bytes_accessed=sum(a.size for a in flat) * 2,
            transcendentals=0,
        ),
        name="weight_sums",
    )(*flat)


def body(
    block_input, cotangent, segments, attn_weight, attn_out, ffn_in, ffn_out, cross_weight, gains
):
    enc = lax.axis_index("section") == 0
    idx = lax.axis_index("mp")
    n = lax.axis_size("mp")
    dp_size = lax.axis_size("dp")
    bits = [1 << b for b in range(n.bit_length() - 1)]
    size, row_count, width = block_input.shape[1:]
    length = size * n
    hid = attn_weight.shape[3]
    ffd = ffn_in.shape[3]
    rows = range(row_count)

    w_qkv = attn_weight[0].reshape(width, 3 * hid)
    w_out = attn_out[0]
    w_gate, w_up = ffn_in[0, :, 0], ffn_in[0, :, 1]
    w_down = ffn_out[0]
    w_cross = cross_weight[0].reshape(width, 2 * hid)
    gain = gains[0]
    x = jnp.swapaxes(block_input[0], 0, 1)
    cot = jnp.swapaxes(cotangent[0], 0, 1)

    order = jnp.arange(n, dtype=jnp.int32) ^ idx
    block_of = jnp.repeat(order, size)[:, None]
    lane = jnp.arange(DK, dtype=jnp.int32)
    local = jnp.concatenate(
        [lax.dynamic_slice_in_dim(segments, (idx ^ j) * size, size, axis=2) for j in range(n)],
        axis=2,
    )[..., None]
    own = jnp.where(enc, local[0], local[1])

    def query_features(seg, causal):
        doc = (lane < DOC_LANES) & (lane != seg)
        later = (lane >= BLOCK_LANE) & (lane < BLOCK_LANE + n)
        later = later & (lane - BLOCK_LANE > block_of) & causal
        return jnp.where(doc | later, BIG, 0.0).astype(BF)

    def key_features(seg):
        doc = (lane < DOC_LANES) & (lane == seg)
        ones = (lane >= OFFSET_LANE) & (lane < OFFSET_LANE + 3)
        place = lane - BLOCK_LANE == block_of
        return jnp.where(doc | ones | place, 1.0, 0.0).astype(BF)

    above = jnp.arange(size)[None, :] > jnp.arange(size)[:, None]
    tri = jnp.where(above & ~enc, BIG, 0.0).astype(F32)
    key_own, key_enc = key_features(own), key_features(local[0])

    mid1, normed2, full1, qkv1, mix1, aug1 = self_stage(
        n,
        x,
        gain,
        w_qkv,
        w_out,
        query_features(own, ~enc),
        key_own,
        tri,
    )
    mid2, third, full_a, full_b, full_cot, full_t, w_kv, kv, q, mix, aug = middle_stage(
        n,
        normed2,
        cot,
        mid1,
        gain[2:3],
        w_gate,
        w_up,
        w_down,
        w_cross,
        query_features(local[1], False),
        key_enc,
    )

    grad1, gain_parts, parts, full_3, full_g, hidden, dgate, dup, dkv, dq = middle_back_stage(
        n,
        third,
        cot,
        gain[2:3],
        gain[1:2],
        w_gate,
        w_up,
        w_down,
        w_cross,
        w_kv,
        key_enc,
        mid1,
        mid2,
        full_a,
        full_cot,
        full_t,
        kv,
        q,
        mix,
        aug,
    )

    def over_rows(total, dim):
        return lax.psum_scatter(total, "dp", scatter_dimension=dim, tiled=True)

    sum_kv = lax.cond(
        enc,
        lambda: jnp.zeros((2 * hid, width), BF),
        lambda: weight_sums([(dkv, full_b)], True),
    )
    sum_kv = lax.ppermute(sum_kv, "section", [(1, 0)])
    early = lax.cond(
        enc,
        lambda: weight_sums(
            [(dgate, full_a), (dup, full_a), (hidden, full_g)], True, 2 * hid
        ),
        lambda: weight_sums(
            [(dgate, full_3), (dup, full_3), (hidden, full_cot), (dq, full_a), (mix, full_g)],
            True,
        ),
    )
    early = lax.dynamic_update_slice(
        early, jnp.where(enc, sum_kv, early[3 * ffd :]), (3 * ffd, 0)
    )
    got_early = over_rows(early, 1)

    def across(tensor, bit):
        decoder = [(n + i, n + (i ^ bit)) for i in range(n)]
        return lax.ppermute(tensor, ("section", "mp"), decoder)

    have = {j: parts[:, j * size : (j + 1) * size] for j in range(n)}
    first = None
    for bit in bits:
        for j in sorted((j for j in have if j & bit), reverse=True):
            came = across(have.pop(j), bit)
            total = have[j ^ bit].astype(F32) + came.astype(F32)
            have[j ^ bit] = total if len(have) == 1 else total.astype(BF)
        if bit == 1:
            first = have[max(have)]
    dec_out = mid2 + have[0].astype(F32)
    block_out = jnp.where(enc, third, dec_out.astype(BF))

    grad1, _, _ = lax.optimization_barrier((grad1, early, first))
    input_grad, gain_first, late = self_back_stage(
        n, x, gain, grad1, w_qkv, w_out, key_own, tri.T, qkv1, mix1, aug1, full1
    )

    late, got_early = lax.optimization_barrier((late, got_early))
    got_late = over_rows(late, 0).astype(F32)
    got_early = got_early.astype(F32)
    quarter = width // dp_size
    out_in = jnp.stack([got_early[:ffd].T, got_early[ffd : 2 * ffd].T], axis=1)
    out_down = got_early[2 * ffd : 3 * ffd]
    out_cross = got_early[3 * ffd :].T.reshape(quarter, 2, hid)
    out_qkv = got_late[:, : 3 * hid].reshape(quarter, 3, hid)
    out_out = got_late[:, 3 * hid :].T
    gain_parts = jnp.sum(gain_parts, axis=1)
    gain_total = jnp.stack([jnp.sum(gain_first, axis=0), gain_parts[1], gain_parts[0]])
    for axis, count in (("mp", n), ("dp", dp_size)):
        for bit in (1 << b for b in range(count.bit_length() - 1)):
            other = lax.ppermute(gain_total, axis, [(i, i ^ bit) for i in range(count)])
            gain_total = gain_total + other
    share = width // (n * dp_size)
    place = (lax.axis_index("dp") * n + idx) * share
    gain_total = lax.dynamic_slice_in_dim(gain_total, place, share, axis=1)
    return (
        jnp.swapaxes(block_out, 0, 1)[None],
        jnp.swapaxes(input_grad, 0, 1)[None],
        out_qkv[None],
        out_out[None],
        out_in[None],
        out_down[None],
        out_cross[None],
        gain_total[None],
    )


def solution(mesh):
    in_specs = (
        P("section", "mp", "dp", None),
        P("section", "mp", "dp", None),
        P(None, "dp", None),
        P("section", None, None, "mp"),
        P("section", "mp", None),
        P("section", None, None, "mp"),
        P("section", "mp", None),
        P("section", None, None, "mp"),
        P("section", None, None),
    )
    out_specs = (
        P("section", "mp", "dp", None),
        P("section", "mp", "dp", None),
        P("section", "dp", None, "mp"),
        P("section", "mp", "dp"),
        P("section", "dp", None, "mp"),
        P("section", "mp", "dp"),
        P("section", "dp", None, "mp"),
        P("section", None, ("dp", "mp")),
    )
    return jax.shard_map(body, mesh=mesh, in_specs=in_specs, out_specs=out_specs, check_vma=False)
```

```python
import functools
import math

import jax
import jax.numpy as jnp
from jax import lax
from jax.experimental import pallas as pl
from jax.experimental.pallas import tpu as pltpu
from jax.sharding import PartitionSpec as P

DK = 64
EPS = 1e-06
BIG = -1e30
SCALE = DK**-0.5
LOG_SCALE = SCALE * math.log2(math.e)
BF, F32 = jnp.bfloat16, jnp.float32

DOC_LANES = 3
OFFSET_LANE = 3
BLOCK_LANE = 8

MESH = pl.DeviceIdType.MESH

NT = (((1,), (1,)), ((), ()))
NN = (((1,), (0,)), ((), ()))
TN = (((0,), (0,)), ((), ()))


def dot(a, b, dims=NN):
    return lax.dot_general(a, b, dims, preferred_element_type=F32)


def norm_scale(tensor, gain):
    return tensor * lax.rsqrt(jnp.mean(tensor * tensor, axis=-1, keepdims=True) + EPS) * gain


def norm_back(tensor, gain, gradient):
    _, pull_back = jax.vjp(norm_scale, tensor, gain)
    return pull_back(gradient)


def split_three(column):
    high = column.astype(BF)
    rest = column - high.astype(F32)
    middle = rest.astype(BF)
    low = (rest - middle.astype(F32)).astype(BF)
    return high, middle, low


def with_offsets(base, column):
    lane = lax.broadcasted_iota(jnp.int32, base.shape, 1)
    out = base.astype(F32)
    for i, piece in enumerate(split_three(column)):
        out = jnp.where(lane == OFFSET_LANE + i, piece.astype(F32), out)
    return out.astype(BF)


def low_bit(j):
    return j & -j


def flipped(index, bit):
    return index + bit - 2 * bit * lax.rem(index // bit, 2)


def greet(n, section=False):
    barrier = pltpu.get_barrier_semaphore()
    idx = lax.axis_index("mp")
    bits = [j for j in range(1, n) if j == low_bit(j)]
    for bit in bits:
        pl.semaphore_signal(
            barrier, inc=1, device_id={"mp": flipped(idx, bit)}, device_id_type=MESH
        )
    if section:
        other = 1 - lax.axis_index("section")
        pl.semaphore_signal(barrier, inc=1, device_id={"section": other}, device_id_type=MESH)
    pl.semaphore_wait(barrier, len(bits) + (1 if section else 0))


class Gather:
    def __init__(self, n, own, got, send, recv):
        self.n, self.own, self.got, self.send, self.recv = n, own, got, send, recv
        self.idx = lax.axis_index("mp")
        self.slots = range(1, n)
        self.parents = sorted({j ^ low_bit(j) for j in self.slots} - {0}, key=int.bit_count)

    def block(self, r, j):
        return self.own.at[r] if j == 0 else self.got.at[r, j - 1]

    def copy(self, r, j):
        return pltpu.make_async_remote_copy(
            src_ref=self.block(r, j ^ low_bit(j)),
            dst_ref=self.got.at[r, j - 1],
            send_sem=self.send.at[r, j - 1],
            recv_sem=self.recv.at[r, j - 1],
            device_id={"mp": flipped(self.idx, low_bit(j))},
            device_id_type=MESH,
        )

    def start(self, r):
        for j in sorted(self.slots, reverse=True):
            if j == low_bit(j):
                self.copy(r, j).start()

    def forward(self, r):
        for parent in self.parents:
            self.copy(r, parent).wait_recv()
            for j in self.slots:
                if j ^ low_bit(j) == parent:
                    self.copy(r, j).start()

    def finish(self, r):
        for j in self.slots:
            if j not in self.parents:
                self.copy(r, j).wait_recv()

    def drain(self, r):
        for j in self.slots:
            self.copy(r, j).wait_send()


class Sums:
    def __init__(self, n, out, back, send, recv):
        self.n, self.out, self.back, self.send, self.recv = n, out, back, send, recv
        self.idx = lax.axis_index("mp")
        self.slots = range(1, n)

    def copy(self, r, j):
        return pltpu.make_async_remote_copy(
            src_ref=self.out.at[r, j - 1],
            dst_ref=self.back.at[r, j - 1],
            send_sem=self.send.at[r, j - 1],
            recv_sem=self.recv.at[r, j - 1],
            device_id={"mp": flipped(self.idx, low_bit(j))},
            device_id_type=MESH,
        )

    def terms(self, j):
        limit = low_bit(j) if j else self.n
        return [j | 1 << b for b in range(self.n.bit_length()) if 1 << b < limit]

    def put(self, r, j, part):
        self.out[r, j - 1] = part.astype(BF)
        if low_bit(j) == 1:
            self.copy(r, j).start()

    def forward(self, r):
        for j in sorted(self.slots, key=low_bit):
            if low_bit(j) == 1:
                continue
            total = self.out[r, j - 1].astype(F32)
            for k in self.terms(j):
                self.copy(r, k).wait_recv()
                total = total + self.back[r, k - 1].astype(F32)
            self.out[r, j - 1] = total.astype(BF)
            self.copy(r, j).start()

    def total(self, r, own):
        for k in self.terms(0):
            self.copy(r, k).wait_recv()
            own = own + self.back[r, k - 1].astype(F32)
        return own

    def drain(self, r):
        for j in self.slots:
            self.copy(r, j).wait_send()


def attend_into(size, heads, q, k, v, query_aug, key_aug, tri, mix, aug):
    keys_aug = key_aug[...]
    blocks = mix.shape[0] // size
    lanes_of = lambda at, head: slice(at + head * DK, at + (head + 1) * DK)
    for head in range(heads):
        lanes = lanes_of(0, head)
        keys = jnp.concatenate([k[0][:, lanes_of(k[1], head)], keys_aug], axis=1)
        values = jnp.concatenate([v[0][:, lanes_of(v[1], head)], keys_aug], axis=1)
        for c in range(blocks):
            rows = slice(c * size, (c + 1) * size)
            base = query_aug[rows, :]
            query = jnp.concatenate([q[0][rows, lanes_of(q[1], head)], base], axis=1)
            scores = []
            for j in range(blocks):
                s = dot(query, keys[j * size : (j + 1) * size], NT)
                scores.append(s + tri[...] if tri is not None and j == c else s)
            top = functools.reduce(jnp.maximum, scores)
            top = jnp.max(top, axis=1, keepdims=True)
            total = None
            for j, s in enumerate(scores):
                p = jnp.exp2((s - top) * LOG_SCALE).astype(BF)
                o = dot(p, values[j * size : (j + 1) * size])
                total = o if total is None else total + o
            weight = total[:, DK + OFFSET_LANE : DK + OFFSET_LANE + 1]
            mix[rows, lanes] = (total[:, :DK] / weight).astype(BF)
            log_raw = top + jnp.log2(weight) * (1.0 / LOG_SCALE)
            aug[rows, lanes] = with_offsets(base, -log_raw)


def attend_back_into(size, heads, q, k, v, grad, mix, aug, key_aug, tri, dq, dk, dv):
    keys_aug = key_aug[...]
    length = k[0].shape[0]
    at = lambda ref, head: slice(ref[1] + head * DK, ref[1] + (head + 1) * DK)
    for head in range(heads):
        key = k[0][:, at(k, head)]
        keys = jnp.concatenate([key, keys_aug], axis=1)
        values = jnp.concatenate([v[0][:, at(v, head)], keys_aug], axis=1)
        grad_k = jnp.zeros((length, DK), F32)
        grad_v = jnp.zeros((length, DK), F32)
        for c in range(length // size):
            rows = slice(c * size, (c + 1) * size)
            query = q[0][rows, at(q, head)]
            slope_in = grad[0][rows, at(grad, head)]
            delta = jnp.sum(
                slope_in.astype(F32) * mix[0][rows, at(mix, head)].astype(F32),
                axis=1,
                keepdims=True,
            )
            queries = jnp.concatenate([query, aug[0][rows, at(aug, head)]], axis=1)
            grads = jnp.concatenate(
                [slope_in, with_offsets(jnp.zeros((size, DK), BF), -delta)], axis=1
            )
            weights, slopes = [], []
            for j in range(length // size):
                block = slice(j * size, (j + 1) * size)
                s = dot(keys[block], queries, NT)
                if tri is not None and j == c:
                    s = s + tri[...]
                p = jnp.exp2(s * LOG_SCALE)
                slope = p * dot(values[block], grads, NT)
                weights.append(p.astype(BF))
                slopes.append(slope.astype(BF))
            weights = jnp.concatenate(weights, axis=0)
            slopes = jnp.concatenate(slopes, axis=0)
            grad_v = grad_v + dot(weights, slope_in)
            grad_k = grad_k + dot(slopes, query)
            dq[0][rows, at(dq, head)] = (dot(slopes, key, TN) * SCALE).astype(BF)
        dk[0][:, at(dk, head)] = (grad_k * SCALE).astype(BF)
        dv[0][:, at(dv, head)] = grad_v.astype(BF)


GELU_A, GELU_B = math.sqrt(2.0 / math.pi), 0.044715


def gelu_and_slope(x):
    square = x * x
    t = jnp.tanh(GELU_A * x * (1.0 + GELU_B * square))
    half = 0.5 * (1.0 + t)
    slope = half + 0.5 * x * (1.0 - t * t) * (GELU_A * (1.0 + 3.0 * GELU_B * square))
    return x * half, slope


def norm_parts(stream):
    return lax.rsqrt(jnp.mean(stream * stream, axis=-1, keepdims=True) + EPS)


def norm_back_parts(stream, gain, gradient):
    root = norm_parts(stream)
    unit = stream * root
    scaled = gradient * gain
    inner = jnp.mean(scaled * unit, axis=-1, keepdims=True)
    return root * (scaled - unit * inner), gradient * unit


def gain_terms(terms):
    return jnp.sum(terms.reshape(terms.shape[0] // 8, 8, terms.shape[1]), axis=0)


VMEM_LIMIT = 60 * 1024 * 1024


def call_stage(kernel, name, number, inputs, outputs, scratch, flops):
    vmem = pl.BlockSpec(memory_space=pltpu.VMEM)
    hbm = pl.BlockSpec(memory_space=pl.ANY)
    return pl.pallas_call(
        kernel,
        in_specs=[vmem if near else hbm for _, near in inputs],
        out_specs=[vmem if near else hbm for _, _, near in outputs],
        out_shape=[jax.ShapeDtypeStruct(shape, kind) for shape, kind, _ in outputs],
        scratch_shapes=scratch,
        compiler_params=pltpu.CompilerParams(
            collective_id=number, has_side_effects=True, vmem_limit_bytes=VMEM_LIMIT
        ),
        cost_estimate=pl.CostEstimate(
            flops=flops, bytes_accessed=1 << 25, transcendentals=1 << 24
        ),
        name=name,
    )(*(array for array, _ in inputs))


def self_stage_kernel(n, *refs):
    (x, gain, w_qkv, w_out, query_aug, key_aug, tri) = refs[:7]
    (total, normed, full_out, qkv_out, mix_out, aug_out) = refs[7:13]
    (own, got, out, back, qkv, mix, aug) = refs[13:20]
    sems = refs[20:]
    rows, size = x.shape[:2]
    hid = w_out.shape[0]
    gather = Gather(n, own, got, *sems[:2])
    sums = Sums(n, out, back, *sems[2:4])
    save = sems[4]
    greet(n)

    def saves(r, which):
        for i in which:
            if i < n:
                pair = (gather.block(r, i), full_out.at[r, pl.ds(i * size, size)])
            else:
                ref, dst = ((qkv, qkv_out), (mix, mix_out), (aug, aug_out))[i - n]
                pair = (ref.at[r], dst.at[r])
            yield pltpu.make_async_copy(*pair, save.at[r, i])

    def finish(r):
        stream = x[r].astype(F32) + sums.total(r, total[r])
        total[r] = stream
        normed[r] = (stream * norm_parts(stream) * gain[1:2]).astype(BF)

    for r in range(rows):
        stream = x[r].astype(F32)
        own[r] = (stream * norm_parts(stream) * gain[0:1]).astype(BF)
        gather.start(r)
    gather.forward(0)

    @pl.loop(0, rows)
    def _(r):
        gather.finish(r)
        for j in range(n):
            qkv[r, j * size : (j + 1) * size, :] = dot(
                gather.block(r, j)[...], w_qkv[...]
            ).astype(BF)
        for copy in saves(r, range(n + 1)):
            copy.start()

        @pl.when(r > 0)
        def _():
            sums.forward(r - 1)

        row = qkv.at[r]
        attend_into(
            size,
            hid // DK,
            (row, 0),
            (row, hid),
            (row, 2 * hid),
            query_aug.at[r],
            key_aug.at[r],
            tri,
            mix.at[r],
            aug.at[r],
        )
        for copy in saves(r, range(n + 1, n + 3)):
            copy.start()

        @pl.when(r + 1 < rows)
        def _():
            gather.forward(r + 1)

        for j in reversed(range(n)):
            part = dot(mix[r, j * size : (j + 1) * size, :], w_out[...])
            if j:
                sums.put(r, j, part)
            else:
                total[r] = part

        @pl.when(r > 0)
        def _():
            finish(r - 1)

    sums.forward(rows - 1)
    finish(rows - 1)

    @pl.loop(0, rows)
    def _(r):
        gather.drain(r)
        sums.drain(r)
        for copy in saves(r, range(n + 3)):
            copy.wait()


def self_stage(n, x, gain, w_qkv, w_out, query_aug, key_aug, tri):
    rows, size, width = x.shape
    length, hid = n * size, w_out.shape[0]
    slots = (rows, n - 1)
    return call_stage(
        functools.partial(self_stage_kernel, n),
        "self_stage",
        1,
        [(a, True) for a in (x, gain, w_qkv, w_out, query_aug, key_aug, tri)],
        [
            ((rows, size, width), F32, True),
            ((rows, size, width), BF, True),
            ((rows, length, width), BF, False),
            ((rows, length, 3 * hid), BF, False),
            ((rows, length, hid), BF, False),
            ((rows, length, hid), BF, False),
        ],
        [
            pltpu.VMEM((rows, size, width), BF),
            *[pltpu.VMEM((*slots, size, width), BF)] * 3,
            pltpu.VMEM((rows, length, 3 * hid), BF),
            pltpu.VMEM((rows, length, hid), BF),
            pltpu.VMEM((rows, length, hid), BF),
            *[pltpu.SemaphoreType.DMA(slots)] * 4,
            pltpu.SemaphoreType.DMA((rows, n + 3)),
        ],
        rows * length * width * hid * 8 + rows * length * length * hid * 16,
    )


def self_back_kernel(n, *refs):
    (x, gain, slope, w_qkv, w_out, key_aug, tri_t) = refs[:7]
    (qkv_in, mix_in, aug_in, full_in, ahead_in) = refs[7:12]
    (total, gain_out, weights) = refs[12:15]
    (own, got, out, back, qkv, mix, aug, grad, dqkv, full, acc) = refs[15:26]
    sems = refs[26:]
    rows, size = x.shape[:2]
    hid = w_out.shape[0]
    gather = Gather(n, own, got, *sems[:2])
    sums = Sums(n, out, back, *sems[2:4])
    load, load_full, load_ahead = sems[4:]
    ahead = 1 if rows > 1 else 0
    greet(n)

    def loads(r):
        for i, (src, dst) in enumerate(((qkv_in, qkv), (mix_in, mix), (aug_in, aug))):
            yield pltpu.make_async_copy(src.at[r], dst.at[r], load.at[r, i])

    def ahead_loads():
        for j in range(1, n):
            yield pltpu.make_async_copy(
                ahead_in.at[pl.ds(j * size, size)], got.at[0, j - 1], load_ahead.at[j]
            )

    def full_load(r):
        return pltpu.make_async_copy(full_in.at[r], full, load_full.at[0])

    def add_weights(r):
        full_load(r).wait()
        acc[:, : 3 * hid] += dot(full[...], dqkv[r], TN)
        acc[:, 3 * hid :] += functools.reduce(
            jnp.add,
            [
                dot(gather.block(r, j)[...], mix[r, j * size : (j + 1) * size, :], TN)
                for j in range(n)
            ],
        )

    def finish(r):
        part, terms = norm_back_parts(
            x[r].astype(F32), gain[0:1], sums.total(r, total[r])
        )
        gain_out[...] += gain_terms(terms)
        total[r] = slope[r] + part

    for r in range(rows):
        own[r] = slope[r].astype(BF)
        if r >= ahead:
            gather.start(r)
        else:
            for copy in ahead_loads():
                copy.start()
        for copy in loads(r):
            copy.start()
    full_load(0).start()
    gain_out[...] = jnp.zeros_like(gain_out)
    acc[...] = jnp.zeros_like(acc)
    if not ahead:
        gather.forward(0)

    @pl.loop(0, rows)
    def _(r):
        @pl.when(r < ahead)
        def _():
            for copy in ahead_loads():
                copy.wait()

        @pl.when(r >= ahead)
        def _():
            gather.finish(r)

        for j in range(n):
            grad[j * size : (j + 1) * size, :] = dot(
                gather.block(r, j)[...], w_out[...], NT
            ).astype(BF)
        for copy in loads(r):
            copy.wait()

        @pl.when(r > 0)
        def _():
            sums.forward(r - 1)

        row, result = qkv.at[r], dqkv.at[r]
        attend_back_into(
            size,
            hid // DK,
            (row, 0),
            (row, hid),
            (row, 2 * hid),
            (grad, 0),
            (mix.at[r], 0),
            (aug.at[r], 0),
            key_aug.at[r],
            tri_t,
            (result, 0),
            (result, hid),
            (result, 2 * hid),
        )

        @pl.when(r + 1 < rows)
        def _():
            gather.forward(r + 1)

        for j in reversed(range(n)):
            part = dot(dqkv[r, j * size : (j + 1) * size, :], w_qkv[...], NT)
            if j:
                sums.put(r, j, part)
            else:
                total[r] = part

        @pl.when(r > 0)
        def _():
            add_weights(r - 1)
            full_load(r).start()
            finish(r - 1)

    sums.forward(rows - 1)
    add_weights(rows - 1)
    weights[...] = acc[...].astype(BF)
    finish(rows - 1)

    @pl.loop(0, rows)
    def _(r):
        @pl.when(r >= ahead)
        def _():
            gather.drain(r)

        sums.drain(r)


def self_back_stage(
    n, x, gain, slope, w_qkv, w_out, key_aug, tri_t, qkv, mix, aug, full, first
):
    rows, size, width = x.shape
    length, hid = n * size, w_out.shape[0]
    slots = (rows, n - 1)
    return call_stage(
        functools.partial(self_back_kernel, n),
        "self_back_stage",
        2,
        [(a, True) for a in (x, gain, slope, w_qkv, w_out, key_aug, tri_t)]
        + [(a, False) for a in (qkv, mix, aug, full, first)],
        [
            ((rows, size, width), F32, True),
            ((8, width), F32, True),
            ((width, 4 * hid), BF, True),
        ],
        [
            pltpu.VMEM((rows, size, width), BF),
            *[pltpu.VMEM((*slots, size, width), BF)] * 3,
            pltpu.VMEM((rows, length, 3 * hid), BF),
            pltpu.VMEM((rows, length, hid), BF),
            pltpu.VMEM((rows, length, hid), BF),
            pltpu.VMEM((length, hid), BF),
            pltpu.VMEM((rows, length, 3 * hid), BF),
            pltpu.VMEM((length, width), BF),
            pltpu.VMEM((width, 4 * hid), F32),
            *[pltpu.SemaphoreType.DMA(slots)] * 4,
            pltpu.SemaphoreType.DMA((rows, 3)),
            pltpu.SemaphoreType.DMA((1,)),
            pltpu.SemaphoreType.DMA((n,)),
        ],
        rows * length * width * hid * 8 + rows * length * length * hid * 40,
    )


def middle_kernel(n, *refs):
    (x, cot, mid1, gain, w_gate, w_up, w_down, w_cross, query_aug, key_aug) = refs[:10]
    (mid2, third, full_a, full_b, full_cot, full_t, w_kv_out) = refs[10:17]
    (kv_out, q_out, mix_out, aug_out) = refs[17:21]
    (got_a, got_b, got_c, out, back, memory, w_kv, kv, q, mix, aug) = refs[21:32]
    sems = refs[32:]
    rows, size = x.shape[:2]
    hid = q.shape[2]
    enc = lax.axis_index("section") == 0
    gather_a = Gather(n, x, got_a, *sems[0:2])
    gather_b = Gather(n, memory, got_b, *sems[2:4])
    gather_c = Gather(n, cot, got_c, *sems[4:6])
    sums = Sums(n, out, back, *sems[6:8])
    gather_t = Gather(n, third, got_a, *sems[8:10])
    pair_send, pair_recv, save_a, save_b, save_c, save_t, save_x, weight_sems = sems[10:]
    greet(n, True)
    weight_copy = pltpu.make_async_remote_copy(
        src_ref=w_cross,
        dst_ref=w_kv,
        send_sem=weight_sems.at[0],
        recv_sem=weight_sems.at[1],
        device_id={"section": 1 - lax.axis_index("section")},
        device_id_type=MESH,
    )
    weight_save = pltpu.make_async_copy(w_kv, w_kv_out, weight_sems.at[2])

    def block_saves(gather, dst, sem, r):
        for j in range(n):
            yield pltpu.make_async_copy(
                gather.block(r, j), dst.at[r, pl.ds(j * size, size)], sem.at[r, j]
            )

    def cross_saves(r):
        for i, (src, dst) in enumerate(
            ((kv, kv_out), (q, q_out), (mix, mix_out), (aug, aug_out))
        ):
            yield pltpu.make_async_copy(src.at[r], dst.at[r], save_x.at[r, i])

    def pair_copy(r):
        return pltpu.make_async_remote_copy(
            src_ref=third.at[r],
            dst_ref=memory.at[r],
            send_sem=pair_send.at[r],
            recv_sem=pair_recv.at[r],
            device_id={"section": 1 - lax.axis_index("section")},
            device_id_type=MESH,
        )

    def finish(r):
        stream = mid1[r] + sums.total(r, mid2[r])
        mid2[r] = stream
        third[r] = (stream * norm_parts(stream) * gain[...]).astype(BF)

    for r in range(rows):
        gather_a.start(r)
    gather_a.forward(0)

    @pl.when(enc)
    def _():
        weight_copy.start()

        @pl.loop(0, rows)
        def _(r):
            gather_a.finish(r)
            for copy in block_saves(gather_a, full_a, save_a, r):
                copy.start()

            @pl.when(r > 0)
            def _():
                sums.forward(r - 1)

            for j in reversed(range(n)):
                block = gather_a.block(r, j)[...]
                gate = dot(block, w_gate[...])
                up = dot(block, w_up[...])
                hidden = (gelu_and_slope(gate)[0] * up).astype(BF)
                part = dot(hidden, w_down[...])
                if j:
                    sums.put(r, j, part)
                else:
                    mid2[r] = part

            @pl.when(r + 1 < rows)
            def _():
                gather_a.forward(r + 1)

            @pl.when(r > 0)
            def _():
                finish(r - 1)
                pair_copy(r - 1).start()

        sums.forward(rows - 1)
        finish(rows - 1)
        pair_copy(rows - 1).start()

        @pl.loop(0, rows)
        def _(r):
            pair_copy(r).wait_send()
            gather_a.drain(r)
            for copy in block_saves(gather_a, full_a, save_a, r):
                copy.wait()

        weight_copy.wait_send()

    @pl.when(jnp.logical_not(enc))
    def _():
        for r in range(rows):
            gather_c.start(r)

        @pl.loop(0, rows)
        def _(r):
            gather_a.finish(r)
            for copy in block_saves(gather_a, full_a, save_a, r):
                copy.start()
            for j in range(n):
                q[r, j * size : (j + 1) * size, :] = dot(
                    gather_a.block(r, j)[...], w_cross[:, :hid]
                ).astype(BF)

            @pl.when(r + 1 < rows)
            def _():
                gather_a.forward(r + 1)

        @pl.loop(0, rows)
        def _(r):
            gather_c.forward(r)
            gather_c.finish(r)
            for copy in block_saves(gather_c, full_cot, save_c, r):
                copy.start()

        def launch(r):
            pair_copy(r).wait_recv()
            gather_b.start(r)

        weight_copy.wait_recv()
        weight_save.start()
        for r in range(min(2, rows)):
            launch(r)
        gather_b.forward(0)

        @pl.loop(0, rows)
        def _(r):
            gather_b.finish(r)
            for copy in block_saves(gather_b, full_b, save_b, r):
                copy.start()
            for j in range(n):
                kv[r, j * size : (j + 1) * size, :] = dot(
                    gather_b.block(r, j)[...], w_kv[...]
                ).astype(BF)

            @pl.when(r > 0)
            def _():
                sums.forward(r - 1)

            @pl.when(r + 2 < rows)
            def _():
                launch(r + 2)

            row = kv.at[r]
            attend_into(
                size,
                hid // DK,
                (q.at[r], 0),
                (row, 0),
                (row, hid),
                query_aug.at[r],
                key_aug.at[r],
                None,
                mix.at[r],
                aug.at[r],
            )
            for copy in cross_saves(r):
                copy.start()

            @pl.when(r + 1 < rows)
            def _():
                gather_b.forward(r + 1)

            gather_a.drain(r)
            for copy in block_saves(gather_a, full_a, save_a, r):
                copy.wait()
            for j in reversed(range(n)):
                part = dot(mix[r, j * size : (j + 1) * size, :], w_cross[:, hid:], NT)
                if j:
                    sums.put(r, j, part)
                else:
                    mid2[r] = part

            @pl.when(r > 0)
            def _():
                finish(r - 1)

            @pl.when(r == 1)
            def _():
                gather_t.start(0)

            @pl.when(r == 2)
            def _():
                gather_t.forward(0)

        sums.forward(rows - 1)
        if rows > 1:
            if rows == 2:
                gather_t.forward(0)
            gather_t.finish(0)
            for copy in block_saves(gather_t, full_t, save_t, 0):
                copy.start()
        finish(rows - 1)
        if rows > 1:
            gather_t.drain(0)
            for copy in block_saves(gather_t, full_t, save_t, 0):
                copy.wait()

        weight_save.wait()

        @pl.loop(0, rows)
        def _(r):
            gather_b.drain(r)
            for copy in block_saves(gather_b, full_b, save_b, r):
                copy.wait()
            gather_c.drain(r)
            for copy in block_saves(gather_c, full_cot, save_c, r):
                copy.wait()
            for copy in cross_saves(r):
                copy.wait()

    @pl.loop(0, rows)
    def _(r):
        sums.drain(r)


def middle_stage(n, x, cot, mid1, gain, w_gate, w_up, w_down, w_cross, query_aug, key_aug):
    rows, size, width = x.shape
    length, hid, ffd = n * size, w_cross.shape[1] // 2, w_gate.shape[1]
    slots = (rows, n - 1)
    full = ((rows, length, width), BF, False)
    head = ((rows, length, hid), BF, False)
    near = (x, cot, mid1, gain, w_gate, w_up, w_down, w_cross, query_aug, key_aug)
    return call_stage(
        functools.partial(middle_kernel, n),
        "middle_stage",
        3,
        [(a, True) for a in near],
        [
            ((rows, size, width), F32, True),
            ((rows, size, width), BF, True),
            full,
            full,
            full,
            full,
            ((width, 2 * hid), BF, False),
            ((rows, length, 2 * hid), BF, False),
            head,
            head,
            head,
        ],
        [
            *[pltpu.VMEM((*slots, size, width), BF)] * 5,
            pltpu.VMEM((rows, size, width), BF),
            pltpu.VMEM((width, 2 * hid), BF),
            pltpu.VMEM((rows, length, 2 * hid), BF),
            *[pltpu.VMEM((rows, length, hid), BF)] * 3,
            *[pltpu.SemaphoreType.DMA(slots)] * 10,
            *[pltpu.SemaphoreType.DMA((rows,))] * 2,
            *[pltpu.SemaphoreType.DMA((rows, n))] * 4,
            pltpu.SemaphoreType.DMA((rows, 4)),
            pltpu.SemaphoreType.DMA((3,)),
        ],
        rows * length * width * ffd * 6 + rows * length * length * hid * 16,
    )


def middle_back_kernel(n, *refs):
    (third, cot, gain2, gain1, w_gate, w_up, w_down, w_cross, w_kv, key_aug) = refs[:10]
    (mid1_in, mid2_in, fwd_in, cot_in, third_in) = refs[10:15]
    (kv_in, q_in, mix_in, aug_in) = refs[15:19]
    (grad, gain_out, parts_out, full_3, full_g) = refs[19:24]
    (hidden_out, dgate_out, dup_out, dkv_out, dq_out, ahead_out) = refs[24:30]
    (own, got, out, back, rest, dmem) = refs[30:36]
    (mid, full, kv, q, mix, aug, dq, dkv, hidden_s, dgate_s, dup_s, part_s) = refs[36:48]
    ready = refs[48]
    sems = refs[49:]
    rows, size = third.shape[:2]
    hid = q.shape[1]
    enc = lax.axis_index("section") == 0
    gather_3 = Gather(n, third, got, *sems[0:2])
    gather_g = Gather(n, own, got, *sems[2:4])
    sums_a = Sums(n, out, back, *sems[4:6])
    sums_b = Sums(n, out, back, *sems[6:8])
    sums_m = Sums(n, out, back, *sems[8:10])
    gather_s = Gather(n, own, got, *sems[10:12])
    pair_send, pair_recv, save_3, save_g, save_f, save_p, save_d, load_m, load_f, load_x = sems[12:22]
    save_s = sems[22]
    ahead = 1 if rows > 1 else 0
    greet(n, True)
    gain_out[...] = jnp.zeros_like(gain_out)

    def block_saves(gather, dst, sem, r):
        for j in range(n):
            yield pltpu.make_async_copy(
                gather.block(r, j), dst.at[r, pl.ds(j * size, size)], sem.at[r, j]
            )

    def pair_copy(r):
        return pltpu.make_async_remote_copy(
            src_ref=dmem.at[r],
            dst_ref=dmem.at[r],
            send_sem=pair_send.at[r],
            recv_sem=pair_recv.at[r],
            device_id={"section": 1 - lax.axis_index("section")},
            device_id_type=MESH,
        )

    def mid_load(i, source, r):
        return pltpu.make_async_copy(source.at[r], mid.at[i], load_m.at[i])

    def full_load(source, r):
        return pltpu.make_async_copy(source.at[r], full, load_f.at[0])

    def cross_loads(r):
        for i, (src, dst) in enumerate(((kv_in, kv), (q_in, q), (mix_in, mix), (aug_in, aug))):
            yield pltpu.make_async_copy(src.at[r], dst, load_x.at[i])

    def ffn_saves(r):
        for i, (src, dst) in enumerate(
            ((hidden_s, hidden_out), (dgate_s, dgate_out), (dup_s, dup_out))
        ):
            yield pltpu.make_async_copy(src, dst.at[r], save_f.at[r, i])

    def part_save(r, j):
        return pltpu.make_async_copy(
            part_s.at[j], parts_out.at[r, pl.ds(j * size, size)], save_p.at[j]
        )

    def feed_forward(r, normed_of, grad_of, sums, with_out):
        @pl.when(r > 0)
        def _():
            for copy in ffn_saves(r - 1):
                copy.wait()

        for j in reversed(range(n)):
            at = slice(j * size, (j + 1) * size)
            normed, slope_in = normed_of(j), grad_of(j)
            gate = dot(normed, w_gate[...])
            up = dot(normed, w_up[...])
            active, slope = gelu_and_slope(gate)
            hidden = (active * up).astype(BF)
            hidden_s[at, :] = hidden
            back_hidden = dot(slope_in, w_down[...], NT)
            dgate = (back_hidden * up * slope).astype(BF)
            dup = (back_hidden * active).astype(BF)
            dgate_s[at, :] = dgate
            dup_s[at, :] = dup
            part = dot(dgate, w_gate[...], NT) + dot(dup, w_up[...], NT)
            if j:
                sums.put(r, j, part)
            else:
                rest[r] = part
            if with_out:
                part = dot(hidden, w_down[...]).astype(BF)

                @pl.when(r > 0)
                def _():
                    part_save(r - 1, j).wait()

                part_s[j] = part
                part_save(r, j).start()
        for copy in ffn_saves(r):
            copy.start()

    def finish_third(r, sums, add_cot):
        mid_load(0, mid2_in, r).wait()
        if add_cot:
            arriving = dmem[r].astype(F32) + cot[r].astype(F32)
        else:
            arriving = sums.total(r, rest[r])
        part, terms = norm_back_parts(mid[0], gain2[...], arriving)
        gain_out[0] += gain_terms(terms)
        if not add_cot:
            part = part + cot[r].astype(F32)
        grad[r] = part
        own[r] = part.astype(BF)

    def dkv_save(r):
        return pltpu.make_async_copy(dkv, dkv_out.at[r], save_d.at[0])

    def dq_save(r):
        return pltpu.make_async_copy(dq.at[r], dq_out.at[r], save_d.at[1 + r])

    def finish_memory(r):
        dmem[r] = sums_m.total(r, rest[r]).astype(BF)
        pair_copy(r).start()

    def finish_second(r, sums):
        mid_load(1, mid1_in, r).wait()
        part, terms = norm_back_parts(mid[1], gain1[...], sums.total(r, rest[r]))
        gain_out[1] += gain_terms(terms)
        grad[r] = grad[r] + part

    last = rows - 1

    def lead():
        own[0] = grad[0].astype(BF)
        gather_s.start(0)

    def lead_saves():
        for j in range(n):
            yield pltpu.make_async_copy(
                gather_s.block(0, j), ahead_out.at[pl.ds(j * size, size)], save_s.at[j]
            )

    def finish_lead():
        if ahead:
            gather_s.finish(0)
            for copy in lead_saves():
                copy.start()
            for copy in lead_saves():
                copy.wait()
            gather_s.drain(0)

    @pl.when(jnp.logical_not(enc))
    def _():
        def third_loads(r):
            for j in range(1, n):
                yield pltpu.make_async_copy(
                    third_in.at[r, pl.ds(j * size, size)], got.at[r, j - 1], save_3.at[r, j]
                )

        for r in range(ahead, rows):
            gather_3.start(r)
        full_load(cot_in, 0).start()
        if ahead:
            for copy in third_loads(0):
                copy.start()
        else:
            gather_3.forward(0)

        @pl.loop(0, rows)
        def _(r):
            @pl.when(r < ahead)
            def _():
                for copy in third_loads(r):
                    copy.wait()

            @pl.when(r >= ahead)
            def _():
                gather_3.finish(r)

            for copy in block_saves(gather_3, full_3, save_3, r):
                copy.start()
            full_load(cot_in, r).wait()

            @pl.when(r > ahead)
            def _():
                gather_3.drain(r - 1)

            @pl.when(r > 0)
            def _():
                sums_a.forward(r - 1)
                mid_load(0, mid2_in, r - 1).start()

            for copy in block_saves(gather_3, full_3, save_3, r):
                copy.wait()
            feed_forward(
                r,
                lambda j: gather_3.block(r, j)[...],
                lambda j: full[j * size : (j + 1) * size, :],
                sums_a,
                True,
            )

            @pl.when(r + 1 < rows)
            def _():
                full_load(cot_in, r + 1).start()
                gather_3.forward(r + 1)

            @pl.when(r > 0)
            def _():
                finish_third(r - 1, sums_a, False)
                gather_g.start(r - 1)

        gather_3.drain(last)
        sums_a.forward(last)
        mid_load(0, mid2_in, last).start()
        for copy in cross_loads(0):
            copy.start()
        gather_g.forward(0)
        finish_third(last, sums_a, False)
        gather_g.start(last)

        @pl.loop(0, rows)
        def _(r):
            gather_g.finish(r)
            for copy in block_saves(gather_g, full_g, save_g, r):
                copy.start()
            for j in range(n):
                at = slice(j * size, (j + 1) * size)
                full[at, :hid] = dot(gather_g.block(r, j)[...], w_cross[:, hid:]).astype(BF)
            for copy in cross_loads(r):
                copy.wait()

            @pl.when(r > 0)
            def _():
                dkv_save(r - 1).wait()
                sums_m.forward(r - 1)

            attend_back_into(
                size,
                hid // DK,
                (q, 0),
                (kv, 0),
                (kv, hid),
                (full, 0),
                (mix, 0),
                (aug, 0),
                key_aug.at[r],
                None,
                (dq.at[r], 0),
                (dkv, 0),
                (dkv, hid),
            )
            dkv_save(r).start()
            dq_save(r).start()

            @pl.when(r + 1 < rows)
            def _():
                for copy in cross_loads(r + 1):
                    copy.start()
                gather_g.forward(r + 1)

            sums_a.drain(r)
            for j in reversed(range(n)):
                part = dot(dkv[j * size : (j + 1) * size, :], w_kv[...], NT)
                if j:
                    sums_m.put(r, j, part)
                else:
                    rest[r] = part

            @pl.when(r > 0)
            def _():
                finish_memory(r - 1)

        sums_m.forward(last)
        finish_memory(last)

        idx = lax.axis_index("mp")
        bits = [j for j in range(1, n) if j == low_bit(j)]
        for bit in bits:
            pl.semaphore_signal(
                ready, inc=1, device_id={"mp": flipped(idx, bit)}, device_id_type=MESH
            )
        pl.semaphore_wait(ready, len(bits))

        @pl.loop(0, rows)
        def _(r):
            sums_m.drain(r)
            gather_g.drain(r)
            for copy in block_saves(gather_g, full_g, save_g, r):
                copy.wait()

            @pl.when(r > 0)
            def _():
                mid_load(1, mid1_in, r - 1).start()

            for j in reversed(range(n)):
                part = dot(dq[r, j * size : (j + 1) * size, :], w_cross[:, :hid], NT)
                if j:
                    sums_b.put(r, j, part)
                else:
                    rest[r] = part

            @pl.when(r > 0)
            def _():
                sums_b.forward(r - 1)
                finish_second(r - 1, sums_b)

            @pl.when(r == 1)
            def _():
                lead()

        sums_b.forward(last)
        mid_load(1, mid1_in, last).start()
        if ahead:
            gather_s.forward(0)
        finish_second(last, sums_b)
        finish_lead()

        @pl.loop(0, rows)
        def _(r):
            pair_copy(r).wait_send()
            dq_save(r).wait()

        for j in range(n):
            part_save(last, j).wait()
        dkv_save(last).wait()

    @pl.when(enc)
    def _():
        full_load(fwd_in, 0).start()

        @pl.loop(0, rows + 1)
        def _(t):
            @pl.when(t < rows)
            def _():
                mid_load(0, mid2_in, t).start()
                pair_copy(t).wait_recv()
                finish_third(t, None, True)
                gather_g.start(t)

            @pl.when(t > 1)
            def _():
                mid_load(1, mid1_in, t - 2).start()

            @pl.when(t > 0)
            def _():
                r = t - 1
                gather_g.forward(r)
                gather_g.finish(r)
                for copy in block_saves(gather_g, full_g, save_g, r):
                    copy.start()
                full_load(fwd_in, r).wait()
                for copy in block_saves(gather_g, full_g, save_g, r):
                    copy.wait()
                feed_forward(
                    r,
                    lambda j: full[j * size : (j + 1) * size, :],
                    lambda j: gather_g.block(r, j)[...],
                    sums_b,
                    False,
                )

                @pl.when(r + 1 < rows)
                def _():
                    full_load(fwd_in, r + 1).start()

                gather_g.drain(r)
                sums_b.forward(r)

            @pl.when(t > 1)
            def _():
                finish_second(t - 2, sums_b)

            @pl.when(t == 2)
            def _():
                lead()

        mid_load(1, mid1_in, last).start()
        if ahead:
            gather_s.forward(0)
        finish_second(last, sums_b)
        finish_lead()

    for copy in ffn_saves(last):
        copy.wait()

    @pl.loop(0, rows)
    def _(r):
        sums_b.drain(r)


def middle_back_stage(
    n,
    third,
    cot,
    gain2,
    gain1,
    w_gate,
    w_up,
    w_down,
    w_cross,
    w_kv,
    key_aug,
    mid1,
    mid2,
    fwd,
    full_cot,
    full_t,
    kv,
    q,
    mix,
    aug,
):
    rows, size, width = third.shape
    length, hid, ffd = n * size, w_cross.shape[1] // 2, w_gate.shape[1]
    slots = (rows, n - 1)
    full = ((rows, length, width), BF, False)
    unit = ((rows, length, ffd), BF, False)
    near = (third, cot, gain2, gain1, w_gate, w_up, w_down, w_cross, w_kv, key_aug)
    return call_stage(
        functools.partial(middle_back_kernel, n),
        "middle_back_stage",
        4,
        [(a, True) for a in near]
        + [(a, False) for a in (mid1, mid2, fwd, full_cot, full_t, kv, q, mix, aug)],
        [
            ((rows, size, width), F32, True),
            ((2, 8, width), F32, True),
            full,
            full,
            full,
            unit,
            unit,
            unit,
            ((rows, length, 2 * hid), BF, False),
            ((rows, length, hid), BF, False),
            ((length, width), BF, False),
        ],
        [
            pltpu.VMEM((rows, size, width), BF),
            *[pltpu.VMEM((*slots, size, width), BF)] * 3,
            pltpu.VMEM((rows, size, width), F32),
            pltpu.VMEM((rows, size, width), BF),
            pltpu.VMEM((2, size, width), F32),
            pltpu.VMEM((length, width), BF),
            pltpu.VMEM((length, 2 * hid), BF),
            *[pltpu.VMEM((length, hid), BF)] * 3,
            pltpu.VMEM((rows, length, hid), BF),
            pltpu.VMEM((length, 2 * hid), BF),
            *[pltpu.VMEM((length, ffd), BF)] * 3,
            pltpu.VMEM((n, size, width), BF),
            pltpu.SemaphoreType.REGULAR,
            *[pltpu.SemaphoreType.DMA(slots)] * 12,
            *[pltpu.SemaphoreType.DMA((rows,))] * 2,
            *[pltpu.SemaphoreType.DMA((rows, n))] * 2,
            pltpu.SemaphoreType.DMA((rows, 3)),
            pltpu.SemaphoreType.DMA((n,)),
            pltpu.SemaphoreType.DMA((rows + 1,)),
            pltpu.SemaphoreType.DMA((2,)),
            pltpu.SemaphoreType.DMA((1,)),
            pltpu.SemaphoreType.DMA((4,)),
            pltpu.SemaphoreType.DMA((n,)),
        ],
        rows * length * width * ffd * 16 + rows * length * length * hid * 40,
    )


def weight_kernel(places, stacked, extra, *refs):
    out, acc = refs[-2:]
    at = pl.program_id(0)

    @pl.when(at == 0)
    def _():
        acc[...] = jnp.zeros_like(acc)

    for i, j, start, count in places:
        where = pl.ds(start, count)
        part = dot(refs[i][...], refs[j][...], TN)
        if stacked:
            acc[where, :] += part
        else:
            acc[:, where] += part

    @pl.when(at == pl.num_programs(0) - 1)
    def _():
        out[: acc.shape[0], :] = acc[...].astype(BF)
        if extra:
            out[acc.shape[0] :, :] = jnp.zeros((extra, acc.shape[1]), BF)


def weight_sums(pairs, stacked, extra=0):
    arrays, places, start = [], [], 0

    def index(array):
        for i, known in enumerate(arrays):
            if known is array:
                return i
        arrays.append(array)
        return len(arrays) - 1

    for a, b in pairs:
        count = (a if stacked else b).shape[-1]
        places.append((index(a), index(b), start, count))
        start += count
    flat = [a.reshape(-1, a.shape[-1]) for a in arrays]
    other = pairs[0][1 if stacked else 0].shape[-1]
    shape = (start, other) if stacked else (other, start)
    tokens, step = flat[0].shape[0], 512
    whole = (shape[0] + extra, shape[1])
    return pl.pallas_call(
        functools.partial(weight_kernel, places, stacked, extra),
        grid=(tokens // step,),
        in_specs=[pl.BlockSpec((step, a.shape[1]), lambda i: (i, 0)) for a in flat],
        out_specs=pl.BlockSpec(whole, lambda i: (0, 0)),
        out_shape=jax.ShapeDtypeStruct(whole, BF),
        scratch_shapes=[pltpu.VMEM(shape, F32)],
        compiler_params=pltpu.CompilerParams(vmem_limit_bytes=VMEM_LIMIT),
        cost_estimate=pl.CostEstimate(
            flops=2 * tokens * start * other,
            bytes_accessed=sum(a.size for a in flat) * 2,
            transcendentals=0,
        ),
        name="weight_sums",
    )(*flat)


def body(
    block_input, cotangent, segments, attn_weight, attn_out, ffn_in, ffn_out, cross_weight, gains
):
    enc = lax.axis_index("section") == 0
    idx = lax.axis_index("mp")
    n = lax.axis_size("mp")
    dp_size = lax.axis_size("dp")
    bits = [1 << b for b in range(n.bit_length() - 1)]
    size, row_count, width = block_input.shape[1:]
    length = size * n
    hid = attn_weight.shape[3]
    ffd = ffn_in.shape[3]
    rows = range(row_count)

    w_qkv = attn_weight[0].reshape(width, 3 * hid)
    w_out = attn_out[0]
    w_gate, w_up = ffn_in[0, :, 0], ffn_in[0, :, 1]
    w_down = ffn_out[0]
    w_cross = cross_weight[0].reshape(width, 2 * hid)
    gain = gains[0]
    x = jnp.swapaxes(block_input[0], 0, 1)
    cot = jnp.swapaxes(cotangent[0], 0, 1)

    order = jnp.arange(n, dtype=jnp.int32) ^ idx
    block_of = jnp.repeat(order, size)[:, None]
    lane = jnp.arange(DK, dtype=jnp.int32)
    local = jnp.concatenate(
        [lax.dynamic_slice_in_dim(segments, (idx ^ j) * size, size, axis=2) for j in range(n)],
        axis=2,
    )[..., None]
    own = jnp.where(enc, local[0], local[1])

    def query_features(seg, causal):
        doc = (lane < DOC_LANES) & (lane != seg)
        later = (lane >= BLOCK_LANE) & (lane < BLOCK_LANE + n)
        later = later & (lane - BLOCK_LANE > block_of) & causal
        return jnp.where(doc | later, BIG, 0.0).astype(BF)

    def key_features(seg):
        doc = (lane < DOC_LANES) & (lane == seg)
        ones = (lane >= OFFSET_LANE) & (lane < OFFSET_LANE + 3)
        place = lane - BLOCK_LANE == block_of
        return jnp.where(doc | ones | place, 1.0, 0.0).astype(BF)

    above = jnp.arange(size)[None, :] > jnp.arange(size)[:, None]
    tri = jnp.where(above & ~enc, BIG, 0.0).astype(F32)
    key_own, key_enc = key_features(own), key_features(local[0])

    mid1, normed2, full1, qkv1, mix1, aug1 = self_stage(
        n,
        x,
        gain,
        w_qkv,
        w_out,
        query_features(own, ~enc),
        key_own,
        tri,
    )
    mid2, third, full_a, full_b, full_cot, full_t, w_kv, kv, q, mix, aug = middle_stage(
        n,
        normed2,
        cot,
        mid1,
        gain[2:3],
        w_gate,
        w_up,
        w_down,
        w_cross,
        query_features(local[1], False),
        key_enc,
    )

    back_results = middle_back_stage(
        n,
        third,
        cot,
        gain[2:3],
        gain[1:2],
        w_gate,
        w_up,
        w_down,
        w_cross,
        w_kv,
        key_enc,
        mid1,
        mid2,
        full_a,
        full_cot,
        full_t,
        kv,
        q,
        mix,
        aug,
    )

    grad1, gain_parts, parts, full_3, full_g, hidden, dgate, dup, dkv, dq, lead = back_results

    def over_rows(total, dim):
        return lax.psum_scatter(total, "dp", scatter_dimension=dim, tiled=True)

    sum_kv = lax.cond(
        enc,
        lambda: jnp.zeros((2 * hid, width), BF),
        lambda: weight_sums([(dkv, full_b)], True),
    )
    sum_kv = lax.ppermute(sum_kv, "section", [(1, 0)])
    early = lax.cond(
        enc,
        lambda: weight_sums(
            [(dgate, full_a), (dup, full_a), (hidden, full_g)], True, 2 * hid
        ),
        lambda: weight_sums(
            [(dgate, full_3), (dup, full_3), (hidden, full_cot), (dq, full_a), (mix, full_g)],
            True,
        ),
    )
    early = lax.dynamic_update_slice(
        early, jnp.where(enc, sum_kv, early[3 * ffd :]), (3 * ffd, 0)
    )
    got_early = over_rows(early, 1)

    def across(tensor, bit):
        decoder = [(n + i, n + (i ^ bit)) for i in range(n)]
        return lax.ppermute(tensor, ("section", "mp"), decoder)

    have = {j: parts[:, j * size : (j + 1) * size] for j in range(n)}
    first = None
    for bit in bits:
        for j in sorted((j for j in have if j & bit), reverse=True):
            came = across(have.pop(j), bit)
            total = have[j ^ bit].astype(F32) + came.astype(F32)
            have[j ^ bit] = total if len(have) == 1 else total.astype(BF)
        if bit == 1:
            first = have[max(have)]
    dec_out = mid2 + have[0].astype(F32)
    block_out = jnp.where(enc, third, dec_out.astype(BF))

    grad1, _, _ = lax.optimization_barrier((grad1, early, first))
    input_grad, gain_first, late = self_back_stage(
        n, x, gain, grad1, w_qkv, w_out, key_own, tri.T, qkv1, mix1, aug1, full1, lead
    )

    late, got_early = lax.optimization_barrier((late, got_early))
    got_late = over_rows(late, 0).astype(F32)
    got_early = got_early.astype(F32)
    quarter = width // dp_size
    out_in = jnp.stack([got_early[:ffd].T, got_early[ffd : 2 * ffd].T], axis=1)
    out_down = got_early[2 * ffd : 3 * ffd]
    out_cross = got_early[3 * ffd :].T.reshape(quarter, 2, hid)
    out_qkv = got_late[:, : 3 * hid].reshape(quarter, 3, hid)
    out_out = got_late[:, 3 * hid :].T
    gain_parts = jnp.sum(gain_parts, axis=1)
    gain_total = jnp.stack([jnp.sum(gain_first, axis=0), gain_parts[1], gain_parts[0]])
    for axis, count in (("mp", n), ("dp", dp_size)):
        for bit in (1 << b for b in range(count.bit_length() - 1)):
            other = lax.ppermute(gain_total, axis, [(i, i ^ bit) for i in range(count)])
            gain_total = gain_total + other
    share = width // (n * dp_size)
    place = (lax.axis_index("dp") * n + idx) * share
    gain_total = lax.dynamic_slice_in_dim(gain_total, place, share, axis=1)
    return (
        jnp.swapaxes(block_out, 0, 1)[None],
        jnp.swapaxes(input_grad, 0, 1)[None],
        out_qkv[None],
        out_out[None],
        out_in[None],
        out_down[None],
        out_cross[None],
        gain_total[None],
    )


def solution(mesh):
    in_specs = (
        P("section", "mp", "dp", None),
        P("section", "mp", "dp", None),
        P(None, "dp", None),
        P("section", None, None, "mp"),
        P("section", "mp", None),
        P("section", None, None, "mp"),
        P("section", "mp", None),
        P("section", None, None, "mp"),
        P("section", None, None),
    )
    out_specs = (
        P("section", "mp", "dp", None),
        P("section", "mp", "dp", None),
        P("section", "dp", None, "mp"),
        P("section", "mp", "dp"),
        P("section", "dp", None, "mp"),
        P("section", "mp", "dp"),
        P("section", "dp", None, "mp"),
        P("section", None, ("dp", "mp")),
    )
    return jax.shard_map(body, mesh=mesh, in_specs=in_specs, out_specs=out_specs, check_vma=False)
```

```python
import functools
import math

import jax
import jax.numpy as jnp
from jax import lax
from jax.experimental import pallas as pl
from jax.experimental.pallas import tpu as pltpu
from jax.sharding import PartitionSpec as P

DK = 64
EPS = 1e-06
BIG = -1e30
SCALE = DK**-0.5
LOG_SCALE = SCALE * math.log2(math.e)
BF, F32 = jnp.bfloat16, jnp.float32

DOC_LANES = 3
OFFSET_LANE = 3
BLOCK_LANE = 8

MESH = pl.DeviceIdType.MESH

NT = (((1,), (1,)), ((), ()))
NN = (((1,), (0,)), ((), ()))
TN = (((0,), (0,)), ((), ()))


def dot(a, b, dims=NN):
    return lax.dot_general(a, b, dims, preferred_element_type=F32)


def norm_scale(tensor, gain):
    return tensor * lax.rsqrt(jnp.mean(tensor * tensor, axis=-1, keepdims=True) + EPS) * gain


def norm_back(tensor, gain, gradient):
    _, pull_back = jax.vjp(norm_scale, tensor, gain)
    return pull_back(gradient)


def split_three(column):
    high = column.astype(BF)
    rest = column - high.astype(F32)
    middle = rest.astype(BF)
    low = (rest - middle.astype(F32)).astype(BF)
    return high, middle, low


def with_offsets(base, column):
    lane = lax.broadcasted_iota(jnp.int32, base.shape, 1)
    out = base.astype(F32)
    for i, piece in enumerate(split_three(column)):
        out = jnp.where(lane == OFFSET_LANE + i, piece.astype(F32), out)
    return out.astype(BF)


def low_bit(j):
    return j & -j


def flipped(index, bit):
    return index + bit - 2 * bit * lax.rem(index // bit, 2)


def greet(n, section=False):
    barrier = pltpu.get_barrier_semaphore()
    idx = lax.axis_index("mp")
    bits = [j for j in range(1, n) if j == low_bit(j)]
    for bit in bits:
        pl.semaphore_signal(
            barrier, inc=1, device_id={"mp": flipped(idx, bit)}, device_id_type=MESH
        )
    if section:
        other = 1 - lax.axis_index("section")
        pl.semaphore_signal(barrier, inc=1, device_id={"section": other}, device_id_type=MESH)
    pl.semaphore_wait(barrier, len(bits) + (1 if section else 0))


class Gather:
    def __init__(self, n, own, got, send, recv):
        self.n, self.own, self.got, self.send, self.recv = n, own, got, send, recv
        self.idx = lax.axis_index("mp")
        self.slots = range(1, n)
        self.parents = sorted({j ^ low_bit(j) for j in self.slots} - {0}, key=int.bit_count)

    def block(self, r, j):
        return self.own.at[r] if j == 0 else self.got.at[r, j - 1]

    def copy(self, r, j):
        return pltpu.make_async_remote_copy(
            src_ref=self.block(r, j ^ low_bit(j)),
            dst_ref=self.got.at[r, j - 1],
            send_sem=self.send.at[r, j - 1],
            recv_sem=self.recv.at[r, j - 1],
            device_id={"mp": flipped(self.idx, low_bit(j))},
            device_id_type=MESH,
        )

    def start(self, r):
        for j in sorted(self.slots, reverse=True):
            if j == low_bit(j):
                self.copy(r, j).start()

    def forward(self, r):
        for parent in self.parents:
            self.copy(r, parent).wait_recv()
            for j in self.slots:
                if j ^ low_bit(j) == parent:
                    self.copy(r, j).start()

    def finish(self, r):
        for j in self.slots:
            if j not in self.parents:
                self.copy(r, j).wait_recv()

    def drain(self, r):
        for j in self.slots:
            self.copy(r, j).wait_send()


class Sums:
    def __init__(self, n, out, back, send, recv):
        self.n, self.out, self.back, self.send, self.recv = n, out, back, send, recv
        self.idx = lax.axis_index("mp")
        self.slots = range(1, n)

    def copy(self, r, j):
        return pltpu.make_async_remote_copy(
            src_ref=self.out.at[r, j - 1],
            dst_ref=self.back.at[r, j - 1],
            send_sem=self.send.at[r, j - 1],
            recv_sem=self.recv.at[r, j - 1],
            device_id={"mp": flipped(self.idx, low_bit(j))},
            device_id_type=MESH,
        )

    def terms(self, j):
        limit = low_bit(j) if j else self.n
        return [j | 1 << b for b in range(self.n.bit_length()) if 1 << b < limit]

    def put(self, r, j, part):
        self.out[r, j - 1] = part.astype(BF)
        if low_bit(j) == 1:
            self.copy(r, j).start()

    def forward(self, r):
        for j in sorted(self.slots, key=low_bit):
            if low_bit(j) == 1:
                continue
            total = self.out[r, j - 1].astype(F32)
            for k in self.terms(j):
                self.copy(r, k).wait_recv()
                total = total + self.back[r, k - 1].astype(F32)
            self.out[r, j - 1] = total.astype(BF)
            self.copy(r, j).start()

    def total(self, r, own):
        for k in self.terms(0):
            self.copy(r, k).wait_recv()
            own = own + self.back[r, k - 1].astype(F32)
        return own

    def drain(self, r):
        for j in self.slots:
            self.copy(r, j).wait_send()


def attend_into(size, heads, q, k, v, query_aug, key_aug, tri, mix, aug):
    keys_aug = key_aug[...]
    blocks = mix.shape[0] // size
    lanes_of = lambda at, head: slice(at + head * DK, at + (head + 1) * DK)
    for head in range(heads):
        lanes = lanes_of(0, head)
        keys = jnp.concatenate([k[0][:, lanes_of(k[1], head)], keys_aug], axis=1)
        values = jnp.concatenate([v[0][:, lanes_of(v[1], head)], keys_aug], axis=1)
        for c in range(blocks):
            rows = slice(c * size, (c + 1) * size)
            base = query_aug[rows, :]
            query = jnp.concatenate([q[0][rows, lanes_of(q[1], head)], base], axis=1)
            scores = []
            for j in range(blocks):
                s = dot(query, keys[j * size : (j + 1) * size], NT)
                scores.append(s + tri[...] if tri is not None and j == c else s)
            top = functools.reduce(jnp.maximum, scores)
            top = jnp.max(top, axis=1, keepdims=True)
            total = None
            for j, s in enumerate(scores):
                p = jnp.exp2((s - top) * LOG_SCALE).astype(BF)
                o = dot(p, values[j * size : (j + 1) * size])
                total = o if total is None else total + o
            weight = total[:, DK + OFFSET_LANE : DK + OFFSET_LANE + 1]
            mix[rows, lanes] = (total[:, :DK] / weight).astype(BF)
            log_raw = top + jnp.log2(weight) * (1.0 / LOG_SCALE)
            aug[rows, lanes] = with_offsets(base, -log_raw)


def attend_back_into(size, heads, q, k, v, grad, mix, aug, key_aug, tri, dq, dk, dv):
    keys_aug = key_aug[...]
    length = k[0].shape[0]
    at = lambda ref, head: slice(ref[1] + head * DK, ref[1] + (head + 1) * DK)
    for head in range(heads):
        key = k[0][:, at(k, head)]
        keys = jnp.concatenate([key, keys_aug], axis=1)
        values = jnp.concatenate([v[0][:, at(v, head)], keys_aug], axis=1)
        grad_k = jnp.zeros((length, DK), F32)
        grad_v = jnp.zeros((length, DK), F32)
        for c in range(length // size):
            rows = slice(c * size, (c + 1) * size)
            query = q[0][rows, at(q, head)]
            slope_in = grad[0][rows, at(grad, head)]
            delta = jnp.sum(
                slope_in.astype(F32) * mix[0][rows, at(mix, head)].astype(F32),
                axis=1,
                keepdims=True,
            )
            queries = jnp.concatenate([query, aug[0][rows, at(aug, head)]], axis=1)
            grads = jnp.concatenate(
                [slope_in, with_offsets(jnp.zeros((size, DK), BF), -delta)], axis=1
            )
            weights, slopes = [], []
            for j in range(length // size):
                block = slice(j * size, (j + 1) * size)
                s = dot(keys[block], queries, NT)
                if tri is not None and j == c:
                    s = s + tri[...]
                p = jnp.exp2(s * LOG_SCALE)
                slope = p * dot(values[block], grads, NT)
                weights.append(p.astype(BF))
                slopes.append(slope.astype(BF))
            weights = jnp.concatenate(weights, axis=0)
            slopes = jnp.concatenate(slopes, axis=0)
            grad_v = grad_v + dot(weights, slope_in)
            grad_k = grad_k + dot(slopes, query)
            dq[0][rows, at(dq, head)] = (dot(slopes, key, TN) * SCALE).astype(BF)
        dk[0][:, at(dk, head)] = (grad_k * SCALE).astype(BF)
        dv[0][:, at(dv, head)] = grad_v.astype(BF)


GELU_A, GELU_B = math.sqrt(2.0 / math.pi), 0.044715


def gelu_and_slope(x):
    square = x * x
    t = jnp.tanh(GELU_A * x * (1.0 + GELU_B * square))
    half = 0.5 * (1.0 + t)
    slope = half + 0.5 * x * (1.0 - t * t) * (GELU_A * (1.0 + 3.0 * GELU_B * square))
    return x * half, slope


def norm_parts(stream):
    return lax.rsqrt(jnp.mean(stream * stream, axis=-1, keepdims=True) + EPS)


def norm_back_parts(stream, gain, gradient):
    root = norm_parts(stream)
    unit = stream * root
    scaled = gradient * gain
    inner = jnp.mean(scaled * unit, axis=-1, keepdims=True)
    return root * (scaled - unit * inner), gradient * unit


def gain_terms(terms):
    return jnp.sum(terms.reshape(terms.shape[0] // 8, 8, terms.shape[1]), axis=0)


VMEM_LIMIT = 60 * 1024 * 1024


def call_stage(kernel, name, number, inputs, outputs, scratch, flops):
    vmem = pl.BlockSpec(memory_space=pltpu.VMEM)
    hbm = pl.BlockSpec(memory_space=pl.ANY)
    return pl.pallas_call(
        kernel,
        in_specs=[vmem if near else hbm for _, near in inputs],
        out_specs=[vmem if near else hbm for _, _, near in outputs],
        out_shape=[jax.ShapeDtypeStruct(shape, kind) for shape, kind, _ in outputs],
        scratch_shapes=scratch,
        compiler_params=pltpu.CompilerParams(
            collective_id=number, has_side_effects=True, vmem_limit_bytes=VMEM_LIMIT
        ),
        cost_estimate=pl.CostEstimate(
            flops=flops, bytes_accessed=1 << 25, transcendentals=1 << 24
        ),
        name=name,
    )(*(array for array, _ in inputs))


def self_stage_kernel(n, *refs):
    (x, gain, w_qkv, w_out, query_aug, key_aug, tri) = refs[:7]
    (total, normed, full_out, qkv_out, mix_out, aug_out) = refs[7:13]
    (own, got, out, back, qkv, mix, aug) = refs[13:20]
    sems = refs[20:]
    rows, size = x.shape[:2]
    hid = w_out.shape[0]
    gather = Gather(n, own, got, *sems[:2])
    sums = Sums(n, out, back, *sems[2:4])
    save = sems[4]
    greet(n)

    def saves(r, which):
        for i in which:
            if i < n:
                pair = (gather.block(r, i), full_out.at[r, pl.ds(i * size, size)])
            else:
                ref, dst = ((qkv, qkv_out), (mix, mix_out), (aug, aug_out))[i - n]
                pair = (ref.at[r], dst.at[r])
            yield pltpu.make_async_copy(*pair, save.at[r, i])

    def finish(r):
        stream = x[r].astype(F32) + sums.total(r, total[r])
        total[r] = stream
        normed[r] = (stream * norm_parts(stream) * gain[1:2]).astype(BF)

    for r in range(rows):
        stream = x[r].astype(F32)
        own[r] = (stream * norm_parts(stream) * gain[0:1]).astype(BF)
        gather.start(r)
    gather.forward(0)

    @pl.loop(0, rows)
    def _(r):
        gather.finish(r)
        for j in range(n):
            qkv[r, j * size : (j + 1) * size, :] = dot(
                gather.block(r, j)[...], w_qkv[...]
            ).astype(BF)
        for copy in saves(r, range(n + 1)):
            copy.start()

        @pl.when(r > 0)
        def _():
            sums.forward(r - 1)

        row = qkv.at[r]
        attend_into(
            size,
            hid // DK,
            (row, 0),
            (row, hid),
            (row, 2 * hid),
            query_aug.at[r],
            key_aug.at[r],
            tri,
            mix.at[r],
            aug.at[r],
        )
        for copy in saves(r, range(n + 1, n + 3)):
            copy.start()

        @pl.when(r + 1 < rows)
        def _():
            gather.forward(r + 1)

        for j in reversed(range(n)):
            part = dot(mix[r, j * size : (j + 1) * size, :], w_out[...])
            if j:
                sums.put(r, j, part)
            else:
                total[r] = part

        @pl.when(r > 0)
        def _():
            finish(r - 1)

    sums.forward(rows - 1)
    finish(rows - 1)

    @pl.loop(0, rows)
    def _(r):
        gather.drain(r)
        sums.drain(r)
        for copy in saves(r, range(n + 3)):
            copy.wait()


def self_stage(n, x, gain, w_qkv, w_out, query_aug, key_aug, tri):
    rows, size, width = x.shape
    length, hid = n * size, w_out.shape[0]
    slots = (rows, n - 1)
    return call_stage(
        functools.partial(self_stage_kernel, n),
        "self_stage",
        1,
        [(a, True) for a in (x, gain, w_qkv, w_out, query_aug, key_aug, tri)],
        [
            ((rows, size, width), F32, True),
            ((rows, size, width), BF, True),
            ((rows, length, width), BF, False),
            ((rows, length, 3 * hid), BF, False),
            ((rows, length, hid), BF, False),
            ((rows, length, hid), BF, False),
        ],
        [
            pltpu.VMEM((rows, size, width), BF),
            *[pltpu.VMEM((*slots, size, width), BF)] * 3,
            pltpu.VMEM((rows, length, 3 * hid), BF),
            pltpu.VMEM((rows, length, hid), BF),
            pltpu.VMEM((rows, length, hid), BF),
            *[pltpu.SemaphoreType.DMA(slots)] * 4,
            pltpu.SemaphoreType.DMA((rows, n + 3)),
        ],
        rows * length * width * hid * 8 + rows * length * length * hid * 16,
    )


def self_back_kernel(n, *refs):
    (x, gain, slope, w_qkv, w_out, key_aug, tri_t) = refs[:7]
    (qkv_in, mix_in, aug_in, full_in, ahead_in, cross_in) = refs[7:13]
    (total, gain_out, weights) = refs[13:16]
    (own, got, out, back, qkv, mix, aug, grad, dqkv, full, acc) = refs[16:27]
    sems = refs[27:]
    rows, size = x.shape[:2]
    hid = w_out.shape[0]
    gather = Gather(n, own, got, *sems[:2])
    sums = Sums(n, out, back, *sems[2:4])
    load, load_full, load_ahead, load_cross = sems[4:]
    ahead = 1 if rows > 1 else 0
    greet(n)

    def loads(r):
        for i, (src, dst) in enumerate(((qkv_in, qkv), (mix_in, mix), (aug_in, aug))):
            yield pltpu.make_async_copy(src.at[r], dst.at[r], load.at[r, i])

    def ahead_loads():
        for j in range(1, n):
            yield pltpu.make_async_copy(
                ahead_in.at[pl.ds(j * size, size)], got.at[0, j - 1], load_ahead.at[j]
            )

    def full_load(r):
        return pltpu.make_async_copy(full_in.at[r], full, load_full.at[0])

    def add_weights(r):
        full_load(r).wait()
        acc[:, : 3 * hid] += dot(full[...], dqkv[r], TN)
        acc[:, 3 * hid :] += functools.reduce(
            jnp.add,
            [
                dot(gather.block(r, j)[...], mix[r, j * size : (j + 1) * size, :], TN)
                for j in range(n)
            ],
        )

    def finish(r):
        part, terms = norm_back_parts(
            x[r].astype(F32), gain[0:1], sums.total(r, total[r])
        )
        gain_out[...] += gain_terms(terms)
        total[r] = slope[r] + part

    for r in range(rows):
        own[r] = slope[r].astype(BF)
        if r >= ahead:
            gather.start(r)
        else:
            for copy in ahead_loads():
                copy.start()
        for copy in loads(r):
            copy.start()
    cross_load = pltpu.make_async_copy(
        cross_in, weights.at[:, pl.ds(4 * hid, 2 * hid)], load_cross.at[0]
    )
    cross_load.start()
    full_load(0).start()
    gain_out[...] = jnp.zeros_like(gain_out)
    acc[...] = jnp.zeros_like(acc)
    if not ahead:
        gather.forward(0)

    @pl.loop(0, rows)
    def _(r):
        @pl.when(r < ahead)
        def _():
            for copy in ahead_loads():
                copy.wait()

        @pl.when(r >= ahead)
        def _():
            gather.finish(r)

        for j in range(n):
            grad[j * size : (j + 1) * size, :] = dot(
                gather.block(r, j)[...], w_out[...], NT
            ).astype(BF)
        for copy in loads(r):
            copy.wait()

        @pl.when(r > 0)
        def _():
            sums.forward(r - 1)

        row, result = qkv.at[r], dqkv.at[r]
        attend_back_into(
            size,
            hid // DK,
            (row, 0),
            (row, hid),
            (row, 2 * hid),
            (grad, 0),
            (mix.at[r], 0),
            (aug.at[r], 0),
            key_aug.at[r],
            tri_t,
            (result, 0),
            (result, hid),
            (result, 2 * hid),
        )

        @pl.when(r + 1 < rows)
        def _():
            gather.forward(r + 1)

        for j in reversed(range(n)):
            part = dot(dqkv[r, j * size : (j + 1) * size, :], w_qkv[...], NT)
            if j:
                sums.put(r, j, part)
            else:
                total[r] = part

        @pl.when(r > 0)
        def _():
            add_weights(r - 1)
            full_load(r).start()
            finish(r - 1)

    sums.forward(rows - 1)
    add_weights(rows - 1)
    weights[:, : 4 * hid] = acc[...].astype(BF)
    cross_load.wait()
    finish(rows - 1)

    @pl.loop(0, rows)
    def _(r):
        @pl.when(r >= ahead)
        def _():
            gather.drain(r)

        sums.drain(r)


def self_back_stage(
    n, x, gain, slope, w_qkv, w_out, key_aug, tri_t, qkv, mix, aug, full, first, cross
):
    rows, size, width = x.shape
    length, hid = n * size, w_out.shape[0]
    slots = (rows, n - 1)
    return call_stage(
        functools.partial(self_back_kernel, n),
        "self_back_stage",
        2,
        [(a, True) for a in (x, gain, slope, w_qkv, w_out, key_aug, tri_t)]
        + [(a, False) for a in (qkv, mix, aug, full, first, cross)],
        [
            ((rows, size, width), F32, True),
            ((8, width), F32, True),
            ((width, 6 * hid), BF, True),
        ],
        [
            pltpu.VMEM((rows, size, width), BF),
            *[pltpu.VMEM((*slots, size, width), BF)] * 3,
            pltpu.VMEM((rows, length, 3 * hid), BF),
            pltpu.VMEM((rows, length, hid), BF),
            pltpu.VMEM((rows, length, hid), BF),
            pltpu.VMEM((length, hid), BF),
            pltpu.VMEM((rows, length, 3 * hid), BF),
            pltpu.VMEM((length, width), BF),
            pltpu.VMEM((width, 4 * hid), F32),
            *[pltpu.SemaphoreType.DMA(slots)] * 4,
            pltpu.SemaphoreType.DMA((rows, 3)),
            pltpu.SemaphoreType.DMA((1,)),
            pltpu.SemaphoreType.DMA((n,)),
            pltpu.SemaphoreType.DMA((1,)),
        ],
        rows * length * width * hid * 8 + rows * length * length * hid * 40,
    )


def middle_kernel(n, *refs):
    (x, cot, mid1, gain, w_gate, w_up, w_down, w_cross, query_aug, key_aug) = refs[:10]
    (mid2, third, full_a, full_b, full_cot, full_t, w_kv_out) = refs[10:17]
    (kv_out, q_out, mix_out, aug_out) = refs[17:21]
    (got_a, got_b, got_c, out, back, memory, w_kv, kv, q, mix, aug) = refs[21:32]
    sems = refs[32:]
    rows, size = x.shape[:2]
    hid = q.shape[2]
    enc = lax.axis_index("section") == 0
    gather_a = Gather(n, x, got_a, *sems[0:2])
    gather_b = Gather(n, memory, got_b, *sems[2:4])
    gather_c = Gather(n, cot, got_c, *sems[4:6])
    sums = Sums(n, out, back, *sems[6:8])
    gather_t = Gather(n, third, got_a, *sems[8:10])
    pair_send, pair_recv, save_a, save_b, save_c, save_t, save_x, weight_sems = sems[10:]
    greet(n, True)
    weight_copy = pltpu.make_async_remote_copy(
        src_ref=w_cross,
        dst_ref=w_kv,
        send_sem=weight_sems.at[0],
        recv_sem=weight_sems.at[1],
        device_id={"section": 1 - lax.axis_index("section")},
        device_id_type=MESH,
    )
    weight_save = pltpu.make_async_copy(w_kv, w_kv_out, weight_sems.at[2])

    def block_saves(gather, dst, sem, r):
        for j in range(n):
            yield pltpu.make_async_copy(
                gather.block(r, j), dst.at[r, pl.ds(j * size, size)], sem.at[r, j]
            )

    def cross_saves(r):
        for i, (src, dst) in enumerate(
            ((kv, kv_out), (q, q_out), (mix, mix_out), (aug, aug_out))
        ):
            yield pltpu.make_async_copy(src.at[r], dst.at[r], save_x.at[r, i])

    def pair_copy(r):
        return pltpu.make_async_remote_copy(
            src_ref=third.at[r],
            dst_ref=memory.at[r],
            send_sem=pair_send.at[r],
            recv_sem=pair_recv.at[r],
            device_id={"section": 1 - lax.axis_index("section")},
            device_id_type=MESH,
        )

    def finish(r):
        stream = mid1[r] + sums.total(r, mid2[r])
        mid2[r] = stream
        third[r] = (stream * norm_parts(stream) * gain[...]).astype(BF)

    for r in range(rows):
        gather_a.start(r)
    gather_a.forward(0)

    @pl.when(enc)
    def _():
        weight_copy.start()

        @pl.loop(0, rows)
        def _(r):
            gather_a.finish(r)
            for copy in block_saves(gather_a, full_a, save_a, r):
                copy.start()

            @pl.when(r > 0)
            def _():
                sums.forward(r - 1)

            for j in reversed(range(n)):
                block = gather_a.block(r, j)[...]
                gate = dot(block, w_gate[...])
                up = dot(block, w_up[...])
                hidden = (gelu_and_slope(gate)[0] * up).astype(BF)
                part = dot(hidden, w_down[...])
                if j:
                    sums.put(r, j, part)
                else:
                    mid2[r] = part

            @pl.when(r + 1 < rows)
            def _():
                gather_a.forward(r + 1)

            @pl.when(r > 0)
            def _():
                finish(r - 1)
                pair_copy(r - 1).start()

        sums.forward(rows - 1)
        finish(rows - 1)
        pair_copy(rows - 1).start()

        @pl.loop(0, rows)
        def _(r):
            pair_copy(r).wait_send()
            gather_a.drain(r)
            for copy in block_saves(gather_a, full_a, save_a, r):
                copy.wait()

        weight_copy.wait_send()

    @pl.when(jnp.logical_not(enc))
    def _():
        for r in range(rows):
            gather_c.start(r)

        @pl.loop(0, rows)
        def _(r):
            gather_a.finish(r)
            for copy in block_saves(gather_a, full_a, save_a, r):
                copy.start()
            for j in range(n):
                q[r, j * size : (j + 1) * size, :] = dot(
                    gather_a.block(r, j)[...], w_cross[:, :hid]
                ).astype(BF)

            @pl.when(r + 1 < rows)
            def _():
                gather_a.forward(r + 1)

        @pl.loop(0, rows)
        def _(r):
            gather_c.forward(r)
            gather_c.finish(r)
            for copy in block_saves(gather_c, full_cot, save_c, r):
                copy.start()

        def launch(r):
            pair_copy(r).wait_recv()
            gather_b.start(r)

        weight_copy.wait_recv()
        weight_save.start()
        for r in range(min(2, rows)):
            launch(r)
        gather_b.forward(0)

        @pl.loop(0, rows)
        def _(r):
            gather_b.finish(r)
            for copy in block_saves(gather_b, full_b, save_b, r):
                copy.start()
            for j in range(n):
                kv[r, j * size : (j + 1) * size, :] = dot(
                    gather_b.block(r, j)[...], w_kv[...]
                ).astype(BF)

            @pl.when(r > 0)
            def _():
                sums.forward(r - 1)

            @pl.when(r + 2 < rows)
            def _():
                launch(r + 2)

            row = kv.at[r]
            attend_into(
                size,
                hid // DK,
                (q.at[r], 0),
                (row, 0),
                (row, hid),
                query_aug.at[r],
                key_aug.at[r],
                None,
                mix.at[r],
                aug.at[r],
            )
            for copy in cross_saves(r):
                copy.start()

            @pl.when(r + 1 < rows)
            def _():
                gather_b.forward(r + 1)

            gather_a.drain(r)
            for copy in block_saves(gather_a, full_a, save_a, r):
                copy.wait()
            for j in reversed(range(n)):
                part = dot(mix[r, j * size : (j + 1) * size, :], w_cross[:, hid:], NT)
                if j:
                    sums.put(r, j, part)
                else:
                    mid2[r] = part

            @pl.when(r > 0)
            def _():
                finish(r - 1)

            @pl.when(r == 1)
            def _():
                gather_t.start(0)

            @pl.when(r == 2)
            def _():
                gather_t.forward(0)

        sums.forward(rows - 1)
        if rows > 1:
            if rows == 2:
                gather_t.forward(0)
            gather_t.finish(0)
            for copy in block_saves(gather_t, full_t, save_t, 0):
                copy.start()
        finish(rows - 1)
        if rows > 1:
            gather_t.drain(0)
            for copy in block_saves(gather_t, full_t, save_t, 0):
                copy.wait()

        weight_save.wait()

        @pl.loop(0, rows)
        def _(r):
            gather_b.drain(r)
            for copy in block_saves(gather_b, full_b, save_b, r):
                copy.wait()
            gather_c.drain(r)
            for copy in block_saves(gather_c, full_cot, save_c, r):
                copy.wait()
            for copy in cross_saves(r):
                copy.wait()

    @pl.loop(0, rows)
    def _(r):
        sums.drain(r)


def middle_stage(n, x, cot, mid1, gain, w_gate, w_up, w_down, w_cross, query_aug, key_aug):
    rows, size, width = x.shape
    length, hid, ffd = n * size, w_cross.shape[1] // 2, w_gate.shape[1]
    slots = (rows, n - 1)
    full = ((rows, length, width), BF, False)
    head = ((rows, length, hid), BF, False)
    near = (x, cot, mid1, gain, w_gate, w_up, w_down, w_cross, query_aug, key_aug)
    return call_stage(
        functools.partial(middle_kernel, n),
        "middle_stage",
        3,
        [(a, True) for a in near],
        [
            ((rows, size, width), F32, True),
            ((rows, size, width), BF, True),
            full,
            full,
            full,
            full,
            ((width, 2 * hid), BF, False),
            ((rows, length, 2 * hid), BF, False),
            head,
            head,
            head,
        ],
        [
            *[pltpu.VMEM((*slots, size, width), BF)] * 5,
            pltpu.VMEM((rows, size, width), BF),
            pltpu.VMEM((width, 2 * hid), BF),
            pltpu.VMEM((rows, length, 2 * hid), BF),
            *[pltpu.VMEM((rows, length, hid), BF)] * 3,
            *[pltpu.SemaphoreType.DMA(slots)] * 10,
            *[pltpu.SemaphoreType.DMA((rows,))] * 2,
            *[pltpu.SemaphoreType.DMA((rows, n))] * 4,
            pltpu.SemaphoreType.DMA((rows, 4)),
            pltpu.SemaphoreType.DMA((3,)),
        ],
        rows * length * width * ffd * 6 + rows * length * length * hid * 16,
    )


def middle_back_kernel(n, *refs):
    (third, cot, gain2, gain1, w_gate, w_up, w_down, w_cross, w_kv, key_aug) = refs[:10]
    (mid1_in, mid2_in, fwd_in, cot_in, third_in) = refs[10:15]
    (kv_in, q_in, mix_in, aug_in) = refs[15:19]
    (grad, gain_out, parts_out, full_3, full_g) = refs[19:24]
    (hidden_out, dgate_out, dup_out, dkv_out, dq_out, ahead_out) = refs[24:30]
    (own, got, out, back, rest, dmem) = refs[30:36]
    (mid, full, kv, q, mix, aug, dq, dkv, hidden_s, dgate_s, dup_s, part_s) = refs[36:48]
    ready = refs[48]
    sems = refs[49:]
    rows, size = third.shape[:2]
    hid = q.shape[1]
    enc = lax.axis_index("section") == 0
    gather_3 = Gather(n, third, got, *sems[0:2])
    gather_g = Gather(n, own, got, *sems[2:4])
    sums_a = Sums(n, out, back, *sems[4:6])
    sums_b = Sums(n, out, back, *sems[6:8])
    sums_m = Sums(n, out, back, *sems[8:10])
    gather_s = Gather(n, own, got, *sems[10:12])
    pair_send, pair_recv, save_3, save_g, save_f, save_p, save_d, load_m, load_f, load_x = sems[12:22]
    save_s = sems[22]
    ahead = 1 if rows > 1 else 0
    greet(n, True)
    gain_out[...] = jnp.zeros_like(gain_out)

    def block_saves(gather, dst, sem, r):
        for j in range(n):
            yield pltpu.make_async_copy(
                gather.block(r, j), dst.at[r, pl.ds(j * size, size)], sem.at[r, j]
            )

    def pair_copy(r):
        return pltpu.make_async_remote_copy(
            src_ref=dmem.at[r],
            dst_ref=dmem.at[r],
            send_sem=pair_send.at[r],
            recv_sem=pair_recv.at[r],
            device_id={"section": 1 - lax.axis_index("section")},
            device_id_type=MESH,
        )

    def mid_load(i, source, r):
        return pltpu.make_async_copy(source.at[r], mid.at[i], load_m.at[i])

    def full_load(source, r):
        return pltpu.make_async_copy(source.at[r], full, load_f.at[0])

    def cross_loads(r):
        for i, (src, dst) in enumerate(((kv_in, kv), (q_in, q), (mix_in, mix), (aug_in, aug))):
            yield pltpu.make_async_copy(src.at[r], dst, load_x.at[i])

    def ffn_saves(r):
        for i, (src, dst) in enumerate(
            ((hidden_s, hidden_out), (dgate_s, dgate_out), (dup_s, dup_out))
        ):
            yield pltpu.make_async_copy(src, dst.at[r], save_f.at[r, i])

    def part_save(r, j):
        return pltpu.make_async_copy(
            part_s.at[j], parts_out.at[r, pl.ds(j * size, size)], save_p.at[j]
        )

    def feed_forward(r, normed_of, grad_of, sums, with_out):
        @pl.when(r > 0)
        def _():
            for copy in ffn_saves(r - 1):
                copy.wait()

        for j in reversed(range(n)):
            at = slice(j * size, (j + 1) * size)
            normed, slope_in = normed_of(j), grad_of(j)
            gate = dot(normed, w_gate[...])
            up = dot(normed, w_up[...])
            active, slope = gelu_and_slope(gate)
            hidden = (active * up).astype(BF)
            hidden_s[at, :] = hidden
            back_hidden = dot(slope_in, w_down[...], NT)
            dgate = (back_hidden * up * slope).astype(BF)
            dup = (back_hidden * active).astype(BF)
            dgate_s[at, :] = dgate
            dup_s[at, :] = dup
            part = dot(dgate, w_gate[...], NT) + dot(dup, w_up[...], NT)
            if j:
                sums.put(r, j, part)
            else:
                rest[r] = part
            if with_out:
                part = dot(hidden, w_down[...]).astype(BF)

                @pl.when(r > 0)
                def _():
                    part_save(r - 1, j).wait()

                part_s[j] = part
                part_save(r, j).start()
        for copy in ffn_saves(r):
            copy.start()

    def finish_third(r, sums, add_cot):
        mid_load(0, mid2_in, r).wait()
        if add_cot:
            arriving = dmem[r].astype(F32) + cot[r].astype(F32)
        else:
            arriving = sums.total(r, rest[r])
        part, terms = norm_back_parts(mid[0], gain2[...], arriving)
        gain_out[0] += gain_terms(terms)
        if not add_cot:
            part = part + cot[r].astype(F32)
        grad[r] = part
        own[r] = part.astype(BF)

    def dkv_save(r):
        return pltpu.make_async_copy(dkv, dkv_out.at[r], save_d.at[0])

    def dq_save(r):
        return pltpu.make_async_copy(dq.at[r], dq_out.at[r], save_d.at[1 + r])

    def finish_memory(r):
        dmem[r] = sums_m.total(r, rest[r]).astype(BF)
        pair_copy(r).start()

    def finish_second(r, sums):
        mid_load(1, mid1_in, r).wait()
        part, terms = norm_back_parts(mid[1], gain1[...], sums.total(r, rest[r]))
        gain_out[1] += gain_terms(terms)
        grad[r] = grad[r] + part

    last = rows - 1

    def lead():
        own[0] = grad[0].astype(BF)
        gather_s.start(0)

    def lead_saves():
        for j in range(n):
            yield pltpu.make_async_copy(
                gather_s.block(0, j), ahead_out.at[pl.ds(j * size, size)], save_s.at[j]
            )

    def finish_lead():
        if ahead:
            gather_s.finish(0)
            for copy in lead_saves():
                copy.start()
            for copy in lead_saves():
                copy.wait()
            gather_s.drain(0)

    @pl.when(jnp.logical_not(enc))
    def _():
        def third_loads(r):
            for j in range(1, n):
                yield pltpu.make_async_copy(
                    third_in.at[r, pl.ds(j * size, size)], got.at[r, j - 1], save_3.at[r, j]
                )

        for r in range(ahead, rows):
            gather_3.start(r)
        full_load(cot_in, 0).start()
        if ahead:
            for copy in third_loads(0):
                copy.start()
        else:
            gather_3.forward(0)

        @pl.loop(0, rows)
        def _(r):
            @pl.when(r < ahead)
            def _():
                for copy in third_loads(r):
                    copy.wait()

            @pl.when(r >= ahead)
            def _():
                gather_3.finish(r)

            for copy in block_saves(gather_3, full_3, save_3, r):
                copy.start()
            full_load(cot_in, r).wait()

            @pl.when(r > ahead)
            def _():
                gather_3.drain(r - 1)

            @pl.when(r > 0)
            def _():
                sums_a.forward(r - 1)
                mid_load(0, mid2_in, r - 1).start()

            for copy in block_saves(gather_3, full_3, save_3, r):
                copy.wait()
            feed_forward(
                r,
                lambda j: gather_3.block(r, j)[...],
                lambda j: full[j * size : (j + 1) * size, :],
                sums_a,
                True,
            )

            @pl.when(r + 1 < rows)
            def _():
                full_load(cot_in, r + 1).start()
                gather_3.forward(r + 1)

            @pl.when(r > 0)
            def _():
                finish_third(r - 1, sums_a, False)
                gather_g.start(r - 1)

        gather_3.drain(last)
        sums_a.forward(last)
        mid_load(0, mid2_in, last).start()
        for copy in cross_loads(0):
            copy.start()
        gather_g.forward(0)
        finish_third(last, sums_a, False)
        gather_g.start(last)

        @pl.loop(0, rows)
        def _(r):
            gather_g.finish(r)
            for copy in block_saves(gather_g, full_g, save_g, r):
                copy.start()
            for j in range(n):
                at = slice(j * size, (j + 1) * size)
                full[at, :hid] = dot(gather_g.block(r, j)[...], w_cross[:, hid:]).astype(BF)
            for copy in cross_loads(r):
                copy.wait()

            @pl.when(r > 0)
            def _():
                dkv_save(r - 1).wait()
                sums_m.forward(r - 1)

            attend_back_into(
                size,
                hid // DK,
                (q, 0),
                (kv, 0),
                (kv, hid),
                (full, 0),
                (mix, 0),
                (aug, 0),
                key_aug.at[r],
                None,
                (dq.at[r], 0),
                (dkv, 0),
                (dkv, hid),
            )
            dkv_save(r).start()
            dq_save(r).start()

            @pl.when(r + 1 < rows)
            def _():
                for copy in cross_loads(r + 1):
                    copy.start()
                gather_g.forward(r + 1)

            sums_a.drain(r)
            for j in reversed(range(n)):
                part = dot(dkv[j * size : (j + 1) * size, :], w_kv[...], NT)
                if j:
                    sums_m.put(r, j, part)
                else:
                    rest[r] = part

            @pl.when(r > 0)
            def _():
                finish_memory(r - 1)

        sums_m.forward(last)
        finish_memory(last)

        idx = lax.axis_index("mp")
        bits = [j for j in range(1, n) if j == low_bit(j)]
        for bit in bits:
            pl.semaphore_signal(
                ready, inc=1, device_id={"mp": flipped(idx, bit)}, device_id_type=MESH
            )
        pl.semaphore_wait(ready, len(bits))

        @pl.loop(0, rows)
        def _(r):
            sums_m.drain(r)
            gather_g.drain(r)
            for copy in block_saves(gather_g, full_g, save_g, r):
                copy.wait()

            @pl.when(r > 0)
            def _():
                mid_load(1, mid1_in, r - 1).start()

            for j in reversed(range(n)):
                part = dot(dq[r, j * size : (j + 1) * size, :], w_cross[:, :hid], NT)
                if j:
                    sums_b.put(r, j, part)
                else:
                    rest[r] = part

            @pl.when(r > 0)
            def _():
                sums_b.forward(r - 1)
                finish_second(r - 1, sums_b)

            @pl.when(r == 1)
            def _():
                lead()

        sums_b.forward(last)
        mid_load(1, mid1_in, last).start()
        if ahead:
            gather_s.forward(0)
        finish_second(last, sums_b)
        finish_lead()

        @pl.loop(0, rows)
        def _(r):
            pair_copy(r).wait_send()
            dq_save(r).wait()

        for j in range(n):
            part_save(last, j).wait()
        dkv_save(last).wait()

    @pl.when(enc)
    def _():
        full_load(fwd_in, 0).start()

        @pl.loop(0, rows + 1)
        def _(t):
            @pl.when(t < rows)
            def _():
                mid_load(0, mid2_in, t).start()
                pair_copy(t).wait_recv()
                finish_third(t, None, True)
                gather_g.start(t)

            @pl.when(t > 1)
            def _():
                mid_load(1, mid1_in, t - 2).start()

            @pl.when(t > 0)
            def _():
                r = t - 1
                gather_g.forward(r)
                gather_g.finish(r)
                for copy in block_saves(gather_g, full_g, save_g, r):
                    copy.start()
                full_load(fwd_in, r).wait()
                for copy in block_saves(gather_g, full_g, save_g, r):
                    copy.wait()
                feed_forward(
                    r,
                    lambda j: full[j * size : (j + 1) * size, :],
                    lambda j: gather_g.block(r, j)[...],
                    sums_b,
                    False,
                )

                @pl.when(r + 1 < rows)
                def _():
                    full_load(fwd_in, r + 1).start()

                gather_g.drain(r)
                sums_b.forward(r)

            @pl.when(t > 1)
            def _():
                finish_second(t - 2, sums_b)

            @pl.when(t == 2)
            def _():
                lead()

        mid_load(1, mid1_in, last).start()
        if ahead:
            gather_s.forward(0)
        finish_second(last, sums_b)
        finish_lead()

    for copy in ffn_saves(last):
        copy.wait()

    @pl.loop(0, rows)
    def _(r):
        sums_b.drain(r)


def middle_back_stage(
    n,
    third,
    cot,
    gain2,
    gain1,
    w_gate,
    w_up,
    w_down,
    w_cross,
    w_kv,
    key_aug,
    mid1,
    mid2,
    fwd,
    full_cot,
    full_t,
    kv,
    q,
    mix,
    aug,
):
    rows, size, width = third.shape
    length, hid, ffd = n * size, w_cross.shape[1] // 2, w_gate.shape[1]
    slots = (rows, n - 1)
    full = ((rows, length, width), BF, False)
    unit = ((rows, length, ffd), BF, False)
    near = (third, cot, gain2, gain1, w_gate, w_up, w_down, w_cross, w_kv, key_aug)
    return call_stage(
        functools.partial(middle_back_kernel, n),
        "middle_back_stage",
        4,
        [(a, True) for a in near]
        + [(a, False) for a in (mid1, mid2, fwd, full_cot, full_t, kv, q, mix, aug)],
        [
            ((rows, size, width), F32, True),
            ((2, 8, width), F32, True),
            full,
            full,
            full,
            unit,
            unit,
            unit,
            ((rows, length, 2 * hid), BF, False),
            ((rows, length, hid), BF, False),
            ((length, width), BF, False),
        ],
        [
            pltpu.VMEM((rows, size, width), BF),
            *[pltpu.VMEM((*slots, size, width), BF)] * 3,
            pltpu.VMEM((rows, size, width), F32),
            pltpu.VMEM((rows, size, width), BF),
            pltpu.VMEM((2, size, width), F32),
            pltpu.VMEM((length, width), BF),
            pltpu.VMEM((length, 2 * hid), BF),
            *[pltpu.VMEM((length, hid), BF)] * 3,
            pltpu.VMEM((rows, length, hid), BF),
            pltpu.VMEM((length, 2 * hid), BF),
            *[pltpu.VMEM((length, ffd), BF)] * 3,
            pltpu.VMEM((n, size, width), BF),
            pltpu.SemaphoreType.REGULAR,
            *[pltpu.SemaphoreType.DMA(slots)] * 12,
            *[pltpu.SemaphoreType.DMA((rows,))] * 2,
            *[pltpu.SemaphoreType.DMA((rows, n))] * 2,
            pltpu.SemaphoreType.DMA((rows, 3)),
            pltpu.SemaphoreType.DMA((n,)),
            pltpu.SemaphoreType.DMA((rows + 1,)),
            pltpu.SemaphoreType.DMA((2,)),
            pltpu.SemaphoreType.DMA((1,)),
            pltpu.SemaphoreType.DMA((4,)),
            pltpu.SemaphoreType.DMA((n,)),
        ],
        rows * length * width * ffd * 16 + rows * length * length * hid * 40,
    )


def weight_kernel(places, stacked, extra, *refs):
    out, acc = refs[-2:]
    at = pl.program_id(0)

    @pl.when(at == 0)
    def _():
        acc[...] = jnp.zeros_like(acc)

    for i, j, start, count in places:
        where = pl.ds(start, count)
        part = dot(refs[i][...], refs[j][...], TN)
        if stacked:
            acc[where, :] += part
        else:
            acc[:, where] += part

    @pl.when(at == pl.num_programs(0) - 1)
    def _():
        out[: acc.shape[0], :] = acc[...].astype(BF)
        if extra:
            out[acc.shape[0] :, :] = jnp.zeros((extra, acc.shape[1]), BF)


def weight_sums(pairs, stacked, extra=0):
    arrays, places, start = [], [], 0

    def index(array):
        for i, known in enumerate(arrays):
            if known is array:
                return i
        arrays.append(array)
        return len(arrays) - 1

    for a, b in pairs:
        count = (a if stacked else b).shape[-1]
        places.append((index(a), index(b), start, count))
        start += count
    flat = [a.reshape(-1, a.shape[-1]) for a in arrays]
    other = pairs[0][1 if stacked else 0].shape[-1]
    shape = (start, other) if stacked else (other, start)
    tokens, step = flat[0].shape[0], 512
    whole = (shape[0] + extra, shape[1])
    return pl.pallas_call(
        functools.partial(weight_kernel, places, stacked, extra),
        grid=(tokens // step,),
        in_specs=[pl.BlockSpec((step, a.shape[1]), lambda i: (i, 0)) for a in flat],
        out_specs=pl.BlockSpec(whole, lambda i: (0, 0)),
        out_shape=jax.ShapeDtypeStruct(whole, BF),
        scratch_shapes=[pltpu.VMEM(shape, F32)],
        compiler_params=pltpu.CompilerParams(vmem_limit_bytes=VMEM_LIMIT),
        cost_estimate=pl.CostEstimate(
            flops=2 * tokens * start * other,
            bytes_accessed=sum(a.size for a in flat) * 2,
            transcendentals=0,
        ),
        name="weight_sums",
    )(*flat)


def body(
    block_input, cotangent, segments, attn_weight, attn_out, ffn_in, ffn_out, cross_weight, gains
):
    enc = lax.axis_index("section") == 0
    idx = lax.axis_index("mp")
    n = lax.axis_size("mp")
    dp_size = lax.axis_size("dp")
    bits = [1 << b for b in range(n.bit_length() - 1)]
    size, row_count, width = block_input.shape[1:]
    length = size * n
    hid = attn_weight.shape[3]
    ffd = ffn_in.shape[3]
    rows = range(row_count)

    w_qkv = attn_weight[0].reshape(width, 3 * hid)
    w_out = attn_out[0]
    w_gate, w_up = ffn_in[0, :, 0], ffn_in[0, :, 1]
    w_down = ffn_out[0]
    w_cross = cross_weight[0].reshape(width, 2 * hid)
    gain = gains[0]
    x = jnp.swapaxes(block_input[0], 0, 1)
    cot = jnp.swapaxes(cotangent[0], 0, 1)

    order = jnp.arange(n, dtype=jnp.int32) ^ idx
    block_of = jnp.repeat(order, size)[:, None]
    lane = jnp.arange(DK, dtype=jnp.int32)
    local = jnp.concatenate(
        [lax.dynamic_slice_in_dim(segments, (idx ^ j) * size, size, axis=2) for j in range(n)],
        axis=2,
    )[..., None]
    own = jnp.where(enc, local[0], local[1])

    def query_features(seg, causal):
        doc = (lane < DOC_LANES) & (lane != seg)
        later = (lane >= BLOCK_LANE) & (lane < BLOCK_LANE + n)
        later = later & (lane - BLOCK_LANE > block_of) & causal
        return jnp.where(doc | later, BIG, 0.0).astype(BF)

    def key_features(seg):
        doc = (lane < DOC_LANES) & (lane == seg)
        ones = (lane >= OFFSET_LANE) & (lane < OFFSET_LANE + 3)
        place = lane - BLOCK_LANE == block_of
        return jnp.where(doc | ones | place, 1.0, 0.0).astype(BF)

    above = jnp.arange(size)[None, :] > jnp.arange(size)[:, None]
    tri = jnp.where(above & ~enc, BIG, 0.0).astype(F32)
    key_own, key_enc = key_features(own), key_features(local[0])

    mid1, normed2, full1, qkv1, mix1, aug1 = self_stage(
        n,
        x,
        gain,
        w_qkv,
        w_out,
        query_features(own, ~enc),
        key_own,
        tri,
    )
    mid2, third, full_a, full_b, full_cot, full_t, w_kv, kv, q, mix, aug = middle_stage(
        n,
        normed2,
        cot,
        mid1,
        gain[2:3],
        w_gate,
        w_up,
        w_down,
        w_cross,
        query_features(local[1], False),
        key_enc,
    )

    back_results = middle_back_stage(
        n,
        third,
        cot,
        gain[2:3],
        gain[1:2],
        w_gate,
        w_up,
        w_down,
        w_cross,
        w_kv,
        key_enc,
        mid1,
        mid2,
        full_a,
        full_cot,
        full_t,
        kv,
        q,
        mix,
        aug,
    )

    grad1, gain_parts, parts, full_3, full_g, hidden, dgate, dup, dkv, dq, lead = back_results

    def over_rows(total, dim):
        return lax.psum_scatter(total, "dp", scatter_dimension=dim, tiled=True)

    blank = jnp.zeros((width, 2 * hid), BF)
    sum_kv, sum_qo = lax.cond(
        enc,
        lambda: (blank, blank),
        lambda: (
            weight_sums([(full_b, dkv)], False),
            weight_sums([(full_a, dq), (full_g, mix)], False),
        ),
    )
    sum_kv, dgate = lax.optimization_barrier((sum_kv, dgate))
    sum_kv = lax.ppermute(sum_kv, "section", [(1, 0)])
    early = lax.cond(
        enc,
        lambda: weight_sums([(dgate, full_a), (dup, full_a), (hidden, full_g)], True),
        lambda: weight_sums([(dgate, full_3), (dup, full_3), (hidden, full_cot)], True),
    )
    early, sum_kv = lax.optimization_barrier((early, sum_kv))
    sum_cross = jnp.where(enc, sum_kv, sum_qo)
    got_early = over_rows(early, 1)

    def across(tensor, bit):
        decoder = [(n + i, n + (i ^ bit)) for i in range(n)]
        return lax.ppermute(tensor, ("section", "mp"), decoder)

    have = {j: parts[:, j * size : (j + 1) * size] for j in range(n)}
    first = None
    for bit in bits:
        for j in sorted((j for j in have if j & bit), reverse=True):
            came = across(have.pop(j), bit)
            total = have[j ^ bit].astype(F32) + came.astype(F32)
            have[j ^ bit] = total if len(have) == 1 else total.astype(BF)
        if bit == 1:
            first = have[max(have)]
    dec_out = mid2 + have[0].astype(F32)
    block_out = jnp.where(enc, third, dec_out.astype(BF))

    grad1, _ = lax.optimization_barrier((grad1, early))
    input_grad, gain_first, late = self_back_stage(
        n, x, gain, grad1, w_qkv, w_out, key_own, tri.T, qkv1, mix1, aug1, full1, lead, sum_cross
    )

    late, got_early = lax.optimization_barrier((late, got_early))
    got_late = over_rows(late, 0).astype(F32)
    got_early = got_early.astype(F32)
    quarter = width // dp_size
    out_in = jnp.stack([got_early[:ffd].T, got_early[ffd : 2 * ffd].T], axis=1)
    out_down = got_early[2 * ffd :]
    out_cross = got_late[:, 4 * hid :].reshape(quarter, 2, hid)
    out_qkv = got_late[:, : 3 * hid].reshape(quarter, 3, hid)
    out_out = got_late[:, 3 * hid : 4 * hid].T
    gain_parts = jnp.sum(gain_parts, axis=1)
    gain_total = jnp.stack([jnp.sum(gain_first, axis=0), gain_parts[1], gain_parts[0]])
    for axis, count in (("mp", n), ("dp", dp_size)):
        for bit in (1 << b for b in range(count.bit_length() - 1)):
            other = lax.ppermute(gain_total, axis, [(i, i ^ bit) for i in range(count)])
            gain_total = gain_total + other
    share = width // (n * dp_size)
    place = (lax.axis_index("dp") * n + idx) * share
    gain_total = lax.dynamic_slice_in_dim(gain_total, place, share, axis=1)
    return (
        jnp.swapaxes(block_out, 0, 1)[None],
        jnp.swapaxes(input_grad, 0, 1)[None],
        out_qkv[None],
        out_out[None],
        out_in[None],
        out_down[None],
        out_cross[None],
        gain_total[None],
    )


def solution(mesh):
    in_specs = (
        P("section", "mp", "dp", None),
        P("section", "mp", "dp", None),
        P(None, "dp", None),
        P("section", None, None, "mp"),
        P("section", "mp", None),
        P("section", None, None, "mp"),
        P("section", "mp", None),
        P("section", None, None, "mp"),
        P("section", None, None),
    )
    out_specs = (
        P("section", "mp", "dp", None),
        P("section", "mp", "dp", None),
        P("section", "dp", None, "mp"),
        P("section", "mp", "dp"),
        P("section", "dp", None, "mp"),
        P("section", "mp", "dp"),
        P("section", "dp", None, "mp"),
        P("section", None, ("dp", "mp")),
    )
    return jax.shard_map(body, mesh=mesh, in_specs=in_specs, out_specs=out_specs, check_vma=False)
```
